256 devices in a mesh: grp: 4 (over y), blk: 64 (over z, x, core).
Axes of the slice: x: 4, y: 4, z: 8, core: 2. Of those that a mesh axis runs over, the one named last changes fastest.
Arguments:
- adjoint_init: float32 [5, 128, 65536], P(None, 'grp', 'blk'), may hold values from -6 to 6
- adjoint_rhs: float32 [5, 128, 65536], P(None, 'grp', 'blk'), may hold values from -24 to 24
- flow_state: float32 [5, 128, 65536], P(None, 'grp', 'blk'), may hold values from -2 to 8, as said below
- face_weights: bfloat16 [6, 128, 65536], P(None, 'grp', 'blk'), may hold values from 0.29882812 to 1.1953125
- pseudo_time: float32 [128, 65536], P('grp', 'blk'), may hold values from 1 to 4
- tet_coords: float32 [4, 3, 524288], P(None, None, ('grp', 'blk')), may hold values from -6 to 6
- tet_weights: float32 [4, 524288], P(None, ('grp', 'blk')), may hold values from 0.25 to 1
- tet_cell: int32 [524288], P(('grp', 'blk')), may hold values from 0 to 32767
- tet_vertex: int32 [4, 524288], P(None, ('grp', 'blk')), may hold values from 0 to 1535
- tet_count: int32 [256, 64], P(('grp', 'blk')), may hold values from 1 to 32, as said below
Outputs:
- adjoint_field: float32 [5, 128, 65536], P(None, 'grp', 'blk')
- sensitivity: float32 [3, 393216], P(None, ('grp', 'blk'))
The draws below stay inside these ranges and needn't reach their ends.
Inputs may be any that keep to these rules, and one draw needn't show every extreme that they name: `flow_state`: the density is 0.5 to 2, pressure 0.4 (energy - momentum squared / (2 density)) is about 0.5 to 2, each velocity component is below 1 in magnitude. A block's slots are grouped by owner: slots o * 32 to (o + 1) * 32 - 1 of a block are for owner o of its group, and the first tet_count[block, o] of them are live. In every group one owner, drawn from the seed, gets exactly 32 live tetrahedra from every block of the group. `tet_vertex`: A corner's vertex belongs to the owner of its slot's range. `tet_cell`: cell index x 32 * 32 + y * 32 + z within the block.
All inputs are finite; a program needn't handle non-finite values.
Results may differ from the reference program's by a relative error of at most 0.0003.
Values sent between devices are 32-bit elements; how exact they have to be, the bound alone decides.
A program may use at most 128 MiB of HBM per device.

```python
import math
import jax
import jax.numpy as jnp
from jax import lax

EDGE = 32
SWEEPS = 2
TET_DEV = 2048
VERT_DEV = 1536
OWNERS = 64
SOURCES = 256
CAP = 32
CELLS = 32768
NX = 128
NYZ = 65536
TETS = 524288
NVERT = 393216


GAMMA = 1.4


def draw_flow_state(key, part):
    keys = jax.random.split(key, 3)
    shape = (NX, NYZ)
    density = jnp.exp(jax.random.uniform(keys[0], shape, jnp.float32, math.log(0.5), math.log(2.0)))
    velocity = jnp.clip(0.3 * jax.random.normal(keys[1], (3,) + shape, jnp.float32), -0.9, 0.9)
    pressure = jnp.exp(jax.random.uniform(keys[2], shape, jnp.float32, math.log(0.5), math.log(2.0)))
    energy = pressure / (GAMMA - 1.0) + 0.5 * density * jnp.sum(velocity * velocity, axis=0)
    return jnp.concatenate([density[None], density[None] * velocity, energy[None]], 0).astype(jnp.float32)


def draw_tet_count(key, part):
    keys = jax.random.split(key, 3)
    ceiling = jax.random.randint(keys[0], (SOURCES, 1), max(CAP // 4, 1), CAP + 1)
    drawn_counts = jax.random.randint(keys[1], (SOURCES, OWNERS), jnp.maximum(ceiling // 2, 1), ceiling + 1)
    full_owner = jax.random.randint(keys[2], (SOURCES // OWNERS, 1), 0, OWNERS)
    group_of = jnp.arange(SOURCES) // OWNERS
    is_full = full_owner[group_of] == jnp.arange(OWNERS)[None, :]
    return jnp.where(is_full, CAP, drawn_counts).astype(jnp.int32)


def with_ends(entries, rng, low, top_value):
    place = [jax.random.randint(jax.random.fold_in(rng, axis), (), 0, length) for axis, length in enumerate(entries.shape)]
    longest = entries.shape.index(max(entries.shape))
    next_to = place[:longest] + [(place[longest] + 1) % entries.shape[longest]] + place[longest + 1:]
    return entries.at[tuple(place)].set(low).at[tuple(next_to)].set(top_value)


def level_of(key, dims, shards, smallest, top_value):
    loudness = 1.0
    for position, shards_of in shards:
        draws = jax.random.uniform(jax.random.fold_in(jax.random.fold_in(key, 6), position), (shards_of,), jnp.float32, smallest / len(shards), top_value / len(shards))
        loudness = loudness * jnp.repeat(jnp.exp(draws), dims[position] // shards_of).reshape((-1,) + (1,) * (len(dims) - 1 - position))
    return loudness


def gaussian(rng, dims, deviation, bound, cuts=(), held_as=jnp.bfloat16):
    values = deviation * jax.random.normal(rng, dims, jnp.float32)
    if cuts:
        values = values * level_of(rng, dims, cuts, -0.22, 0.18)
    return jnp.clip(values, -bound, bound).astype(held_as)


def setup_inputs(seed: int = 0) -> dict:
    key_of = jax.random.split(jax.random.key(seed), 11)
    return {
        "adjoint_init": gaussian(key_of[0], (5, NX, NYZ), 1.0, 6.0, ((1, 4), (2, 64)), jnp.float32),
        "adjoint_rhs": gaussian(key_of[1], (5, NX, NYZ), 4.0, 24.0, ((1, 4), (2, 64)), jnp.float32),
        "flow_state": draw_flow_state(jax.random.fold_in(key_of[10], 71), 0),
        "face_weights": jnp.clip(0.29882812 + 0.8964844 * jax.random.uniform(key_of[3], (6, NX, NYZ), jnp.float32) ** level_of(key_of[3], (6, NX, NYZ), ((1, 4), (2, 64)), -0.2, 0.2), 0.29882812, 1.1953125).astype(jnp.bfloat16),
        "pseudo_time": jnp.clip(jnp.exp(math.log(4.0) - 1.3862944 * jax.random.uniform(key_of[4], (NX, NYZ), jnp.float32) ** level_of(key_of[4], (NX, NYZ), ((0, 4), (1, 64)), -0.2, 0.2)), 1.0, 4.0),
        "tet_coords": gaussian(key_of[5], (4, 3, TETS), 1.0, 6.0, ((2, 256),), jnp.float32),
        "tet_weights": jnp.clip(0.25 + 0.75 * jax.random.uniform(key_of[6], (4, TETS), jnp.float32) ** level_of(key_of[6], (4, TETS), ((1, 256),), -0.2, 0.2), 0.25, 1.0),
        "tet_cell": with_ends(jax.random.randint(key_of[7], (TETS,), 0, CELLS), jax.random.fold_in(key_of[7], 1), 0, CELLS - 1).astype(jnp.int32),
        "tet_vertex": with_ends(jax.random.randint(key_of[8], (4, TETS), 0, VERT_DEV), jax.random.fold_in(key_of[8], 1), 0, VERT_DEV - 1).astype(jnp.int32),
        "tet_count": draw_tet_count(jax.random.fold_in(key_of[10], 71), 0),
    }


GAMMA = 1.4

def flow_split(state):
    density = state[0]
    velocity = state[1:4] / density
    speed_sq = lax.optimization_barrier(jnp.sum(velocity * velocity, axis=0))
    pressure = (GAMMA - 1.0) * (state[4] - 0.5 * density * speed_sq)
    return (velocity, speed_sq, pressure)

def jacobians(state):
    density = state[0]
    velocity, speed_sq, pressure = flow_split(state)
    enthalpy = (state[4] + pressure) / density
    reach = jnp.sqrt(speed_sq) + jnp.sqrt(GAMMA * pressure / density)
    half_sq = 0.5 * (GAMMA - 1.0) * speed_sq
    tables = []
    for axis_id in range(3):
        normal_vel = velocity[axis_id]
        matrix = [[1.0 if column == axis_id + 1 else 0.0 for column in range(5)]]
        for first in range(3):
            n_first = 1.0 if first == axis_id else 0.0
            line = [half_sq * n_first - velocity[first] * normal_vel]
            for second in range(3):
                n_second = 1.0 if second == axis_id else 0.0
                entry = velocity[first] * n_second - (GAMMA - 1.0) * n_first * velocity[second]
                if first == second:
                    entry = entry + normal_vel
                line.append(entry)
            line.append((GAMMA - 1.0) * n_first)
            matrix.append(line)
        energy_line = [normal_vel * (half_sq - enthalpy)]
        for second in range(3):
            n_second = 1.0 if second == axis_id else 0.0
            energy_line.append(enthalpy * n_second - (GAMMA - 1.0) * normal_vel * velocity[second])
        energy_line.append(GAMMA * normal_vel)
        matrix.append(energy_line)
        tables.append(matrix)
    return (reach, tables)

def apply_transpose(matrix, adjoint):
    result = []
    for column in range(5):
        total = matrix[0][column] * adjoint[0]
        for line in range(1, 5):
            total = total + matrix[line][column] * adjoint[line]
        result.append(total)
    return jnp.stack(result)

def relax_cells(reach, tables, faces, pseudo, rhs, neighbours):
    total = rhs
    weight = pseudo
    for direction in range(6):
        axis_id = direction // 2
        sign_value = 1.0 if direction % 2 == 0 else -1.0
        nearby = neighbours[direction]
        face = faces[direction].astype(jnp.float32)
        total = total + 0.5 * face * (sign_value * apply_transpose(tables[axis_id], nearby) + reach * nearby)
        weight = weight + 0.5 * reach * face
    return total / weight

def cross_product(left, right):
    return jnp.stack([left[1] * right[2] - left[2] * right[1], left[2] * right[0] - left[0] * right[2], left[0] * right[1] - left[1] * right[0]])

def tet_terms(adj_tet, state_tet, coords, weights, live):
    velocity, speed_sq, pressure = flow_split(state_tet)
    volume_weight = pressure * adj_tet[4]
    face_weight = pressure * adj_tet[1:4]
    corner = [coords[k] for k in range(4)]
    edge_one = corner[1] - corner[0]
    edge_two = corner[2] - corner[0]
    edge_three = corner[3] - corner[0]
    grad_one = cross_product(edge_two, edge_three) / 6.0
    grad_two = cross_product(edge_three, edge_one) / 6.0
    grad_three = cross_product(edge_one, edge_two) / 6.0
    grad_zero = -(grad_one + grad_two + grad_three)
    side_one = corner[2] - corner[1]
    side_two = corner[3] - corner[1]
    face_two = 0.5 * cross_product(side_two, face_weight)
    face_three = 0.5 * cross_product(face_weight, side_one)
    face_one = -(face_two + face_three)
    terms = jnp.stack([volume_weight * grad_zero, volume_weight * grad_one + face_one, volume_weight * grad_two + face_two, volume_weight * grad_three + face_three])
    return terms * (weights * live)[:, None, :]

def reference(adjoint_init, adjoint_rhs, flow_state, face_weights, pseudo_time, tet_coords, tet_weights, tet_cell, tet_vertex, tet_count):
    column_pos = jnp.arange(NYZ, dtype=jnp.int32) % EDGE
    keep_upper = (column_pos != EDGE - 1).astype(jnp.float32)
    keep_lower = (column_pos != 0).astype(jnp.float32)
    zero_span = jnp.zeros((5, EDGE), jnp.float32)
    zero_single = jnp.zeros((5, 1), jnp.float32)

    def sweep_once(adjoint):
        padded = jnp.pad(adjoint, ((0, 0), (1, 1), (0, 0)))

        def plane(row):
            here = lax.dynamic_index_in_dim(padded, row + 1, 1, keepdims=False)
            above = lax.dynamic_index_in_dim(padded, row + 2, 1, keepdims=False)
            below = lax.dynamic_index_in_dim(padded, row, 1, keepdims=False)
            state = lax.dynamic_index_in_dim(flow_state, row, 1, keepdims=False)
            faces = lax.dynamic_index_in_dim(face_weights, row, 1, keepdims=False)
            pseudo = lax.dynamic_index_in_dim(pseudo_time, row, 0, keepdims=False)
            rhs = lax.dynamic_index_in_dim(adjoint_rhs, row, 1, keepdims=False)
            neighbours = [above, below, jnp.concatenate([here[:, EDGE:], zero_span], 1), jnp.concatenate([zero_span, here[:, :-EDGE]], 1), jnp.concatenate([here[:, 1:], zero_single], 1) * keep_upper, jnp.concatenate([zero_single, here[:, :-1]], 1) * keep_lower]
            reach, tables = jacobians(state)
            return relax_cells(reach, tables, faces, pseudo, rhs, neighbours)
        planes = lax.map(plane, jnp.arange(NX, dtype=jnp.int32))
        return jnp.transpose(planes, (1, 0, 2))
    adjoint = adjoint_init
    for sweep_index in range(SWEEPS):
        adjoint = sweep_once(adjoint)
    index = jnp.arange(TETS, dtype=jnp.int32)
    source = index // TET_DEV
    slot = index % TET_DEV
    owner_slot = slot // CAP
    live = (slot % CAP < tet_count[source, owner_slot]).astype(jnp.float32)
    group = source // OWNERS
    column = source % OWNERS
    grid_x = group * EDGE + tet_cell // (EDGE * EDGE)
    grid_col = column * (EDGE * EDGE) + tet_cell % (EDGE * EDGE)
    adj_tet = adjoint[:, grid_x, grid_col]
    state_tet = flow_state[:, grid_x, grid_col]
    terms = tet_terms(adj_tet, state_tet, tet_coords, tet_weights, live)
    target = (((group * OWNERS + owner_slot) * VERT_DEV)[None, :] + tet_vertex).reshape(-1)
    data = jnp.transpose(terms, (1, 0, 2)).reshape(3, -1)
    sums = jnp.stack([jax.ops.segment_sum(data[k], target, num_segments=NVERT) for k in range(3)])
    return (adjoint, sums)
```

```python
import functools

import jax
import jax.numpy as jnp
from jax import lax
from jax.experimental import pallas as pl
from jax.experimental.pallas import tpu as pltpu
from jax.sharding import PartitionSpec as P

SWEEPS = 2
VERT_DEV = 1536
CAP = 32
LANES = 128
GAMMA = 1.4
LOCAL = 8
MESH = pl.DeviceIdType.MESH
F32 = jnp.float32
BF16 = jnp.bfloat16


def lane_iota(shape):
    return lax.broadcasted_iota(jnp.int32, shape, len(shape) - 1)


def row_iota(shape):
    return lax.broadcasted_iota(jnp.int32, shape, len(shape) - 2)


def cross(a, b):
    return [
        a[1] * b[2] - a[2] * b[1],
        a[2] * b[0] - a[0] * b[2],
        a[0] * b[1] - a[1] * b[0],
    ]


def kernel(
    groups,
    blocks,
    init_hbm,
    rhs_hbm,
    flow_hbm,
    face_hbm,
    pseudo_hbm,
    coords_hbm,
    weights_hbm,
    cell_hbm,
    vertex_hbm,
    count_hbm,
    adj_out,
    sens_out,
    adj_a,
    adj_b,
    adj_c,
    rhs,
    flow,
    face,
    pseudo,
    coords,
    weights,
    cell,
    vertex,
    count,
    gface,
    scaled,
    coef,
    press,
    y_send,
    y_recv,
    table,
    onehot,
    geom,
    send,
    recv,
    left_op,
    right_op,
    load_sem,
    out_sem,
    halo_send,
    halo_recv,
    term_send,
    term_recv,
):
    group = lax.axis_index("grp")
    block = lax.axis_index("blk")
    columns = 8
    chunks = blocks // 8

    loads = [
        (flow_hbm, flow),
        (face_hbm, face),
        (pseudo_hbm, pseudo),
        (rhs_hbm, rhs),
        (cell_hbm, cell),
        (coords_hbm, coords),
        (weights_hbm, weights),
        (vertex_hbm, vertex),
        (count_hbm, count),
    ]
    for tile in range(columns):
        pltpu.make_async_copy(
            init_hbm.at[:, :, pl.ds(tile * LANES, LANES)],
            adj_a.at[:, 1 + tile, pl.ds(8, 32), :],
            load_sem.at[len(loads)],
        ).start()
    for position, (source, target) in enumerate(loads):
        pltpu.make_async_copy(source, target, load_sem.at[position]).start()

    def loaded(*wanted):
        for position, (source, target) in enumerate(loads):
            if any(target is one for one in wanted):
                pltpu.make_async_copy(source, target, load_sem.at[position]).wait()

    def inner(ref):
        return ref.at[:, pl.ds(1, columns), pl.ds(8, 32), :]

    grp_up = {"grp": lax.rem(group + 1, groups)}
    grp_down = {"grp": lax.rem(group + groups - 1, groups)}
    blk_up = {"blk": lax.rem(block + 1, blocks)}
    blk_down = {"blk": lax.rem(block + blocks - 1, blocks)}

    barrier = pltpu.get_barrier_semaphore()
    for device in (grp_up, grp_down):
        pl.semaphore_signal(barrier, inc=1, device_id=device, device_id_type=MESH)

    def greet(step, carry):
        pl.semaphore_signal(
            barrier,
            inc=1,
            device_id={"blk": lax.rem(block + step, blocks)},
            device_id_type=MESH,
        )
        return carry

    lax.fori_loop(1, blocks, greet, 0)

    tile_lane = lane_iota((8, LANES))
    lane_block = tile_lane // CAP

    def halo_copies(adj, sweep):
        span = pl.ds(1, columns)
        parts = [
            (adj.at[:, span, pl.ds(39, 1), :], adj.at[:, span, pl.ds(7, 1), :], grp_up),
            (adj.at[:, span, pl.ds(8, 1), :], adj.at[:, span, pl.ds(40, 1), :], grp_down),
            (y_send.at[sweep, 0], y_recv.at[sweep, 0], blk_up),
            (y_send.at[sweep, 1], y_recv.at[sweep, 1], blk_down),
        ]
        return [
            pltpu.make_async_remote_copy(
                src_ref=source,
                dst_ref=target,
                send_sem=halo_send.at[sweep, position],
                recv_sem=halo_recv.at[sweep, position],
                device_id=device,
                device_id_type=MESH,
            )
            for position, (source, target, device) in enumerate(parts)
        ]

    def pack(adj, sweep):
        for field in range(5):
            for side, tile, home in ((0, columns, 3), (1, 1, 0)):
                total = None
                for part in range(4):
                    value = adj[field, tile, pl.ds(8 + 8 * part, 8), :]
                    turn = (part - home) % 4 * CAP
                    if turn:
                        value = pltpu.roll(value, turn, 1)
                    total = value if total is None else jnp.where(lane_block == part, value, total)
                y_send[sweep, side, field] = total

    def unpack(adj, sweep):
        for field in range(5):
            for side, tile, home in ((0, 0, 3), (1, columns + 1, 0)):
                value = y_recv[sweep, side, field]
                for part in range(4):
                    turn = (home - part) % 4 * CAP
                    adj[field, tile, pl.ds(8 + 8 * part, 8), :] = (
                        pltpu.roll(value, turn, 1) if turn else value
                    )

    def sweep_tile(source, store, tile, part):
        rows = pl.ds(8 * part, 8)
        here = pl.ds(8 * part + 8, 8)
        center = [source[f, tile + 1, here, :] for f in range(5)]
        upper = [source[f, tile + 2, here, :] for f in range(5)]
        lower = [source[f, tile, here, :] for f in range(5)]
        pairs = [
            (
                [source[f, tile + 1, pl.ds(8 * part + 9, 8), :] for f in range(5)],
                [source[f, tile + 1, pl.ds(8 * part + 7, 8), :] for f in range(5)],
            ),
            (
                [
                    pltpu.roll(jnp.where(tile_lane >= CAP, center[f], upper[f]), LANES - CAP, 1)
                    for f in range(5)
                ],
                [
                    pltpu.roll(jnp.where(tile_lane < LANES - CAP, center[f], lower[f]), CAP, 1)
                    for f in range(5)
                ],
            ),
            (
                [pltpu.roll(center[f], LANES - 1, 1) for f in range(5)],
                [pltpu.roll(center[f], 1, 1) for f in range(5)],
            ),
        ]
        velocity = [coef[k, tile, rows, :] for k in range(3)]
        half_sq = coef[3, tile, rows, :]
        enthalpy = coef[4, tile, rows, :]
        reach = coef[5, tile, rows, :]
        sums = None
        moved = None
        flux = None
        first = []
        turned = None
        for axis, (plus, minus) in enumerate(pairs):
            g_plus = gface[2 * axis, tile, rows, :]
            g_minus = gface[2 * axis + 1, tile, rows, :]
            ahead = [g_plus * value for value in plus]
            behind = [g_minus * value for value in minus]
            diff = [a - b for a, b in zip(ahead, behind)]
            both = [a + b for a, b in zip(ahead, behind)]
            sums = both if sums is None else [a + b for a, b in zip(sums, both)]
            dot = (
                velocity[0] * diff[1]
                + velocity[1] * diff[2]
                + velocity[2] * diff[3]
                + enthalpy * diff[4]
            )
            first.append(diff[0] + dot)
            speed = velocity[axis]
            part_moved = [speed * diff[k] for k in range(1, 5)]
            moved = part_moved if moved is None else [a + b for a, b in zip(moved, part_moved)]
            flux = speed * dot if flux is None else flux + speed * dot
            turned = diff[1 + axis] if turned is None else turned + diff[1 + axis]
        turned = turned + moved[3]
        scaled_turn = (GAMMA - 1.0) * turned
        result = [half_sq * turned - flux]
        for k in range(3):
            result.append(first[k] - scaled_turn * velocity[k] + moved[k])
        result.append(scaled_turn + moved[3])
        for f in range(5):
            store(f, tile, part, scaled[f, tile, rows, :] + reach * sums[f] + result[f])

    def store_b(f, tile, part, value):
        adj_b[f, tile + 1, pl.ds(8 * part + 8, 8), :] = value

    def store_c(f, tile, part, value):
        adj_c[f, pl.ds(8 * part, 8), pl.ds(pl.multiple_of(tile * LANES, LANES), LANES)] = value

    def interior(source, store):
        def body(tile, carry):
            for part in (1, 2):
                sweep_tile(source, store, tile, part)
            return carry

        lax.fori_loop(1, columns - 1, body, 0)

    def boundary(source, store):
        def body(tile, carry):
            for part in (0, 3):
                sweep_tile(source, store, tile, part)
            return carry

        lax.fori_loop(0, columns, body, 0)

        def ends(step, carry):
            for part in (1, 2):
                sweep_tile(source, store, step * (columns - 1), part)
            return carry

        lax.fori_loop(0, 2, ends, 0)

    pltpu.make_async_copy(inner(adj_a), inner(adj_a), load_sem.at[len(loads)]).wait()
    pack(adj_a, 0)
    pl.semaphore_wait(barrier, blocks + 1)
    first_halo = halo_copies(adj_a, 0)
    for copy in first_halo:
        copy.start()

    loaded(flow, face, pseudo, rhs)
    tall_row = row_iota((16, LANES))
    tall_lane = lane_iota((16, LANES))

    def coefficients(step, carry):
        tile = step // 2
        half = step % 2
        rows = pl.ds(pl.multiple_of(half * 16, 16), 16)
        lanes = pl.ds(pl.multiple_of(tile * LANES, LANES), LANES)
        density = flow[0, rows, lanes]
        inverse = 1.0 / density
        velocity = [flow[1 + k, rows, lanes] * inverse for k in range(3)]
        energy = flow[4, rows, lanes]
        speed_sq = (
            velocity[0] * velocity[0] + velocity[1] * velocity[1] + velocity[2] * velocity[2]
        )
        pressure = (GAMMA - 1.0) * (energy - 0.5 * density * speed_sq)
        enthalpy = (energy + pressure) * inverse
        reach = jnp.sqrt(speed_sq) + jnp.sqrt(GAMMA * pressure * inverse)
        for k in range(3):
            coef[k, tile, rows, :] = velocity[k]
        coef[3, tile, rows, :] = 0.5 * (GAMMA - 1.0) * speed_sq
        coef[4, tile, rows, :] = enthalpy
        coef[5, tile, rows, :] = reach
        press[tile, rows, :] = pressure
        faces = [face[d, rows, lanes].astype(F32) for d in range(6)]
        open_sum = faces[0] + faces[1] + faces[2] + faces[3] + faces[4] + faces[5]
        share = 1.0 / (pseudo[rows, lanes] + 0.5 * reach * open_sum)
        half_share = 0.5 * share
        across = tall_row + half * 16
        along = tall_lane + tile * LANES
        height = tall_lane % 32
        outside = [
            (across == 31) & (group == groups - 1),
            (across == 0) & (group == 0),
            (along >= 992) & (block == blocks - 1),
            (along < 32) & (block == 0),
            height == 31,
            height == 0,
        ]
        for d in range(6):
            gface[d, tile, rows, :] = jnp.where(outside[d], 0.0, faces[d] * half_share)
        for f in range(5):
            scaled[f, tile, rows, :] = rhs[f, rows, lanes] * share
        return carry

    lax.fori_loop(0, 2 * columns, coefficients, 0)
    interior(adj_a, store_b)
    for copy in first_halo:
        copy.wait_recv()
    unpack(adj_a, 0)
    boundary(adj_a, store_b)

    pack(adj_b, 1)
    second_halo = halo_copies(adj_b, 1)
    for copy in second_halo:
        copy.start()
    interior(adj_b, store_c)

    loaded(cell, coords, weights, vertex, count)

    def pick_cells(chunk, carry):
        lanes = pl.ds(pl.multiple_of(chunk * 256, 256), 256)
        place = jnp.bitwise_and(cell[:, lanes], 1023)
        for band in range(8):
            rows = band * 128 + row_iota((128, 256))
            onehot[pl.ds(band * 128, 128), lanes] = jnp.where(rows == place, 1.0, 0.0).astype(BF16)
        return carry

    lax.fori_loop(0, chunks, pick_cells, 0)

    tile_row = row_iota((8, LANES))
    own_block = lane_block == tile_row % 4
    upper_half = tile_row < 4
    slot = tile_lane % CAP

    def spread(even, odd):
        value = jnp.where(own_block, jnp.where(upper_half, even, odd), 0.0)
        value = value + pltpu.roll(value, CAP, 1)
        return value + pltpu.roll(value, 2 * CAP, 1)

    def by_corner(values):
        total = values[3]
        for k in range(3):
            total = jnp.where(lane_block == k, values[k], total)
        return total

    def geometry(chunk, carry):
        even = pl.ds(pl.multiple_of(chunk * 256, 128), 128)
        odd = pl.ds(pl.multiple_of(chunk * 256 + 128, 128), 128)
        rows = pl.ds(pl.multiple_of(chunk * 8, 8), 8)
        corner = [
            [spread(coords[k, c : c + 1, even], coords[k, c : c + 1, odd]) for k in range(3)]
            for c in range(4)
        ]
        edge = [[corner[c][k] - corner[0][k] for k in range(3)] for c in range(1, 4)]
        grads = [
            [value / 6.0 for value in cross(edge[1], edge[2])],
            [value / 6.0 for value in cross(edge[2], edge[0])],
            [value / 6.0 for value in cross(edge[0], edge[1])],
        ]
        grad_zero = [-(grads[0][k] + grads[1][k] + grads[2][k]) for k in range(3)]
        side_two = [0.5 * (corner[3][k] - corner[1][k]) for k in range(3)]
        side_three = [-0.5 * (corner[2][k] - corner[1][k]) for k in range(3)]
        side_one = [-(side_two[k] + side_three[k]) for k in range(3)]
        weight = by_corner([spread(weights[c : c + 1, even], weights[c : c + 1, odd]) for c in range(4)])
        counts = jnp.broadcast_to(count[...], (8, blocks))
        wanted = lane_iota((8, blocks)) == chunk * 8 + row_iota((8, blocks))
        own_count = jnp.sum(jnp.where(wanted, counts, 0), axis=1, keepdims=True)
        weight = jnp.where(slot < own_count, weight, 0.0)
        for k in range(3):
            gradient = by_corner([grad_zero[k], grads[0][k], grads[1][k], grads[2][k]])
            side = by_corner([jnp.zeros_like(side_one[k]), side_one[k], side_two[k], side_three[k]])
            geom[k, rows, :] = weight * gradient
            geom[3 + k, rows, :] = weight * side
        send[3, rows, :] = by_corner(
            [
                spread(vertex[c : c + 1, even].astype(F32), vertex[c : c + 1, odd].astype(F32))
                for c in range(4)
            ]
        )
        return carry

    lax.fori_loop(0, chunks, geometry, 0)

    for copy in second_halo:
        copy.wait_recv()
    unpack(adj_b, 1)
    boundary(adj_b, store_c)
    adj_copy = pltpu.make_async_copy(adj_c, adj_out, out_sem)
    adj_copy.start()

    def fill_table(step, carry):
        tile = step // 2
        half = step % 2
        rows = pl.ds(pl.multiple_of(half * 16, 16), 16)
        lanes = pl.ds(pl.multiple_of(tile * LANES, LANES), LANES)
        pressure = press[tile, rows, :]
        for f in range(4):
            value = pressure * adj_c[1 + f, rows, lanes]
            high = value.astype(BF16)
            low = (value - high.astype(F32)).astype(BF16)
            table[pl.ds(pl.multiple_of(f * 32 + half * 16, 16), 16), lanes] = high
            table[pl.ds(pl.multiple_of(128 + f * 32 + half * 16, 16), 16), lanes] = low
        return carry

    lax.fori_loop(0, 2 * columns, fill_table, 0)

    def terms(chunk, carry):
        lanes = pl.ds(pl.multiple_of(chunk * 256, 256), 256)
        rows = pl.ds(pl.multiple_of(chunk * 8, 8), 8)
        found = jnp.dot(table[...], onehot[:, lanes], preferred_element_type=F32)
        found = found[:128] + found[128:]
        plane = jnp.right_shift(cell[:, lanes], 10)
        mine = row_iota((32, 256)) == plane
        fields = []
        for f in range(4):
            value = jnp.where(mine, found[32 * f : 32 * f + 32], 0.0)
            value = jnp.sum(value, axis=0, keepdims=True)
            fields.append(spread(value[:, :128], value[:, 128:]))
        b, a = fields[:3], fields[3]
        gradient = [geom[k, rows, :] for k in range(3)]
        side = [geom[3 + k, rows, :] for k in range(3)]
        turn = cross(side, b)
        for k in range(3):
            send[k, rows, :] = a * gradient[k] + turn[k]
        return carry

    lax.fori_loop(0, chunks, terms, 0)

    planes = blocks // LOCAL
    z, x, core = block // LOCAL, block % LOCAL // 2, block % 2

    def partner(step):
        far = step // LOCAL
        near = step % LOCAL
        return (
            lax.rem(z + far, planes) * LOCAL
            + lax.rem(x + near // 2, 4) * 2
            + lax.rem(core + near % 2, 2)
        )

    def post(step, carry):
        owner = partner(step)
        pltpu.make_async_remote_copy(
            src_ref=send.at[:, pl.ds(owner, 1), :],
            dst_ref=recv.at[:, pl.ds(step - 1, 1), :],
            send_sem=term_send,
            recv_sem=term_recv,
            device_id={"blk": owner},
            device_id_type=MESH,
        ).start()
        return carry

    lax.fori_loop(1, blocks, post, 0)
    recv[:, pl.ds(blocks - 1, 1), :] = send[:, pl.ds(block, 1), :]
    others = pltpu.make_async_remote_copy(
        src_ref=send.at[:, pl.ds(0, blocks - 1), :],
        dst_ref=recv.at[:, pl.ds(0, blocks - 1), :],
        send_sem=term_send,
        recv_sem=term_recv,
        device_id=blk_up,
        device_id_type=MESH,
    )
    others.wait_recv()

    def operands(chunk, carry):
        rows = pl.ds(pl.multiple_of(chunk * 8, 8), 8)
        vertices = recv[3, rows, :].astype(jnp.int32)
        major = jnp.right_shift(vertices, 7)
        minor = jnp.bitwise_and(vertices, 127)
        halves = []
        for k in range(3):
            value = recv[k, rows, :]
            high = value.astype(BF16).astype(F32)
            halves += [high, value - high]
        for s in range(8):
            lanes = pl.ds(pl.multiple_of(chunk * 1024 + s * LANES, LANES), LANES)
            right_op[:, lanes] = jnp.where(row_iota((128, LANES)) == minor[s : s + 1], 1.0, 0.0).astype(BF16)
            hit = row_iota((16, LANES)) == major[s : s + 1]
            for n, value in enumerate(halves):
                left_op[pl.ds(16 * n, 16), lanes] = jnp.where(hit, value[s : s + 1], 0.0).astype(BF16)
        return carry

    lax.fori_loop(0, chunks, operands, 0)
    sums = lax.dot_general(
        left_op[...], right_op[...], (((1,), (1,)), ((), ())), preferred_element_type=F32
    )
    for k in range(3):
        both = sums[32 * k : 32 * k + 16] + sums[32 * k + 16 : 32 * k + 32]
        for h in range(VERT_DEV // LANES):
            sens_out[k : k + 1, h * LANES : (h + 1) * LANES] = both[h : h + 1]

    for copy in first_halo + second_halo:
        copy.wait_send()
    others.wait_send()
    adj_copy.wait()


def local(groups, blocks, init, rhs, flow, face, pseudo, coords, weights, cell, vertex, count):
    slots = blocks * CAP
    vmem = pltpu.VMEM
    return pl.pallas_call(
        functools.partial(kernel, groups, blocks),
        out_shape=(
            jax.ShapeDtypeStruct((5, 32, 1024), F32),
            jax.ShapeDtypeStruct((3, VERT_DEV), F32),
        ),
        in_specs=[pl.BlockSpec(memory_space=pl.ANY)] * 10,
        out_specs=(
            pl.BlockSpec(memory_space=pl.ANY),
            pl.BlockSpec(memory_space=pltpu.VMEM),
        ),
        scratch_shapes=[
            vmem((5, 10, 48, LANES), F32),
            vmem((5, 10, 48, LANES), F32),
            vmem((5, 32, 1024), F32),
            vmem((5, 32, 1024), F32),
            vmem((5, 32, 1024), F32),
            vmem((6, 32, 1024), BF16),
            vmem((32, 1024), F32),
            vmem((3, 4, slots), F32),
            vmem((4, slots), F32),
            vmem((1, slots), jnp.int32),
            vmem((4, slots), jnp.int32),
            vmem((1, blocks), jnp.int32),
            vmem((6, 8, 32, LANES), F32),
            vmem((5, 8, 32, LANES), F32),
            vmem((6, 8, 32, LANES), F32),
            vmem((8, 32, LANES), F32),
            vmem((SWEEPS, 2, 5, 8, LANES), F32),
            vmem((SWEEPS, 2, 5, 8, LANES), F32),
            vmem((256, 1024), BF16),
            vmem((1024, slots), BF16),
            vmem((6, blocks, LANES), F32),
            vmem((4, blocks, LANES), F32),
            vmem((4, blocks, LANES), F32),
            vmem((96, slots * 4), BF16),
            vmem((128, slots * 4), BF16),
            pltpu.SemaphoreType.DMA((10,)),
            pltpu.SemaphoreType.DMA,
            pltpu.SemaphoreType.DMA((SWEEPS, 4)),
            pltpu.SemaphoreType.DMA((SWEEPS, 4)),
            pltpu.SemaphoreType.DMA,
            pltpu.SemaphoreType.DMA,
        ],
        compiler_params=pltpu.CompilerParams(
            collective_id=0, has_side_effects=True, vmem_limit_bytes=60 * 1024 * 1024
        ),
    )(
        init,
        rhs,
        flow,
        face,
        pseudo,
        jnp.transpose(coords, (1, 0, 2)),
        weights,
        cell.reshape(1, slots),
        vertex,
        count,
    )


def solution(mesh):
    return jax.shard_map(
        functools.partial(local, mesh.shape["grp"], mesh.shape["blk"]),
        mesh=mesh,
        in_specs=(
            P(None, "grp", "blk"),
            P(None, "grp", "blk"),
            P(None, "grp", "blk"),
            P(None, "grp", "blk"),
            P("grp", "blk"),
            P(None, None, ("grp", "blk")),
            P(None, ("grp", "blk")),
            P(("grp", "blk")),
            P(None, ("grp", "blk")),
            P(("grp", "blk"), None),
        ),
        out_specs=(P(None, "grp", "blk"), P(None, ("grp", "blk"))),
        check_vma=False,
    )
```

```python
import functools

import jax
import jax.numpy as jnp
from jax import lax
from jax.experimental import pallas as pl
from jax.experimental.pallas import tpu as pltpu
from jax.sharding import PartitionSpec as P

SWEEPS = 2
VERT_DEV = 1536
CAP = 32
LANES = 128
GAMMA = 1.4
LOCAL = 8
MESH = pl.DeviceIdType.MESH
F32 = jnp.float32
BF16 = jnp.bfloat16


def lane_iota(shape):
    return lax.broadcasted_iota(jnp.int32, shape, len(shape) - 1)


def row_iota(shape):
    return lax.broadcasted_iota(jnp.int32, shape, len(shape) - 2)


def cross(a, b):
    return [
        a[1] * b[2] - a[2] * b[1],
        a[2] * b[0] - a[0] * b[2],
        a[0] * b[1] - a[1] * b[0],
    ]


def kernel(
    groups,
    blocks,
    init_hbm,
    rhs_hbm,
    flow_hbm,
    face_hbm,
    pseudo_hbm,
    coords_hbm,
    weights_hbm,
    cell_hbm,
    vertex_hbm,
    count_hbm,
    adj_out,
    recv,
    adj_a,
    adj_b,
    adj_c,
    rhs,
    flow,
    face,
    pseudo,
    coords,
    weights,
    cell,
    vertex,
    count,
    gface,
    scaled,
    coef,
    press,
    y_send,
    y_recv,
    table,
    onehot,
    found,
    geom,
    send,
    load_sem,
    out_sem,
    halo_send,
    halo_recv,
    term_send,
    term_recv,
):
    group = lax.axis_index("grp")
    block = lax.axis_index("blk")
    columns = 8
    chunks = blocks // 8

    loads = [
        (flow_hbm, flow),
        (face_hbm, face),
        (pseudo_hbm, pseudo),
        (rhs_hbm, rhs),
        (cell_hbm, cell),
        (coords_hbm, coords),
        (weights_hbm, weights),
        (vertex_hbm, vertex),
        (count_hbm, count),
    ]
    for tile in range(columns):
        pltpu.make_async_copy(
            init_hbm.at[:, :, pl.ds(tile * LANES, LANES)],
            adj_a.at[:, 1 + tile, pl.ds(8, 32), :],
            load_sem.at[len(loads)],
        ).start()
    for position, (source, target) in enumerate(loads):
        pltpu.make_async_copy(source, target, load_sem.at[position]).start()

    def loaded(*wanted):
        for position, (source, target) in enumerate(loads):
            if any(target is one for one in wanted):
                pltpu.make_async_copy(source, target, load_sem.at[position]).wait()

    def inner(ref):
        return ref.at[:, pl.ds(1, columns), pl.ds(8, 32), :]

    grp_up = {"grp": lax.rem(group + 1, groups)}
    grp_down = {"grp": lax.rem(group + groups - 1, groups)}
    blk_up = {"blk": lax.rem(block + 1, blocks)}
    blk_down = {"blk": lax.rem(block + blocks - 1, blocks)}

    barrier = pltpu.get_barrier_semaphore()
    for device in (grp_up, grp_down):
        pl.semaphore_signal(barrier, inc=1, device_id=device, device_id_type=MESH)

    def greet(step, carry):
        pl.semaphore_signal(
            barrier,
            inc=1,
            device_id={"blk": lax.rem(block + step, blocks)},
            device_id_type=MESH,
        )
        return carry

    lax.fori_loop(1, blocks, greet, 0)

    tile_lane = lane_iota((8, LANES))
    lane_block = tile_lane // CAP

    def halo_copies(adj, sweep):
        span = pl.ds(1, columns)
        parts = [
            (adj.at[:, span, pl.ds(39, 1), :], adj.at[:, span, pl.ds(7, 1), :], grp_up),
            (adj.at[:, span, pl.ds(8, 1), :], adj.at[:, span, pl.ds(40, 1), :], grp_down),
            (y_send.at[sweep, 0], y_recv.at[sweep, 0], blk_up),
            (y_send.at[sweep, 1], y_recv.at[sweep, 1], blk_down),
        ]
        return [
            pltpu.make_async_remote_copy(
                src_ref=source,
                dst_ref=target,
                send_sem=halo_send.at[sweep, position],
                recv_sem=halo_recv.at[sweep, position],
                device_id=device,
                device_id_type=MESH,
            )
            for position, (source, target, device) in enumerate(parts)
        ]

    def pack(adj, sweep):
        for field in range(5):
            for side, tile, home in ((0, columns, 3), (1, 1, 0)):
                total = None
                for part in range(4):
                    value = adj[field, tile, pl.ds(8 + 8 * part, 8), :]
                    turn = (part - home) % 4 * CAP
                    if turn:
                        value = pltpu.roll(value, turn, 1)
                    total = value if total is None else jnp.where(lane_block == part, value, total)
                y_send[sweep, side, field] = total

    def unpack(adj, sweep):
        for field in range(5):
            for side, tile, home in ((0, 0, 3), (1, columns + 1, 0)):
                value = y_recv[sweep, side, field]
                for part in range(4):
                    turn = (home - part) % 4 * CAP
                    adj[field, tile, pl.ds(8 + 8 * part, 8), :] = (
                        pltpu.roll(value, turn, 1) if turn else value
                    )

    def sweep_tile(source, store, tile, part):
        rows = pl.ds(8 * part, 8)
        here = pl.ds(8 * part + 8, 8)
        center = [source[f, tile + 1, here, :] for f in range(5)]
        upper = [source[f, tile + 2, here, :] for f in range(5)]
        lower = [source[f, tile, here, :] for f in range(5)]
        pairs = [
            (
                [source[f, tile + 1, pl.ds(8 * part + 9, 8), :] for f in range(5)],
                [source[f, tile + 1, pl.ds(8 * part + 7, 8), :] for f in range(5)],
            ),
            (
                [
                    pltpu.roll(jnp.where(tile_lane >= CAP, center[f], upper[f]), LANES - CAP, 1)
                    for f in range(5)
                ],
                [
                    pltpu.roll(jnp.where(tile_lane < LANES - CAP, center[f], lower[f]), CAP, 1)
                    for f in range(5)
                ],
            ),
            (
                [pltpu.roll(center[f], LANES - 1, 1) for f in range(5)],
                [pltpu.roll(center[f], 1, 1) for f in range(5)],
            ),
        ]
        velocity = [coef[k, tile, rows, :] for k in range(3)]
        half_sq = coef[3, tile, rows, :]
        enthalpy = coef[4, tile, rows, :]
        reach = coef[5, tile, rows, :]
        sums = None
        moved = None
        flux = None
        first = []
        turned = None
        for axis, (plus, minus) in enumerate(pairs):
            g_plus = gface[2 * axis, tile, rows, :]
            g_minus = gface[2 * axis + 1, tile, rows, :]
            ahead = [g_plus * value for value in plus]
            behind = [g_minus * value for value in minus]
            diff = [a - b for a, b in zip(ahead, behind)]
            both = [a + b for a, b in zip(ahead, behind)]
            sums = both if sums is None else [a + b for a, b in zip(sums, both)]
            dot = (
                velocity[0] * diff[1]
                + velocity[1] * diff[2]
                + velocity[2] * diff[3]
                + enthalpy * diff[4]
            )
            first.append(diff[0] + dot)
            speed = velocity[axis]
            part_moved = [speed * diff[k] for k in range(1, 5)]
            moved = part_moved if moved is None else [a + b for a, b in zip(moved, part_moved)]
            flux = speed * dot if flux is None else flux + speed * dot
            turned = diff[1 + axis] if turned is None else turned + diff[1 + axis]
        turned = turned + moved[3]
        scaled_turn = (GAMMA - 1.0) * turned
        result = [half_sq * turned - flux]
        for k in range(3):
            result.append(first[k] - scaled_turn * velocity[k] + moved[k])
        result.append(scaled_turn + moved[3])
        for f in range(5):
            store(f, tile, part, scaled[f, tile, rows, :] + reach * sums[f] + result[f])

    def store_b(f, tile, part, value):
        adj_b[f, tile + 1, pl.ds(8 * part + 8, 8), :] = value

    def store_c(f, tile, part, value):
        adj_c[f, pl.ds(8 * part, 8), pl.ds(pl.multiple_of(tile * LANES, LANES), LANES)] = value

    def interior(source, store):
        def body(tile, carry):
            for part in (1, 2):
                sweep_tile(source, store, tile, part)
            return carry

        lax.fori_loop(1, columns - 1, body, 0, unroll=4)

    def boundary(source, store):
        def body(tile, carry):
            for part in (0, 3):
                sweep_tile(source, store, tile, part)
            return carry

        lax.fori_loop(0, columns, body, 0, unroll=4)

        def ends(step, carry):
            for part in (1, 2):
                sweep_tile(source, store, step * (columns - 1), part)
            return carry

        lax.fori_loop(0, 2, ends, 0)

    pltpu.make_async_copy(inner(adj_a), inner(adj_a), load_sem.at[len(loads)]).wait()
    pack(adj_a, 0)
    pl.semaphore_wait(barrier, blocks + 1)
    first_halo = halo_copies(adj_a, 0)
    for copy in first_halo:
        copy.start()

    loaded(flow, face, pseudo, rhs)
    tall_row = row_iota((16, LANES))
    tall_lane = lane_iota((16, LANES))

    def coefficients(step, carry):
        tile = step // 2
        half = step % 2
        rows = pl.ds(pl.multiple_of(half * 16, 16), 16)
        lanes = pl.ds(pl.multiple_of(tile * LANES, LANES), LANES)
        density = flow[0, rows, lanes]
        inverse = 1.0 / density
        velocity = [flow[1 + k, rows, lanes] * inverse for k in range(3)]
        energy = flow[4, rows, lanes]
        speed_sq = (
            velocity[0] * velocity[0] + velocity[1] * velocity[1] + velocity[2] * velocity[2]
        )
        pressure = (GAMMA - 1.0) * (energy - 0.5 * density * speed_sq)
        enthalpy = (energy + pressure) * inverse
        reach = jnp.sqrt(speed_sq) + jnp.sqrt(GAMMA * pressure * inverse)
        for k in range(3):
            coef[k, tile, rows, :] = velocity[k]
        coef[3, tile, rows, :] = 0.5 * (GAMMA - 1.0) * speed_sq
        coef[4, tile, rows, :] = enthalpy
        coef[5, tile, rows, :] = reach
        press[tile, rows, :] = pressure
        faces = [face[d, rows, lanes].astype(F32) for d in range(6)]
        open_sum = faces[0] + faces[1] + faces[2] + faces[3] + faces[4] + faces[5]
        share = 1.0 / (pseudo[rows, lanes] + 0.5 * reach * open_sum)
        half_share = 0.5 * share
        across = tall_row + half * 16
        along = tall_lane + tile * LANES
        height = tall_lane % 32
        outside = [
            (across == 31) & (group == groups - 1),
            (across == 0) & (group == 0),
            (along >= 992) & (block == blocks - 1),
            (along < 32) & (block == 0),
            height == 31,
            height == 0,
        ]
        for d in range(6):
            gface[d, tile, rows, :] = jnp.where(outside[d], 0.0, faces[d] * half_share)
        for f in range(5):
            scaled[f, tile, rows, :] = rhs[f, rows, lanes] * share
        return carry

    lax.fori_loop(0, 2 * columns, coefficients, 0, unroll=2)
    interior(adj_a, store_b)
    for copy in first_halo:
        copy.wait_recv()
    unpack(adj_a, 0)
    boundary(adj_a, store_b)

    pack(adj_b, 1)
    second_halo = halo_copies(adj_b, 1)
    for copy in second_halo:
        copy.start()
    interior(adj_b, store_c)

    loaded(cell, coords, weights, vertex, count)

    def pick_cells(chunk, carry):
        lanes = pl.ds(pl.multiple_of(chunk * 256, 256), 256)
        place = jnp.bitwise_and(cell[:, lanes], 1023)
        for band in range(8):
            rows = band * 128 + row_iota((128, 256))
            onehot[pl.ds(band * 128, 128), lanes] = jnp.where(rows == place, 1.0, 0.0).astype(BF16)
        return carry

    lax.fori_loop(0, chunks, pick_cells, 0)

    tile_row = row_iota((8, LANES))
    own_block = lane_block == tile_row % 4
    upper_half = tile_row < 4
    slot = tile_lane % CAP

    def spread(even, odd):
        value = jnp.where(own_block, jnp.where(upper_half, even, odd), 0.0)
        value = value + pltpu.roll(value, CAP, 1)
        return value + pltpu.roll(value, 2 * CAP, 1)

    def by_corner(values):
        total = values[3]
        for k in range(3):
            total = jnp.where(lane_block == k, values[k], total)
        return total

    def geometry(chunk, carry):
        even = pl.ds(pl.multiple_of(chunk * 256, 128), 128)
        odd = pl.ds(pl.multiple_of(chunk * 256 + 128, 128), 128)
        rows = pl.ds(pl.multiple_of(chunk * 8, 8), 8)
        corner = [
            [spread(coords[k, c : c + 1, even], coords[k, c : c + 1, odd]) for k in range(3)]
            for c in range(4)
        ]
        edge = [[corner[c][k] - corner[0][k] for k in range(3)] for c in range(1, 4)]
        grads = [
            [value / 6.0 for value in cross(edge[1], edge[2])],
            [value / 6.0 for value in cross(edge[2], edge[0])],
            [value / 6.0 for value in cross(edge[0], edge[1])],
        ]
        grad_zero = [-(grads[0][k] + grads[1][k] + grads[2][k]) for k in range(3)]
        side_two = [0.5 * (corner[3][k] - corner[1][k]) for k in range(3)]
        side_three = [-0.5 * (corner[2][k] - corner[1][k]) for k in range(3)]
        side_one = [-(side_two[k] + side_three[k]) for k in range(3)]
        weight = by_corner([spread(weights[c : c + 1, even], weights[c : c + 1, odd]) for c in range(4)])
        counts = jnp.broadcast_to(count[...], (8, blocks))
        wanted = lane_iota((8, blocks)) == chunk * 8 + row_iota((8, blocks))
        own_count = jnp.sum(jnp.where(wanted, counts, 0), axis=1, keepdims=True)
        weight = jnp.where(slot < own_count, weight, 0.0)
        for k in range(3):
            gradient = by_corner([grad_zero[k], grads[0][k], grads[1][k], grads[2][k]])
            side = by_corner([jnp.zeros_like(side_one[k]), side_one[k], side_two[k], side_three[k]])
            geom[k, rows, :] = weight * gradient
            geom[3 + k, rows, :] = weight * side
        send[3, rows, :] = by_corner(
            [
                spread(vertex[c : c + 1, even].astype(F32), vertex[c : c + 1, odd].astype(F32))
                for c in range(4)
            ]
        )
        return carry

    lax.fori_loop(0, chunks, geometry, 0, unroll=4)

    for copy in second_halo:
        copy.wait_recv()
    unpack(adj_b, 1)
    boundary(adj_b, store_c)
    adj_copy = pltpu.make_async_copy(adj_c, adj_out, out_sem.at[0])
    adj_copy.start()

    def fill_table(step, carry):
        tile = step // 2
        half = step % 2
        rows = pl.ds(pl.multiple_of(half * 16, 16), 16)
        lanes = pl.ds(pl.multiple_of(tile * LANES, LANES), LANES)
        pressure = press[tile, rows, :]
        for f in range(4):
            value = pressure * adj_c[1 + f, rows, lanes]
            high = value.astype(BF16)
            low = (value - high.astype(F32)).astype(BF16)
            table[pl.ds(pl.multiple_of(f * 32 + half * 16, 16), 16), lanes] = high
            table[pl.ds(pl.multiple_of(128 + f * 32 + half * 16, 16), 16), lanes] = low
        return carry

    lax.fori_loop(0, 2 * columns, fill_table, 0)

    found[...] = jnp.dot(table[...], onehot[...], preferred_element_type=F32)

    def terms(chunk, carry):
        lanes = pl.ds(pl.multiple_of(chunk * 256, 256), 256)
        rows = pl.ds(pl.multiple_of(chunk * 8, 8), 8)
        plane = jnp.right_shift(cell[:, lanes], 10)
        mine = row_iota((32, 256)) == plane
        fields = []
        for f in range(4):
            value = found[32 * f : 32 * f + 32, lanes] + found[128 + 32 * f : 160 + 32 * f, lanes]
            value = jnp.sum(jnp.where(mine, value, 0.0), axis=0, keepdims=True)
            fields.append(spread(value[:, :128], value[:, 128:]))
        b, a = fields[:3], fields[3]
        gradient = [geom[k, rows, :] for k in range(3)]
        side = [geom[3 + k, rows, :] for k in range(3)]
        turn = cross(side, b)
        for k in range(3):
            send[k, rows, :] = a * gradient[k] + turn[k]
        return carry

    lax.fori_loop(0, chunks, terms, 0, unroll=8)

    planes = blocks // LOCAL
    z, x, core = block // LOCAL, block % LOCAL // 2, block % 2

    def partner(step):
        far = step // LOCAL
        near = step % LOCAL
        return (
            lax.rem(z + far, planes) * LOCAL
            + lax.rem(x + near // 2, 4) * 2
            + lax.rem(core + near % 2, 2)
        )

    def post(step, carry):
        owner = partner(step)
        pltpu.make_async_remote_copy(
            src_ref=send.at[:, pl.ds(owner, 1), :],
            dst_ref=recv.at[:, pl.ds(step - 1, 1), :],
            send_sem=term_send,
            recv_sem=term_recv,
            device_id={"blk": owner},
            device_id_type=MESH,
        ).start()
        return carry

    lax.fori_loop(1, blocks, post, 0)
    own = pltpu.make_async_copy(
        send.at[:, pl.ds(block, 1), :], recv.at[:, pl.ds(blocks - 1, 1), :], out_sem.at[1]
    )
    own.start()
    others = pltpu.make_async_remote_copy(
        src_ref=send.at[:, pl.ds(0, blocks - 1), :],
        dst_ref=recv.at[:, pl.ds(0, blocks - 1), :],
        send_sem=term_send,
        recv_sem=term_recv,
        device_id=blk_up,
        device_id_type=MESH,
    )
    others.wait_recv()
    own.wait()

    for copy in first_halo + second_halo:
        copy.wait_send()
    others.wait_send()
    adj_copy.wait()


def vertex_sums(adj, recv_hbm, adj_out, sens_out, recv, held, left_op, right_op, recv_sem, in_sem, back_sem):
    recv_copy = pltpu.make_async_copy(recv_hbm, recv, recv_sem)
    recv_copy.start()
    inward = [
        pltpu.make_async_copy(adj.at[f], held.at[f], in_sem.at[f]) for f in range(5)
    ]
    outward = [
        pltpu.make_async_copy(held.at[f], adj_out.at[f], back_sem.at[f]) for f in range(5)
    ]
    for copy in inward:
        copy.start()
    for arriving, leaving in zip(inward, outward):
        arriving.wait()
        leaving.start()
    recv_copy.wait()
    chunks = recv.shape[1] // 8

    def operands(chunk, carry):
        rows = pl.ds(pl.multiple_of(chunk * 8, 8), 8)
        vertices = recv[3, rows, :].astype(jnp.int32)
        major = jnp.right_shift(vertices, 7)
        minor = jnp.bitwise_and(vertices, 127)
        halves = []
        for k in range(3):
            value = recv[k, rows, :]
            high = value.astype(BF16).astype(F32)
            halves += [high, value - high]
        for s in range(8):
            lanes = pl.ds(pl.multiple_of(chunk * 1024 + s * LANES, LANES), LANES)
            right_op[:, lanes] = jnp.where(row_iota((128, LANES)) == minor[s : s + 1], 1.0, 0.0).astype(BF16)
            hit = row_iota((16, LANES)) == major[s : s + 1]
            for n, value in enumerate(halves):
                left_op[pl.ds(16 * n, 16), lanes] = jnp.where(hit, value[s : s + 1], 0.0).astype(BF16)
        return carry

    lax.fori_loop(0, chunks, operands, 0)
    sums = lax.dot_general(
        left_op[...], right_op[...], (((1,), (1,)), ((), ())), preferred_element_type=F32
    )
    for k in range(3):
        both = sums[32 * k : 32 * k + 16] + sums[32 * k + 16 : 32 * k + 32]
        for h in range(VERT_DEV // LANES):
            sens_out[k : k + 1, h * LANES : (h + 1) * LANES] = both[h : h + 1]

    for copy in outward:
        copy.wait()


def local(groups, blocks, init, rhs, flow, face, pseudo, coords, weights, cell, vertex, count):
    slots = blocks * CAP
    vmem = pltpu.VMEM
    adjoint, received = pl.pallas_call(
        functools.partial(kernel, groups, blocks),
        out_shape=(
            jax.ShapeDtypeStruct((5, 32, 1024), F32),
            jax.ShapeDtypeStruct((4, blocks, LANES), F32),
        ),
        in_specs=[pl.BlockSpec(memory_space=pltpu.HBM)] * 10,
        out_specs=(
            pl.BlockSpec(memory_space=pl.ANY),
            pl.BlockSpec(memory_space=pl.ANY),
        ),
        scratch_shapes=[
            vmem((5, 10, 48, LANES), F32),
            vmem((5, 10, 48, LANES), F32),
            vmem((5, 32, 1024), F32),
            vmem((5, 32, 1024), F32),
            vmem((5, 32, 1024), F32),
            vmem((6, 32, 1024), BF16),
            vmem((32, 1024), F32),
            vmem((3, 4, slots), F32),
            vmem((4, slots), F32),
            vmem((1, slots), jnp.int32),
            vmem((4, slots), jnp.int32),
            vmem((1, blocks), jnp.int32),
            vmem((6, 8, 32, LANES), F32),
            vmem((5, 8, 32, LANES), F32),
            vmem((6, 8, 32, LANES), F32),
            vmem((8, 32, LANES), F32),
            vmem((SWEEPS, 2, 5, 8, LANES), F32),
            vmem((SWEEPS, 2, 5, 8, LANES), F32),
            vmem((256, 1024), BF16),
            vmem((1024, slots), BF16),
            vmem((256, slots), F32),
            vmem((6, blocks, LANES), F32),
            vmem((4, blocks, LANES), F32),
            pltpu.SemaphoreType.DMA((10,)),
            pltpu.SemaphoreType.DMA((2,)),
            pltpu.SemaphoreType.DMA((SWEEPS, 4)),
            pltpu.SemaphoreType.DMA((SWEEPS, 4)),
            pltpu.SemaphoreType.DMA,
            pltpu.SemaphoreType.DMA,
        ],
        compiler_params=pltpu.CompilerParams(
            collective_id=0, has_side_effects=True, vmem_limit_bytes=60 * 1024 * 1024
        ),
    )(
        init,
        rhs,
        flow,
        face,
        pseudo,
        jnp.transpose(coords, (1, 0, 2)),
        weights,
        cell.reshape(1, slots),
        vertex,
        count,
    )
    return pl.pallas_call(
        vertex_sums,
        out_shape=(
            jax.ShapeDtypeStruct((5, 32, 1024), F32),
            jax.ShapeDtypeStruct((3, VERT_DEV), F32),
        ),
        in_specs=[pl.BlockSpec(memory_space=pl.ANY)] * 2,
        out_specs=(
            pl.BlockSpec(memory_space=pl.ANY),
            pl.BlockSpec(memory_space=pltpu.VMEM),
        ),
        scratch_shapes=[
            vmem((4, blocks, LANES), F32),
            vmem((5, 32, 1024), F32),
            vmem((96, slots * 4), BF16),
            vmem((128, slots * 4), BF16),
            pltpu.SemaphoreType.DMA,
            pltpu.SemaphoreType.DMA((5,)),
            pltpu.SemaphoreType.DMA((5,)),
        ],
        compiler_params=pltpu.CompilerParams(vmem_limit_bytes=60 * 1024 * 1024),
    )(adjoint, received)


def solution(mesh):
    return jax.shard_map(
        functools.partial(local, mesh.shape["grp"], mesh.shape["blk"]),
        mesh=mesh,
        in_specs=(
            P(None, "grp", "blk"),
            P(None, "grp", "blk"),
            P(None, "grp", "blk"),
            P(None, "grp", "blk"),
            P("grp", "blk"),
            P(None, None, ("grp", "blk")),
            P(None, ("grp", "blk")),
            P(("grp", "blk")),
            P(None, ("grp", "blk")),
            P(("grp", "blk"), None),
        ),
        out_specs=(P(None, "grp", "blk"), P(None, ("grp", "blk"))),
        check_vma=False,
    )
```

```python
import functools

import jax
import jax.numpy as jnp
from jax import lax
from jax.experimental import pallas as pl
from jax.experimental.pallas import tpu as pltpu
from jax.sharding import PartitionSpec as P

VERT_DEV = 1536
CAP = 32
PLANES = 17
LANES = 128
GAMMA = 1.4
LOCAL = 8
MESH = pl.DeviceIdType.MESH
F32 = jnp.float32
BF16 = jnp.bfloat16


def lane_iota(shape):
    return lax.broadcasted_iota(jnp.int32, shape, len(shape) - 1)


def row_iota(shape):
    return lax.broadcasted_iota(jnp.int32, shape, len(shape) - 2)


def cross(a, b):
    return [
        a[1] * b[2] - a[2] * b[1],
        a[2] * b[0] - a[0] * b[2],
        a[0] * b[1] - a[1] * b[0],
    ]


def kernel(
    groups,
    blocks,
    init_hbm,
    rhs_hbm,
    flow_hbm,
    face_hbm,
    pseudo_hbm,
    coords_hbm,
    weights_hbm,
    cell_hbm,
    vertex_hbm,
    count_hbm,
    adj_out,
    recv,
    adj_a,
    adj_b,
    adj_c,
    rhs,
    flow,
    face,
    pseudo,
    coords,
    weights,
    cell,
    vertex,
    count,
    gface,
    scaled,
    coef,
    press,
    face_send,
    face_recv,
    edge_send,
    edge_recv,
    table,
    onehot,
    found,
    geom,
    send,
    load_sem,
    out_sem,
    halo_send,
    halo_recv,
    term_send,
    term_recv,
):
    group = lax.axis_index("grp")
    block = lax.axis_index("blk")
    columns = 8
    chunks = blocks // 8

    def loaded(*wanted):
        for position, (source, target) in enumerate(loads):
            if any(target is one for one in wanted):
                pltpu.make_async_copy(source, target, load_sem.at[position]).wait()

    def inner(ref):
        return ref.at[:, pl.ds(1, columns), pl.ds(8, 32), :]

    grp_up = {"grp": lax.rem(group + 1, groups)}
    grp_down = {"grp": lax.rem(group + groups - 1, groups)}
    blk_up = {"blk": lax.rem(block + 1, blocks)}
    blk_down = {"blk": lax.rem(block + blocks - 1, blocks)}

    barrier = pltpu.get_barrier_semaphore()
    diagonals = [[{**one, **two} for two in (blk_down, blk_up)] for one in (grp_down, grp_up)]
    for device in [grp_up, grp_down, blk_up, blk_down] + diagonals[0] + diagonals[1]:
        pl.semaphore_signal(barrier, inc=1, device_id=device, device_id_type=MESH)

    loads = [
        (flow_hbm, flow),
        (face_hbm, face),
        (pseudo_hbm, pseudo),
        (rhs_hbm, rhs),
        (cell_hbm, cell),
        (coords_hbm, coords),
        (weights_hbm, weights),
        (vertex_hbm, vertex),
        (count_hbm, count),
    ]
    for tile in range(columns):
        pltpu.make_async_copy(
            init_hbm.at[:, :, pl.ds(tile * LANES, LANES)],
            adj_a.at[:, 1 + tile, pl.ds(8, 32), :],
            load_sem.at[len(loads)],
        ).start()
    for position, (source, target) in enumerate(loads):
        pltpu.make_async_copy(source, target, load_sem.at[position]).start()

    def greet(step, carry):
        pl.semaphore_signal(
            barrier,
            inc=1,
            device_id={"blk": lax.rem(block + step, blocks)},
            device_id_type=MESH,
        )
        return carry

    lax.fori_loop(2, blocks - 1, greet, 0)

    tile_lane = lane_iota((8, LANES))
    tile_row = row_iota((8, LANES))
    lane_block = tile_lane // CAP

    first_end = (tile_row == 0) & (lane_block == 0)
    last_end = (tile_row == 7) & (lane_block == 3)

    def take_plane(read, side):
        if side < 2:
            row = 31 * side
            return jnp.concatenate([read(tile, row, 1) for tile in range(columns)], axis=0)
        tile, home = ((0, 0), (columns - 1, 3))[side - 2]
        total = None
        for part in range(4):
            value = read(tile, 8 * part, 8)
            turn = (part - home) % 4 * CAP
            if turn:
                value = pltpu.roll(value, turn, 1)
            total = value if total is None else jnp.where(lane_block == part, value, total)
        return total

    def in_adjoint(adj, field):
        return lambda tile, row, count: adj[field, tile + 1, pl.ds(8 + row, count), :]

    def in_table(ref, place):
        return lambda tile, row, count: ref[place, tile, pl.ds(row, count), :]

    def fill_face(side):
        for f in range(5):
            face_send[side, f] = take_plane(in_adjoint(adj_a, f), side)
            face_send[side, 5 + f] = take_plane(in_adjoint(adj_b, f), side)
            face_send[side, 10 + f] = take_plane(in_table(coef, (0, 1, 2, 4, 5)[f]), side)
        outward = 2 * (side // 2) + 1 - side % 2
        along = 2 - 2 * (side // 2)
        face_send[side, 15] = take_plane(in_table(gface, outward), side)
        face_send[side, 16] = jnp.where(
            first_end,
            take_plane(in_table(gface, along + 1), side),
            jnp.where(last_end, take_plane(in_table(gface, along), side), 0.0),
        )

    def fill_edge(upper_x, upper_y):
        tile, home = ((1, 0), (columns, 3))[upper_y]
        row = 8 + 31 * upper_x
        lines = [adj_a[f, tile, pl.ds(row, 1), :] for f in range(5)]
        value = jnp.concatenate(lines + [jnp.zeros((3, LANES), F32)], axis=0)
        value = jnp.where(lane_block == home, value, 0.0)
        value = value + pltpu.roll(value, CAP, 1)
        edge_send[upper_x, upper_y] = value + pltpu.roll(value, 2 * CAP, 1)

    def halo_copies():
        parts = [
            (face_send.at[side], face_recv.at[side + 1 - 2 * (side % 2)], device)
            for side, device in enumerate((grp_down, grp_up, blk_down, blk_up))
        ] + [
            (edge_send.at[i, j], edge_recv.at[1 - i, 1 - j], diagonals[i][j])
            for i in range(2)
            for j in range(2)
        ]
        return [
            pltpu.make_async_remote_copy(
                src_ref=source,
                dst_ref=target,
                send_sem=halo_send.at[position],
                recv_sem=halo_recv.at[position],
                device_id=device,
                device_id_type=MESH,
            )
            for position, (source, target, device) in enumerate(parts)
        ]

    def one_way(faces_of, side, axis, sign, weight, value):
        velocity = [faces_of[side, 10 + k] for k in range(3)]
        enthalpy = faces_of[side, 13]
        reach = faces_of[side, 14]
        half_sq = (0.5 * (GAMMA - 1.0)) * (
            velocity[0] * velocity[0] + velocity[1] * velocity[1] + velocity[2] * velocity[2]
        )
        speed = velocity[axis]
        dot = (
            velocity[0] * value[1]
            + velocity[1] * value[2]
            + velocity[2] * value[3]
            + enthalpy * value[4]
        )
        turned = value[1 + axis] + speed * value[4]
        scaled_turn = (GAMMA - 1.0) * turned
        result = [half_sq * turned - speed * dot]
        for k in range(3):
            entry = speed * value[1 + k] - scaled_turn * velocity[k]
            result.append(entry + value[0] + dot if k == axis else entry)
        result.append(scaled_turn + speed * value[4])
        steady, signed = weight * reach, weight * sign
        return [signed * result[f] + steady * value[f] for f in range(5)]

    def complete(side):
        axis, cross_axis = side // 2, 1 - side // 2
        sign = 2.0 * (side % 2) - 1.0
        mine = [face_send[side, f] for f in range(5)]
        theirs = [face_recv[side, f] for f in range(5)]
        gain = one_way(face_send, side, axis, sign, face_send[side, 15], theirs)
        outer = one_way(face_recv, side, axis, -sign, face_recv[side, 15], mine)
        if side < 2:
            ends = edge_recv[side, 0], edge_recv[side, 1]
        else:
            ends = edge_recv[0, side - 2], edge_recv[1, side - 2]
        corner = [
            jnp.where(last_end, ends[1][f : f + 1], jnp.where(first_end, ends[0][f : f + 1], 0.0))
            for f in range(5)
        ]
        end_sign = jnp.where(last_end, 1.0, -1.0)
        extra = one_way(face_recv, side, cross_axis, end_sign, face_recv[side, 16], corner)
        for f in range(5):
            halo = face_recv[side, 5 + f] + outer[f] + extra[f]
            if side < 2:
                own_row, halo_row = ((8, 7), (39, 40))[side]
                for tile in range(columns):
                    adj_b[f, 1 + tile, pl.ds(halo_row, 1), :] = halo[tile : tile + 1]
                    adj_b[f, 1 + tile, pl.ds(own_row, 1), :] = (
                        adj_b[f, 1 + tile, pl.ds(own_row, 1), :] + gain[f][tile : tile + 1]
                    )
            else:
                tile, home, halo_tile, halo_home = ((1, 0, 0, 3), (columns, 3, columns + 1, 0))[side - 2]
                for part in range(4):
                    rows = pl.ds(8 + 8 * part, 8)
                    turn = (halo_home - part) % 4 * CAP
                    adj_b[f, halo_tile, rows, :] = pltpu.roll(halo, turn, 1) if turn else halo
                    turn = (home - part) % 4 * CAP
                    moved = pltpu.roll(gain[f], turn, 1) if turn else gain[f]
                    adj_b[f, tile, rows, :] = adj_b[f, tile, rows, :] + jnp.where(
                        lane_block == home, moved, 0.0
                    )

    def sweep_tile(source, store, tile, part):
        rows = pl.ds(8 * part, 8)
        here = pl.ds(8 * part + 8, 8)
        center = [source[f, tile + 1, here, :] for f in range(5)]
        upper = [source[f, tile + 2, here, :] for f in range(5)]
        lower = [source[f, tile, here, :] for f in range(5)]
        pairs = [
            (
                [source[f, tile + 1, pl.ds(8 * part + 9, 8), :] for f in range(5)],
                [source[f, tile + 1, pl.ds(8 * part + 7, 8), :] for f in range(5)],
            ),
            (
                [
                    pltpu.roll(jnp.where(tile_lane >= CAP, center[f], upper[f]), LANES - CAP, 1)
                    for f in range(5)
                ],
                [
                    pltpu.roll(jnp.where(tile_lane < LANES - CAP, center[f], lower[f]), CAP, 1)
                    for f in range(5)
                ],
            ),
            (
                [pltpu.roll(center[f], LANES - 1, 1) for f in range(5)],
                [pltpu.roll(center[f], 1, 1) for f in range(5)],
            ),
        ]
        velocity = [coef[k, tile, rows, :] for k in range(3)]
        half_sq = coef[3, tile, rows, :]
        enthalpy = coef[4, tile, rows, :]
        reach = coef[5, tile, rows, :]
        sums = None
        moved = None
        flux = None
        first = []
        turned = None
        for axis, (plus, minus) in enumerate(pairs):
            g_plus = gface[2 * axis, tile, rows, :]
            g_minus = gface[2 * axis + 1, tile, rows, :]
            ahead = [g_plus * value for value in plus]
            behind = [g_minus * value for value in minus]
            diff = [a - b for a, b in zip(ahead, behind)]
            both = [a + b for a, b in zip(ahead, behind)]
            sums = both if sums is None else [a + b for a, b in zip(sums, both)]
            dot = (
                velocity[0] * diff[1]
                + velocity[1] * diff[2]
                + velocity[2] * diff[3]
                + enthalpy * diff[4]
            )
            first.append(diff[0] + dot)
            speed = velocity[axis]
            part_moved = [speed * diff[k] for k in range(1, 5)]
            moved = part_moved if moved is None else [a + b for a, b in zip(moved, part_moved)]
            flux = speed * dot if flux is None else flux + speed * dot
            turned = diff[1 + axis] if turned is None else turned + diff[1 + axis]
        turned = turned + moved[3]
        scaled_turn = (GAMMA - 1.0) * turned
        result = [half_sq * turned - flux]
        for k in range(3):
            result.append(first[k] - scaled_turn * velocity[k] + moved[k])
        result.append(scaled_turn + moved[3])
        for f in range(5):
            store(f, tile, part, scaled[f, tile, rows, :] + reach * sums[f] + result[f])

    def store_b(f, tile, part, value):
        adj_b[f, tile + 1, pl.ds(8 * part + 8, 8), :] = value

    def store_c(f, tile, part, value):
        adj_c[f, pl.ds(8 * part, 8), pl.ds(pl.multiple_of(tile * LANES, LANES), LANES)] = value

    def sweep(source, store):
        def body(tile, carry):
            for part in range(4):
                sweep_tile(source, store, tile, part)
            return carry

        lax.fori_loop(0, columns, body, 0, unroll=2)

    nothing = jnp.zeros((8, LANES), F32)
    for f in range(5):
        for tile in range(columns):
            adj_a[f, 1 + tile, pl.ds(0, 8), :] = nothing
            adj_a[f, 1 + tile, pl.ds(40, 8), :] = nothing
        for part in range(4):
            adj_a[f, 0, pl.ds(8 + 8 * part, 8), :] = nothing
            adj_a[f, columns + 1, pl.ds(8 + 8 * part, 8), :] = nothing

    loaded(flow, face, pseudo, rhs)
    tall_row = row_iota((16, LANES))
    tall_lane = lane_iota((16, LANES))

    def coefficients(step, carry):
        tile = step // 2
        half = step % 2
        rows = pl.ds(pl.multiple_of(half * 16, 16), 16)
        lanes = pl.ds(pl.multiple_of(tile * LANES, LANES), LANES)
        density = flow[0, rows, lanes]
        inverse = 1.0 / density
        velocity = [flow[1 + k, rows, lanes] * inverse for k in range(3)]
        energy = flow[4, rows, lanes]
        speed_sq = (
            velocity[0] * velocity[0] + velocity[1] * velocity[1] + velocity[2] * velocity[2]
        )
        pressure = (GAMMA - 1.0) * (energy - 0.5 * density * speed_sq)
        enthalpy = (energy + pressure) * inverse
        reach = jnp.sqrt(speed_sq) + jnp.sqrt(GAMMA * pressure * inverse)
        for k in range(3):
            coef[k, tile, rows, :] = velocity[k]
        coef[3, tile, rows, :] = 0.5 * (GAMMA - 1.0) * speed_sq
        coef[4, tile, rows, :] = enthalpy
        coef[5, tile, rows, :] = reach
        press[tile, rows, :] = pressure
        faces = [face[d, rows, lanes].astype(F32) for d in range(6)]
        open_sum = faces[0] + faces[1] + faces[2] + faces[3] + faces[4] + faces[5]
        share = 1.0 / (pseudo[rows, lanes] + 0.5 * reach * open_sum)
        half_share = 0.5 * share
        across = tall_row + half * 16
        along = tall_lane + tile * LANES
        height = tall_lane % 32
        outside = [
            (across == 31) & (group == groups - 1),
            (across == 0) & (group == 0),
            (along >= 992) & (block == blocks - 1),
            (along < 32) & (block == 0),
            height == 31,
            height == 0,
        ]
        for d in range(6):
            gface[d, tile, rows, :] = jnp.where(outside[d], 0.0, faces[d] * half_share)
        for f in range(5):
            scaled[f, tile, rows, :] = rhs[f, rows, lanes] * share
        return carry

    lax.fori_loop(0, 2 * columns, coefficients, 0, unroll=2)
    pltpu.make_async_copy(inner(adj_a), inner(adj_a), load_sem.at[len(loads)]).wait()
    sweep(adj_a, store_b)

    for side in range(4):
        fill_face(side)
    for i in range(2):
        for j in range(2):
            fill_edge(i, j)
    pl.semaphore_wait(barrier, blocks + 5)
    halo = halo_copies()
    for copy in halo:
        copy.start()

    loaded(cell, coords, weights, vertex, count)

    def pick_cells(chunk, carry):
        lanes = pl.ds(pl.multiple_of(chunk * 256, 256), 256)
        place = jnp.bitwise_and(cell[:, lanes], 1023)
        for band in range(8):
            rows = band * 128 + row_iota((128, 256))
            onehot[pl.ds(band * 128, 128), lanes] = jnp.where(rows == place, 1.0, 0.0).astype(BF16)
        return carry

    lax.fori_loop(0, chunks, pick_cells, 0)

    own_block = lane_block == tile_row % 4
    upper_half = tile_row < 4
    slot = tile_lane % CAP

    def spread(even, odd):
        value = jnp.where(own_block, jnp.where(upper_half, even, odd), 0.0)
        value = value + pltpu.roll(value, CAP, 1)
        return value + pltpu.roll(value, 2 * CAP, 1)

    def by_corner(values):
        total = values[3]
        for k in range(3):
            total = jnp.where(lane_block == k, values[k], total)
        return total

    def geometry(chunk, carry):
        even = pl.ds(pl.multiple_of(chunk * 256, 128), 128)
        odd = pl.ds(pl.multiple_of(chunk * 256 + 128, 128), 128)
        rows = pl.ds(pl.multiple_of(chunk * 8, 8), 8)
        corner = [
            [spread(coords[k, c : c + 1, even], coords[k, c : c + 1, odd]) for k in range(3)]
            for c in range(4)
        ]
        edge = [[corner[c][k] - corner[0][k] for k in range(3)] for c in range(1, 4)]
        grads = [
            [value / 6.0 for value in cross(edge[1], edge[2])],
            [value / 6.0 for value in cross(edge[2], edge[0])],
            [value / 6.0 for value in cross(edge[0], edge[1])],
        ]
        grad_zero = [-(grads[0][k] + grads[1][k] + grads[2][k]) for k in range(3)]
        side_two = [0.5 * (corner[3][k] - corner[1][k]) for k in range(3)]
        side_three = [-0.5 * (corner[2][k] - corner[1][k]) for k in range(3)]
        side_one = [-(side_two[k] + side_three[k]) for k in range(3)]
        weight = by_corner([spread(weights[c : c + 1, even], weights[c : c + 1, odd]) for c in range(4)])
        counts = jnp.broadcast_to(count[...], (8, blocks))
        wanted = lane_iota((8, blocks)) == chunk * 8 + row_iota((8, blocks))
        own_count = jnp.sum(jnp.where(wanted, counts, 0), axis=1, keepdims=True)
        weight = jnp.where(slot < own_count, weight, 0.0)
        for k in range(3):
            gradient = by_corner([grad_zero[k], grads[0][k], grads[1][k], grads[2][k]])
            side = by_corner([jnp.zeros_like(side_one[k]), side_one[k], side_two[k], side_three[k]])
            geom[k, rows, :] = weight * gradient
            geom[3 + k, rows, :] = weight * side
        send[3, rows, :] = by_corner(
            [
                spread(vertex[c : c + 1, even].astype(F32), vertex[c : c + 1, odd].astype(F32))
                for c in range(4)
            ]
        )
        return carry

    lax.fori_loop(0, chunks, geometry, 0, unroll=4)

    for copy in halo:
        copy.wait_recv()
    for side in range(4):
        complete(side)
    sweep(adj_b, store_c)
    adj_copy = pltpu.make_async_copy(adj_c, adj_out, out_sem.at[0])
    adj_copy.start()

    def fill_table(step, carry):
        tile = step // 2
        half = step % 2
        rows = pl.ds(pl.multiple_of(half * 16, 16), 16)
        lanes = pl.ds(pl.multiple_of(tile * LANES, LANES), LANES)
        pressure = press[tile, rows, :]
        for f in range(4):
            value = pressure * adj_c[1 + f, rows, lanes]
            high = value.astype(BF16)
            low = (value - high.astype(F32)).astype(BF16)
            table[pl.ds(pl.multiple_of(f * 32 + half * 16, 16), 16), lanes] = high
            table[pl.ds(pl.multiple_of(128 + f * 32 + half * 16, 16), 16), lanes] = low
        return carry

    lax.fori_loop(0, 2 * columns, fill_table, 0)

    found[...] = jnp.dot(table[...], onehot[...], preferred_element_type=F32)

    def terms(chunk, carry):
        lanes = pl.ds(pl.multiple_of(chunk * 256, 256), 256)
        rows = pl.ds(pl.multiple_of(chunk * 8, 8), 8)
        plane = jnp.right_shift(cell[:, lanes], 10)
        mine = row_iota((32, 256)) == plane
        fields = []
        for f in range(4):
            value = found[32 * f : 32 * f + 32, lanes] + found[128 + 32 * f : 160 + 32 * f, lanes]
            value = jnp.sum(jnp.where(mine, value, 0.0), axis=0, keepdims=True)
            fields.append(spread(value[:, :128], value[:, 128:]))
        b, a = fields[:3], fields[3]
        gradient = [geom[k, rows, :] for k in range(3)]
        side = [geom[3 + k, rows, :] for k in range(3)]
        turn = cross(side, b)
        for k in range(3):
            send[k, rows, :] = a * gradient[k] + turn[k]
        return carry

    lax.fori_loop(0, chunks, terms, 0, unroll=8)

    planes = blocks // LOCAL
    z, x, core = block // LOCAL, block % LOCAL // 2, block % 2

    def post(step, carry):
        turn = step // LOCAL
        far = planes // 2 + (1 - 2 * (turn % 2)) * ((turn + 1) // 2)
        near = LOCAL - 1 - step % LOCAL
        owner = (
            lax.rem(z + far, planes) * LOCAL
            + lax.rem(x + near // 2, 4) * 2
            + lax.rem(core + near % 2, 2)
        )
        pltpu.make_async_remote_copy(
            src_ref=send.at[:, pl.ds(owner, 1), :],
            dst_ref=recv.at[:, pl.ds(step, 1), :],
            send_sem=term_send,
            recv_sem=term_recv,
            device_id={"blk": owner},
            device_id_type=MESH,
        ).start()
        return carry

    lax.fori_loop(0, blocks - 1, post, 0)
    own = pltpu.make_async_copy(
        send.at[:, pl.ds(block, 1), :], recv.at[:, pl.ds(blocks - 1, 1), :], out_sem.at[1]
    )
    own.start()
    others = pltpu.make_async_remote_copy(
        src_ref=send.at[:, pl.ds(0, blocks - 1), :],
        dst_ref=recv.at[:, pl.ds(0, blocks - 1), :],
        send_sem=term_send,
        recv_sem=term_recv,
        device_id=blk_up,
        device_id_type=MESH,
    )
    others.wait_recv()
    own.wait()

    for copy in halo:
        copy.wait_send()
    others.wait_send()
    adj_copy.wait()


def vertex_sums(adj, recv_hbm, adj_out, sens_out, recv, held, left_op, right_op, recv_sem, in_sem, back_sem):
    recv_copy = pltpu.make_async_copy(recv_hbm, recv, recv_sem)
    recv_copy.start()
    inward = [
        pltpu.make_async_copy(adj.at[f], held.at[f], in_sem.at[f]) for f in range(5)
    ]
    outward = [
        pltpu.make_async_copy(held.at[f], adj_out.at[f], back_sem.at[f]) for f in range(5)
    ]
    for copy in inward:
        copy.start()
    for arriving, leaving in zip(inward, outward):
        arriving.wait()
        leaving.start()
    recv_copy.wait()
    chunks = recv.shape[1] // 8

    def operands(chunk, carry):
        rows = pl.ds(pl.multiple_of(chunk * 8, 8), 8)
        vertices = recv[3, rows, :].astype(jnp.int32)
        major = jnp.right_shift(vertices, 7)
        minor = jnp.bitwise_and(vertices, 127)
        halves = []
        for k in range(3):
            value = recv[k, rows, :]
            high = value.astype(BF16).astype(F32)
            halves += [high, value - high]
        for s in range(8):
            lanes = pl.ds(pl.multiple_of(chunk * 1024 + s * LANES, LANES), LANES)
            right_op[:, lanes] = jnp.where(row_iota((128, LANES)) == minor[s : s + 1], 1.0, 0.0).astype(BF16)
            hit = row_iota((16, LANES)) == major[s : s + 1]
            for n, value in enumerate(halves):
                left_op[pl.ds(16 * n, 16), lanes] = jnp.where(hit, value[s : s + 1], 0.0).astype(BF16)
        return carry

    lax.fori_loop(0, chunks, operands, 0)
    sums = lax.dot_general(
        left_op[...], right_op[...], (((1,), (1,)), ((), ())), preferred_element_type=F32
    )
    for k in range(3):
        both = sums[32 * k : 32 * k + 16] + sums[32 * k + 16 : 32 * k + 32]
        for h in range(VERT_DEV // LANES):
            sens_out[k : k + 1, h * LANES : (h + 1) * LANES] = both[h : h + 1]

    for copy in outward:
        copy.wait()


def local(groups, blocks, init, rhs, flow, face, pseudo, coords, weights, cell, vertex, count):
    slots = blocks * CAP
    vmem = pltpu.VMEM
    adjoint, received = pl.pallas_call(
        functools.partial(kernel, groups, blocks),
        out_shape=(
            jax.ShapeDtypeStruct((5, 32, 1024), F32),
            jax.ShapeDtypeStruct((4, blocks, LANES), F32),
        ),
        in_specs=[pl.BlockSpec(memory_space=pltpu.HBM)] * 10,
        out_specs=(
            pl.BlockSpec(memory_space=pl.ANY),
            pl.BlockSpec(memory_space=pl.ANY),
        ),
        scratch_shapes=[
            vmem((5, 10, 48, LANES), F32),
            vmem((5, 10, 48, LANES), F32),
            vmem((5, 32, 1024), F32),
            vmem((5, 32, 1024), F32),
            vmem((5, 32, 1024), F32),
            vmem((6, 32, 1024), BF16),
            vmem((32, 1024), F32),
            vmem((3, 4, slots), F32),
            vmem((4, slots), F32),
            vmem((1, slots), jnp.int32),
            vmem((4, slots), jnp.int32),
            vmem((1, blocks), jnp.int32),
            vmem((6, 8, 32, LANES), F32),
            vmem((5, 8, 32, LANES), F32),
            vmem((6, 8, 32, LANES), F32),
            vmem((8, 32, LANES), F32),
            vmem((4, PLANES, 8, LANES), F32),
            vmem((4, PLANES, 8, LANES), F32),
            vmem((2, 2, 8, LANES), F32),
            vmem((2, 2, 8, LANES), F32),
            vmem((256, 1024), BF16),
            vmem((1024, slots), BF16),
            vmem((256, slots), F32),
            vmem((6, blocks, LANES), F32),
            vmem((4, blocks, LANES), F32),
            pltpu.SemaphoreType.DMA((10,)),
            pltpu.SemaphoreType.DMA((2,)),
            pltpu.SemaphoreType.DMA((8,)),
            pltpu.SemaphoreType.DMA((8,)),
            pltpu.SemaphoreType.DMA,
            pltpu.SemaphoreType.DMA,
        ],
        compiler_params=pltpu.CompilerParams(
            collective_id=0, has_side_effects=True, vmem_limit_bytes=60 * 1024 * 1024
        ),
    )(
        init,
        rhs,
        flow,
        face,
        pseudo,
        jnp.transpose(coords, (1, 0, 2)),
        weights,
        cell.reshape(1, slots),
        vertex,
        count,
    )
    return pl.pallas_call(
        vertex_sums,
        out_shape=(
            jax.ShapeDtypeStruct((5, 32, 1024), F32),
            jax.ShapeDtypeStruct((3, VERT_DEV), F32),
        ),
        in_specs=[pl.BlockSpec(memory_space=pl.ANY)] * 2,
        out_specs=(
            pl.BlockSpec(memory_space=pl.ANY),
            pl.BlockSpec(memory_space=pltpu.VMEM),
        ),
        scratch_shapes=[
            vmem((4, blocks, LANES), F32),
            vmem((5, 32, 1024), F32),
            vmem((96, slots * 4), BF16),
            vmem((128, slots * 4), BF16),
            pltpu.SemaphoreType.DMA,
            pltpu.SemaphoreType.DMA((5,)),
            pltpu.SemaphoreType.DMA((5,)),
        ],
        compiler_params=pltpu.CompilerParams(vmem_limit_bytes=60 * 1024 * 1024),
    )(adjoint, received)


def solution(mesh):
    return jax.shard_map(
        functools.partial(local, mesh.shape["grp"], mesh.shape["blk"]),
        mesh=mesh,
        in_specs=(
            P(None, "grp", "blk"),
            P(None, "grp", "blk"),
            P(None, "grp", "blk"),
            P(None, "grp", "blk"),
            P("grp", "blk"),
            P(None, None, ("grp", "blk")),
            P(None, ("grp", "blk")),
            P(("grp", "blk")),
            P(None, ("grp", "blk")),
            P(("grp", "blk"), None),
        ),
        out_specs=(P(None, "grp", "blk"), P(None, ("grp", "blk"))),
        check_vma=False,
    )
```

```python
import functools

import jax
import jax.numpy as jnp
from jax import lax
from jax.experimental import pallas as pl
from jax.experimental.pallas import tpu as pltpu
from jax.sharding import PartitionSpec as P

VERT_DEV = 1536
CAP = 32
PLANES = 17
LANES = 128
GAMMA = 1.4
LOCAL = 8
MESH = pl.DeviceIdType.MESH
F32 = jnp.float32
BF16 = jnp.bfloat16


def lane_iota(shape):
    return lax.broadcasted_iota(jnp.int32, shape, len(shape) - 1)


def row_iota(shape):
    return lax.broadcasted_iota(jnp.int32, shape, len(shape) - 2)


def cross(a, b):
    return [
        a[1] * b[2] - a[2] * b[1],
        a[2] * b[0] - a[0] * b[2],
        a[0] * b[1] - a[1] * b[0],
    ]


def kernel(
    groups,
    blocks,
    init_hbm,
    rhs_hbm,
    flow_hbm,
    face_hbm,
    pseudo_hbm,
    coords_hbm,
    weights_hbm,
    cell_hbm,
    vertex_hbm,
    count_hbm,
    adj_out,
    recv,
    adj_a,
    adj_b,
    adj_c,
    rhs,
    flow,
    face,
    pseudo,
    coords,
    weights,
    cell,
    vertex,
    count,
    gface,
    scaled,
    coef,
    press,
    face_send,
    face_recv,
    edge_send,
    edge_recv,
    table,
    onehot,
    found,
    geom,
    send,
    load_sem,
    out_sem,
    halo_send,
    halo_recv,
    term_send,
    term_recv,
    plane_sem,
):
    group = lax.axis_index("grp")
    block = lax.axis_index("blk")
    columns = 8
    chunks = blocks // 8

    def loaded(*wanted):
        for position, (source, target) in enumerate(loads):
            if any(target is one for one in wanted):
                pltpu.make_async_copy(source, target, load_sem.at[position]).wait()

    def inner(ref):
        return ref.at[:, pl.ds(1, columns), pl.ds(8, 32), :]

    grp_up = {"grp": lax.rem(group + 1, groups)}
    grp_down = {"grp": lax.rem(group + groups - 1, groups)}
    blk_up = {"blk": lax.rem(block + 1, blocks)}
    blk_down = {"blk": lax.rem(block + blocks - 1, blocks)}

    barrier = pltpu.get_barrier_semaphore()
    diagonals = [[{**one, **two} for two in (blk_down, blk_up)] for one in (grp_down, grp_up)]
    for device in [grp_up, grp_down, blk_up, blk_down] + diagonals[0] + diagonals[1]:
        pl.semaphore_signal(barrier, inc=1, device_id=device, device_id_type=MESH)

    loads = [
        (flow_hbm, flow),
        (face_hbm, face),
        (pseudo_hbm, pseudo),
        (rhs_hbm, rhs),
        (cell_hbm, cell),
        (coords_hbm, coords),
        (weights_hbm, weights),
        (vertex_hbm, vertex),
        (count_hbm, count),
    ]
    for tile in range(columns):
        pltpu.make_async_copy(
            init_hbm.at[:, :, pl.ds(tile * LANES, LANES)],
            adj_a.at[:, 1 + tile, pl.ds(8, 32), :],
            load_sem.at[len(loads)],
        ).start()
    for position, (source, target) in enumerate(loads):
        pltpu.make_async_copy(source, target, load_sem.at[position]).start()

    planes = blocks // LOCAL
    z, x, core = block // LOCAL, block % LOCAL // 2, block % 2
    for step in range(1, LOCAL):
        beside = z * LOCAL + lax.rem(x + step // 2, 4) * 2 + lax.rem(core + step % 2, 2)
        pl.semaphore_signal(barrier, inc=1, device_id={"blk": beside}, device_id_type=MESH)
    column = [
        {"blk": lax.rem(z + step, planes) * LOCAL + block % LOCAL} for step in range(1, planes)
    ]
    for device in column:
        pl.semaphore_signal(barrier, inc=1, device_id=device, device_id_type=MESH)

    tile_lane = lane_iota((8, LANES))
    tile_row = row_iota((8, LANES))
    lane_block = tile_lane // CAP

    first_end = (tile_row == 0) & (lane_block == 0)
    last_end = (tile_row == 7) & (lane_block == 3)

    def take_plane(read, side):
        if side < 2:
            row = 31 * side
            return jnp.concatenate([read(tile, row, 1) for tile in range(columns)], axis=0)
        tile, home = ((0, 0), (columns - 1, 3))[side - 2]
        total = None
        for part in range(4):
            value = read(tile, 8 * part, 8)
            turn = (part - home) % 4 * CAP
            if turn:
                value = pltpu.roll(value, turn, 1)
            total = value if total is None else jnp.where(lane_block == part, value, total)
        return total

    def in_adjoint(adj, field):
        return lambda tile, row, count: adj[field, tile + 1, pl.ds(8 + row, count), :]

    def in_table(ref, place):
        return lambda tile, row, count: ref[place, tile, pl.ds(row, count), :]

    def fill_face(side):
        for f in range(5):
            face_send[side, f] = take_plane(in_adjoint(adj_a, f), side)
            face_send[side, 5 + f] = take_plane(in_adjoint(adj_b, f), side)
            face_send[side, 10 + f] = take_plane(in_table(coef, (0, 1, 2, 4, 5)[f]), side)
        outward = 2 * (side // 2) + 1 - side % 2
        along = 2 - 2 * (side // 2)
        face_send[side, 15] = take_plane(in_table(gface, outward), side)
        face_send[side, 16] = jnp.where(
            first_end,
            take_plane(in_table(gface, along + 1), side),
            jnp.where(last_end, take_plane(in_table(gface, along), side), 0.0),
        )

    def fill_edge(upper_x, upper_y):
        tile, home = ((1, 0), (columns, 3))[upper_y]
        row = 8 + 31 * upper_x
        lines = [adj_a[f, tile, pl.ds(row, 1), :] for f in range(5)]
        value = jnp.concatenate(lines + [jnp.zeros((3, LANES), F32)], axis=0)
        value = jnp.where(lane_block == home, value, 0.0)
        value = value + pltpu.roll(value, CAP, 1)
        edge_send[upper_x, upper_y] = value + pltpu.roll(value, 2 * CAP, 1)

    def halo_copies():
        parts = [
            (face_send.at[side], face_recv.at[side + 1 - 2 * (side % 2)], device)
            for side, device in enumerate((grp_down, grp_up, blk_down, blk_up))
        ] + [
            (edge_send.at[i, j], edge_recv.at[1 - i, 1 - j], diagonals[i][j])
            for i in range(2)
            for j in range(2)
        ]
        return [
            pltpu.make_async_remote_copy(
                src_ref=source,
                dst_ref=target,
                send_sem=halo_send.at[position],
                recv_sem=halo_recv.at[position],
                device_id=device,
                device_id_type=MESH,
            )
            for position, (source, target, device) in enumerate(parts)
        ]

    def one_way(faces_of, side, axis, sign, weight, value):
        velocity = [faces_of[side, 10 + k] for k in range(3)]
        enthalpy = faces_of[side, 13]
        reach = faces_of[side, 14]
        half_sq = (0.5 * (GAMMA - 1.0)) * (
            velocity[0] * velocity[0] + velocity[1] * velocity[1] + velocity[2] * velocity[2]
        )
        speed = velocity[axis]
        dot = (
            velocity[0] * value[1]
            + velocity[1] * value[2]
            + velocity[2] * value[3]
            + enthalpy * value[4]
        )
        turned = value[1 + axis] + speed * value[4]
        scaled_turn = (GAMMA - 1.0) * turned
        result = [half_sq * turned - speed * dot]
        for k in range(3):
            entry = speed * value[1 + k] - scaled_turn * velocity[k]
            result.append(entry + value[0] + dot if k == axis else entry)
        result.append(scaled_turn + speed * value[4])
        steady, signed = weight * reach, weight * sign
        return [signed * result[f] + steady * value[f] for f in range(5)]

    def complete(side):
        axis, cross_axis = side // 2, 1 - side // 2
        sign = 2.0 * (side % 2) - 1.0
        mine = [face_send[side, f] for f in range(5)]
        theirs = [face_recv[side, f] for f in range(5)]
        gain = one_way(face_send, side, axis, sign, face_send[side, 15], theirs)
        outer = one_way(face_recv, side, axis, -sign, face_recv[side, 15], mine)
        if side < 2:
            ends = edge_recv[side, 0], edge_recv[side, 1]
        else:
            ends = edge_recv[0, side - 2], edge_recv[1, side - 2]
        corner = [
            jnp.where(last_end, ends[1][f : f + 1], jnp.where(first_end, ends[0][f : f + 1], 0.0))
            for f in range(5)
        ]
        end_sign = jnp.where(last_end, 1.0, -1.0)
        extra = one_way(face_recv, side, cross_axis, end_sign, face_recv[side, 16], corner)
        for f in range(5):
            halo = face_recv[side, 5 + f] + outer[f] + extra[f]
            if side < 2:
                own_row, halo_row = ((8, 7), (39, 40))[side]
                for tile in range(columns):
                    adj_b[f, 1 + tile, pl.ds(halo_row, 1), :] = halo[tile : tile + 1]
                    adj_b[f, 1 + tile, pl.ds(own_row, 1), :] = (
                        adj_b[f, 1 + tile, pl.ds(own_row, 1), :] + gain[f][tile : tile + 1]
                    )
            else:
                tile, home, halo_tile, halo_home = ((1, 0, 0, 3), (columns, 3, columns + 1, 0))[side - 2]
                for part in range(4):
                    rows = pl.ds(8 + 8 * part, 8)
                    turn = (halo_home - part) % 4 * CAP
                    adj_b[f, halo_tile, rows, :] = pltpu.roll(halo, turn, 1) if turn else halo
                    turn = (home - part) % 4 * CAP
                    moved = pltpu.roll(gain[f], turn, 1) if turn else gain[f]
                    adj_b[f, tile, rows, :] = adj_b[f, tile, rows, :] + jnp.where(
                        lane_block == home, moved, 0.0
                    )

    def sweep_tile(source, store, tile, part):
        rows = pl.ds(8 * part, 8)
        here = pl.ds(8 * part + 8, 8)
        center = [source[f, tile + 1, here, :] for f in range(5)]
        upper = [source[f, tile + 2, here, :] for f in range(5)]
        lower = [source[f, tile, here, :] for f in range(5)]
        pairs = [
            (
                [source[f, tile + 1, pl.ds(8 * part + 9, 8), :] for f in range(5)],
                [source[f, tile + 1, pl.ds(8 * part + 7, 8), :] for f in range(5)],
            ),
            (
                [
                    pltpu.roll(jnp.where(tile_lane >= CAP, center[f], upper[f]), LANES - CAP, 1)
                    for f in range(5)
                ],
                [
                    pltpu.roll(jnp.where(tile_lane < LANES - CAP, center[f], lower[f]), CAP, 1)
                    for f in range(5)
                ],
            ),
            (
                [pltpu.roll(center[f], LANES - 1, 1) for f in range(5)],
                [pltpu.roll(center[f], 1, 1) for f in range(5)],
            ),
        ]
        velocity = [coef[k, tile, rows, :] for k in range(3)]
        half_sq = coef[3, tile, rows, :]
        enthalpy = coef[4, tile, rows, :]
        reach = coef[5, tile, rows, :]
        sums = None
        moved = None
        flux = None
        first = []
        turned = None
        for axis, (plus, minus) in enumerate(pairs):
            g_plus = gface[2 * axis, tile, rows, :]
            g_minus = gface[2 * axis + 1, tile, rows, :]
            ahead = [g_plus * value for value in plus]
            behind = [g_minus * value for value in minus]
            diff = [a - b for a, b in zip(ahead, behind)]
            both = [a + b for a, b in zip(ahead, behind)]
            sums = both if sums is None else [a + b for a, b in zip(sums, both)]
            dot = (
                velocity[0] * diff[1]
                + velocity[1] * diff[2]
                + velocity[2] * diff[3]
                + enthalpy * diff[4]
            )
            first.append(diff[0] + dot)
            speed = velocity[axis]
            part_moved = [speed * diff[k] for k in range(1, 5)]
            moved = part_moved if moved is None else [a + b for a, b in zip(moved, part_moved)]
            flux = speed * dot if flux is None else flux + speed * dot
            turned = diff[1 + axis] if turned is None else turned + diff[1 + axis]
        turned = turned + moved[3]
        scaled_turn = (GAMMA - 1.0) * turned
        result = [half_sq * turned - flux]
        for k in range(3):
            result.append(first[k] - scaled_turn * velocity[k] + moved[k])
        result.append(scaled_turn + moved[3])
        for f in range(5):
            store(f, tile, part, scaled[f, tile, rows, :] + reach * sums[f] + result[f])

    def store_b(f, tile, part, value):
        adj_b[f, tile + 1, pl.ds(8 * part + 8, 8), :] = value

    def store_c(f, tile, part, value):
        adj_c[f, pl.ds(8 * part, 8), pl.ds(pl.multiple_of(tile * LANES, LANES), LANES)] = value

    def sweep(source, store):
        def body(tile, carry):
            for part in range(4):
                sweep_tile(source, store, tile, part)
            return carry

        lax.fori_loop(0, columns, body, 0, unroll=2)

    nothing = jnp.zeros((8, LANES), F32)
    for f in range(5):
        for tile in range(columns):
            adj_a[f, 1 + tile, pl.ds(0, 8), :] = nothing
            adj_a[f, 1 + tile, pl.ds(40, 8), :] = nothing
        for part in range(4):
            adj_a[f, 0, pl.ds(8 + 8 * part, 8), :] = nothing
            adj_a[f, columns + 1, pl.ds(8 + 8 * part, 8), :] = nothing

    loaded(flow, face, pseudo, rhs)
    tall_row = row_iota((16, LANES))
    tall_lane = lane_iota((16, LANES))

    def coefficients(step, carry):
        tile = step // 2
        half = step % 2
        rows = pl.ds(pl.multiple_of(half * 16, 16), 16)
        lanes = pl.ds(pl.multiple_of(tile * LANES, LANES), LANES)
        density = flow[0, rows, lanes]
        inverse = 1.0 / density
        velocity = [flow[1 + k, rows, lanes] * inverse for k in range(3)]
        energy = flow[4, rows, lanes]
        speed_sq = (
            velocity[0] * velocity[0] + velocity[1] * velocity[1] + velocity[2] * velocity[2]
        )
        pressure = (GAMMA - 1.0) * (energy - 0.5 * density * speed_sq)
        enthalpy = (energy + pressure) * inverse
        reach = jnp.sqrt(speed_sq) + jnp.sqrt(GAMMA * pressure * inverse)
        for k in range(3):
            coef[k, tile, rows, :] = velocity[k]
        coef[3, tile, rows, :] = 0.5 * (GAMMA - 1.0) * speed_sq
        coef[4, tile, rows, :] = enthalpy
        coef[5, tile, rows, :] = reach
        press[tile, rows, :] = pressure
        faces = [face[d, rows, lanes].astype(F32) for d in range(6)]
        open_sum = faces[0] + faces[1] + faces[2] + faces[3] + faces[4] + faces[5]
        share = 1.0 / (pseudo[rows, lanes] + 0.5 * reach * open_sum)
        half_share = 0.5 * share
        across = tall_row + half * 16
        along = tall_lane + tile * LANES
        height = tall_lane % 32
        outside = [
            (across == 31) & (group == groups - 1),
            (across == 0) & (group == 0),
            (along >= 992) & (block == blocks - 1),
            (along < 32) & (block == 0),
            height == 31,
            height == 0,
        ]
        for d in range(6):
            gface[d, tile, rows, :] = jnp.where(outside[d], 0.0, faces[d] * half_share)
        for f in range(5):
            scaled[f, tile, rows, :] = rhs[f, rows, lanes] * share
        return carry

    lax.fori_loop(0, 2 * columns, coefficients, 0, unroll=2)
    pltpu.make_async_copy(inner(adj_a), inner(adj_a), load_sem.at[len(loads)]).wait()
    sweep(adj_a, store_b)

    for side in range(4):
        fill_face(side)
    for i in range(2):
        for j in range(2):
            fill_edge(i, j)
    pl.semaphore_wait(barrier, 8 + LOCAL - 1 + planes - 1)
    halo = halo_copies()
    for copy in halo:
        copy.start()
    for device in column:
        pl.semaphore_signal(plane_sem, inc=1, device_id=device, device_id_type=MESH)

    loaded(cell, coords, weights, vertex, count)

    def pick_cells(chunk, carry):
        lanes = pl.ds(pl.multiple_of(chunk * 256, 256), 256)
        place = jnp.bitwise_and(cell[:, lanes], 1023)
        for band in range(8):
            rows = band * 128 + row_iota((128, 256))
            onehot[pl.ds(band * 128, 128), lanes] = jnp.where(rows == place, 1.0, 0.0).astype(BF16)
        return carry

    lax.fori_loop(0, chunks, pick_cells, 0)

    own_block = lane_block == tile_row % 4
    upper_half = tile_row < 4
    slot = tile_lane % CAP

    def spread(even, odd):
        value = jnp.where(own_block, jnp.where(upper_half, even, odd), 0.0)
        value = value + pltpu.roll(value, CAP, 1)
        return value + pltpu.roll(value, 2 * CAP, 1)

    def by_corner(values):
        total = values[3]
        for k in range(3):
            total = jnp.where(lane_block == k, values[k], total)
        return total

    def geometry(chunk, carry):
        even = pl.ds(pl.multiple_of(chunk * 256, 128), 128)
        odd = pl.ds(pl.multiple_of(chunk * 256 + 128, 128), 128)
        rows = pl.ds(pl.multiple_of(chunk * 8, 8), 8)
        corner = [
            [spread(coords[k, c : c + 1, even], coords[k, c : c + 1, odd]) for k in range(3)]
            for c in range(4)
        ]
        edge = [[corner[c][k] - corner[0][k] for k in range(3)] for c in range(1, 4)]
        grads = [
            [value / 6.0 for value in cross(edge[1], edge[2])],
            [value / 6.0 for value in cross(edge[2], edge[0])],
            [value / 6.0 for value in cross(edge[0], edge[1])],
        ]
        grad_zero = [-(grads[0][k] + grads[1][k] + grads[2][k]) for k in range(3)]
        side_two = [0.5 * (corner[3][k] - corner[1][k]) for k in range(3)]
        side_three = [-0.5 * (corner[2][k] - corner[1][k]) for k in range(3)]
        side_one = [-(side_two[k] + side_three[k]) for k in range(3)]
        weight = by_corner([spread(weights[c : c + 1, even], weights[c : c + 1, odd]) for c in range(4)])
        counts = jnp.broadcast_to(count[...], (8, blocks))
        wanted = lane_iota((8, blocks)) == chunk * 8 + row_iota((8, blocks))
        own_count = jnp.sum(jnp.where(wanted, counts, 0), axis=1, keepdims=True)
        weight = jnp.where(slot < own_count, weight, 0.0)
        for k in range(3):
            gradient = by_corner([grad_zero[k], grads[0][k], grads[1][k], grads[2][k]])
            side = by_corner([jnp.zeros_like(side_one[k]), side_one[k], side_two[k], side_three[k]])
            geom[k, rows, :] = weight * gradient
            geom[3 + k, rows, :] = weight * side
        send[3, rows, :] = by_corner(
            [
                spread(vertex[c : c + 1, even].astype(F32), vertex[c : c + 1, odd].astype(F32))
                for c in range(4)
            ]
        )
        return carry

    lax.fori_loop(0, chunks, geometry, 0, unroll=4)

    for copy in halo:
        copy.wait_recv()
    for side in range(4):
        complete(side)
    sweep(adj_b, store_c)
    adj_copy = pltpu.make_async_copy(adj_c, adj_out, out_sem.at[0])
    adj_copy.start()

    def fill_table(step, carry):
        tile = step // 2
        half = step % 2
        rows = pl.ds(pl.multiple_of(half * 16, 16), 16)
        lanes = pl.ds(pl.multiple_of(tile * LANES, LANES), LANES)
        pressure = press[tile, rows, :]
        for f in range(4):
            value = pressure * adj_c[1 + f, rows, lanes]
            high = value.astype(BF16)
            low = (value - high.astype(F32)).astype(BF16)
            table[pl.ds(pl.multiple_of(f * 32 + half * 16, 16), 16), lanes] = high
            table[pl.ds(pl.multiple_of(128 + f * 32 + half * 16, 16), 16), lanes] = low
        return carry

    lax.fori_loop(0, 2 * columns, fill_table, 0)

    found[...] = jnp.dot(table[...], onehot[...], preferred_element_type=F32)

    def terms(chunk, carry):
        lanes = pl.ds(pl.multiple_of(chunk * 256, 256), 256)
        rows = pl.ds(pl.multiple_of(chunk * 8, 8), 8)
        plane = jnp.right_shift(cell[:, lanes], 10)
        mine = row_iota((32, 256)) == plane
        fields = []
        for f in range(4):
            value = found[32 * f : 32 * f + 32, lanes] + found[128 + 32 * f : 160 + 32 * f, lanes]
            value = jnp.sum(jnp.where(mine, value, 0.0), axis=0, keepdims=True)
            fields.append(spread(value[:, :128], value[:, 128:]))
        b, a = fields[:3], fields[3]
        gradient = [geom[k, rows, :] for k in range(3)]
        side = [geom[3 + k, rows, :] for k in range(3)]
        turn = cross(side, b)
        for k in range(3):
            send[k, rows, :] = a * gradient[k] + turn[k]
        return carry

    lax.fori_loop(0, chunks, terms, 0, unroll=8)

    if planes > 1:
        pl.semaphore_wait(plane_sem, planes - 1)

    def post(step, carry):
        turn = step // LOCAL
        far = planes // 2 + (1 - 2 * (turn % 2)) * ((turn + 1) // 2)
        near = LOCAL - 1 - step % LOCAL
        owner = (
            lax.rem(z + far, planes) * LOCAL
            + lax.rem(x + near // 2, 4) * 2
            + lax.rem(core + near % 2, 2)
        )
        pltpu.make_async_remote_copy(
            src_ref=send.at[:, pl.ds(owner, 1), :],
            dst_ref=recv.at[:, pl.ds(step, 1), :],
            send_sem=term_send,
            recv_sem=term_recv,
            device_id={"blk": owner},
            device_id_type=MESH,
        ).start()
        return carry

    lax.fori_loop(0, blocks - 1, post, 0)
    own = pltpu.make_async_copy(
        send.at[:, pl.ds(block, 1), :], recv.at[:, pl.ds(blocks - 1, 1), :], out_sem.at[1]
    )
    own.start()
    others = pltpu.make_async_remote_copy(
        src_ref=send.at[:, pl.ds(0, blocks - 1), :],
        dst_ref=recv.at[:, pl.ds(0, blocks - 1), :],
        send_sem=term_send,
        recv_sem=term_recv,
        device_id=blk_up,
        device_id_type=MESH,
    )
    others.wait_recv()
    own.wait()

    for copy in halo:
        copy.wait_send()
    others.wait_send()
    adj_copy.wait()


def vertex_sums(adj, recv_hbm, adj_out, sens_out, recv, held, left_op, right_op, recv_sem, in_sem, back_sem):
    recv_copy = pltpu.make_async_copy(recv_hbm, recv, recv_sem)
    recv_copy.start()
    inward = [
        pltpu.make_async_copy(adj.at[f], held.at[f], in_sem.at[f]) for f in range(5)
    ]
    outward = [
        pltpu.make_async_copy(held.at[f], adj_out.at[f], back_sem.at[f]) for f in range(5)
    ]
    for copy in inward:
        copy.start()
    for arriving, leaving in zip(inward, outward):
        arriving.wait()
        leaving.start()
    recv_copy.wait()
    chunks = recv.shape[1] // 8

    bands = [(row_iota((16, LANES)) + 16 * band).astype(F32).astype(BF16) for band in range(8)]
    one, zero = jnp.ones((16, LANES), BF16), jnp.zeros((16, LANES), BF16)

    def operands(chunk, carry):
        rows = pl.ds(pl.multiple_of(chunk * 8, 8), 8)
        vertices = recv[3, rows, :].astype(jnp.int32)
        major = jnp.right_shift(vertices, 7)
        minor = jnp.bitwise_and(vertices, 127)
        halves = []
        for k in range(3):
            value = recv[k, rows, :]
            high = value.astype(BF16).astype(F32)
            halves += [high, value - high]
        for s in range(8):
            lanes = pl.ds(pl.multiple_of(chunk * 1024 + s * LANES, LANES), LANES)
            low = jnp.broadcast_to(minor[s : s + 1].astype(F32), (16, LANES)).astype(BF16)
            for band in range(8):
                right_op[pl.ds(16 * band, 16), lanes] = jnp.where(low == bands[band], one, zero)
            hit = row_iota((16, LANES)) == major[s : s + 1]
            for n, value in enumerate(halves):
                left_op[pl.ds(16 * n, 16), lanes] = jnp.where(hit, value[s : s + 1], 0.0).astype(BF16)
        return carry

    lax.fori_loop(0, chunks, operands, 0)
    sums = lax.dot_general(
        left_op[...], right_op[...], (((1,), (1,)), ((), ())), preferred_element_type=F32
    )
    for k in range(3):
        both = sums[32 * k : 32 * k + 16] + sums[32 * k + 16 : 32 * k + 32]
        for h in range(VERT_DEV // LANES):
            sens_out[k : k + 1, h * LANES : (h + 1) * LANES] = both[h : h + 1]

    for copy in outward:
        copy.wait()


def local(groups, blocks, init, rhs, flow, face, pseudo, coords, weights, cell, vertex, count):
    slots = blocks * CAP
    vmem = pltpu.VMEM
    adjoint, received = pl.pallas_call(
        functools.partial(kernel, groups, blocks),
        out_shape=(
            jax.ShapeDtypeStruct((5, 32, 1024), F32),
            jax.ShapeDtypeStruct((4, blocks, LANES), F32),
        ),
        in_specs=[pl.BlockSpec(memory_space=pltpu.HBM)] * 10,
        out_specs=(
            pl.BlockSpec(memory_space=pl.ANY),
            pl.BlockSpec(memory_space=pl.ANY),
        ),
        scratch_shapes=[
            vmem((5, 10, 48, LANES), F32),
            vmem((5, 10, 48, LANES), F32),
            vmem((5, 32, 1024), F32),
            vmem((5, 32, 1024), F32),
            vmem((5, 32, 1024), F32),
            vmem((6, 32, 1024), BF16),
            vmem((32, 1024), F32),
            vmem((3, 4, slots), F32),
            vmem((4, slots), F32),
            vmem((1, slots), jnp.int32),
            vmem((4, slots), jnp.int32),
            vmem((1, blocks), jnp.int32),
            vmem((6, 8, 32, LANES), F32),
            vmem((5, 8, 32, LANES), F32),
            vmem((6, 8, 32, LANES), F32),
            vmem((8, 32, LANES), F32),
            vmem((4, PLANES, 8, LANES), F32),
            vmem((4, PLANES, 8, LANES), F32),
            vmem((2, 2, 8, LANES), F32),
            vmem((2, 2, 8, LANES), F32),
            vmem((256, 1024), BF16),
            vmem((1024, slots), BF16),
            vmem((256, slots), F32),
            vmem((6, blocks, LANES), F32),
            vmem((4, blocks, LANES), F32),
            pltpu.SemaphoreType.DMA((10,)),
            pltpu.SemaphoreType.DMA((2,)),
            pltpu.SemaphoreType.DMA((8,)),
            pltpu.SemaphoreType.DMA((8,)),
            pltpu.SemaphoreType.DMA,
            pltpu.SemaphoreType.DMA,
            pltpu.SemaphoreType.REGULAR,
        ],
        compiler_params=pltpu.CompilerParams(
            collective_id=0, has_side_effects=True, vmem_limit_bytes=60 * 1024 * 1024
        ),
    )(
        init,
        rhs,
        flow,
        face,
        pseudo,
        jnp.transpose(coords, (1, 0, 2)),
        weights,
        cell.reshape(1, slots),
        vertex,
        count,
    )
    return pl.pallas_call(
        vertex_sums,
        out_shape=(
            jax.ShapeDtypeStruct((5, 32, 1024), F32),
            jax.ShapeDtypeStruct((3, VERT_DEV), F32),
        ),
        in_specs=[pl.BlockSpec(memory_space=pl.ANY)] * 2,
        out_specs=(
            pl.BlockSpec(memory_space=pl.ANY),
            pl.BlockSpec(memory_space=pltpu.VMEM),
        ),
        scratch_shapes=[
            vmem((4, blocks, LANES), F32),
            vmem((5, 32, 1024), F32),
            vmem((96, slots * 4), BF16),
            vmem((128, slots * 4), BF16),
            pltpu.SemaphoreType.DMA,
            pltpu.SemaphoreType.DMA((5,)),
            pltpu.SemaphoreType.DMA((5,)),
        ],
        compiler_params=pltpu.CompilerParams(vmem_limit_bytes=60 * 1024 * 1024),
    )(adjoint, received)


def solution(mesh):
    return jax.shard_map(
        functools.partial(local, mesh.shape["grp"], mesh.shape["blk"]),
        mesh=mesh,
        in_specs=(
            P(None, "grp", "blk"),
            P(None, "grp", "blk"),
            P(None, "grp", "blk"),
            P(None, "grp", "blk"),
            P("grp", "blk"),
            P(None, None, ("grp", "blk")),
            P(None, ("grp", "blk")),
            P(("grp", "blk")),
            P(None, ("grp", "blk")),
            P(("grp", "blk"), None),
        ),
        out_specs=(P(None, "grp", "blk"), P(None, ("grp", "blk"))),
        check_vma=False,
    )
```

```python
import functools

import jax
import jax.numpy as jnp
from jax import lax
from jax.experimental import pallas as pl
from jax.experimental.pallas import tpu as pltpu
from jax.sharding import PartitionSpec as P

VERT_DEV = 1536
CAP = 32
PLANES = 17
LANES = 128
GAMMA = 1.4
LOCAL = 8
MESH = pl.DeviceIdType.MESH
F32 = jnp.float32
BF16 = jnp.bfloat16


def lane_iota(shape):
    return lax.broadcasted_iota(jnp.int32, shape, len(shape) - 1)


def row_iota(shape):
    return lax.broadcasted_iota(jnp.int32, shape, len(shape) - 2)


def cross(a, b):
    return [
        a[1] * b[2] - a[2] * b[1],
        a[2] * b[0] - a[0] * b[2],
        a[0] * b[1] - a[1] * b[0],
    ]


def kernel(
    groups,
    blocks,
    init_hbm,
    rhs_hbm,
    flow_hbm,
    face_hbm,
    pseudo_hbm,
    coords_hbm,
    weights_hbm,
    cell_hbm,
    vertex_hbm,
    count_hbm,
    adj_out,
    recv,
    adj_a,
    adj_b,
    adj_c,
    rhs,
    flow,
    face,
    pseudo,
    coords,
    weights,
    cell,
    vertex,
    count,
    gface,
    scaled,
    coef,
    press,
    face_send,
    face_recv,
    edge_send,
    edge_recv,
    table,
    onehot,
    found,
    geom,
    send,
    load_sem,
    out_sem,
    halo_send,
    halo_recv,
    term_send,
    term_recv,
    plane_sem,
):
    group = lax.axis_index("grp")
    block = lax.axis_index("blk")
    columns = 8
    chunks = blocks // 8

    def loaded(*wanted):
        for position, (source, target) in enumerate(loads):
            if any(target is one for one in wanted):
                pltpu.make_async_copy(source, target, load_sem.at[position]).wait()

    def inner(ref):
        return ref.at[:, pl.ds(1, columns), pl.ds(8, 32), :]

    grp_up = {"grp": lax.rem(group + 1, groups)}
    grp_down = {"grp": lax.rem(group + groups - 1, groups)}
    blk_up = {"blk": lax.rem(block + 1, blocks)}
    blk_down = {"blk": lax.rem(block + blocks - 1, blocks)}

    barrier = pltpu.get_barrier_semaphore()
    diagonals = [[{**one, **two} for two in (blk_down, blk_up)] for one in (grp_down, grp_up)]
    for device in [grp_up, grp_down, blk_up, blk_down] + diagonals[0] + diagonals[1]:
        pl.semaphore_signal(barrier, inc=1, device_id=device, device_id_type=MESH)

    loads = [
        (flow_hbm, flow),
        (face_hbm, face),
        (pseudo_hbm, pseudo),
        (rhs_hbm, rhs),
        (cell_hbm, cell),
        (coords_hbm, coords),
        (weights_hbm, weights),
        (vertex_hbm, vertex),
        (count_hbm, count),
    ]
    for tile in range(columns):
        pltpu.make_async_copy(
            init_hbm.at[:, :, pl.ds(tile * LANES, LANES)],
            adj_a.at[:, 1 + tile, pl.ds(8, 32), :],
            load_sem.at[len(loads)],
        ).start()
    for position, (source, target) in enumerate(loads):
        pltpu.make_async_copy(source, target, load_sem.at[position]).start()

    planes = blocks // LOCAL
    z, x, core = block // LOCAL, block % LOCAL // 2, block % 2
    for step in range(1, LOCAL):
        beside = z * LOCAL + lax.rem(x + step // 2, 4) * 2 + lax.rem(core + step % 2, 2)
        pl.semaphore_signal(barrier, inc=1, device_id={"blk": beside}, device_id_type=MESH)
    column = [
        {"blk": lax.rem(z + step, planes) * LOCAL + block % LOCAL} for step in range(1, planes)
    ]
    for device in column:
        pl.semaphore_signal(barrier, inc=1, device_id=device, device_id_type=MESH)

    tile_lane = lane_iota((8, LANES))
    tile_row = row_iota((8, LANES))
    lane_block = tile_lane // CAP

    first_end = (tile_row == 0) & (lane_block == 0)
    last_end = (tile_row == 7) & (lane_block == 3)

    def take_plane(read, side):
        if side < 2:
            row = 31 * side
            return jnp.concatenate([read(tile, row, 1) for tile in range(columns)], axis=0)
        tile, home = ((0, 0), (columns - 1, 3))[side - 2]
        total = None
        for part in range(4):
            value = read(tile, 8 * part, 8)
            turn = (part - home) % 4 * CAP
            if turn:
                value = pltpu.roll(value, turn, 1)
            total = value if total is None else jnp.where(lane_block == part, value, total)
        return total

    def in_adjoint(adj, field):
        return lambda tile, row, count: adj[field, tile + 1, pl.ds(8 + row, count), :]

    def in_table(ref, place):
        return lambda tile, row, count: ref[place, tile, pl.ds(row, count), :]

    def fill_face(side):
        for f in range(5):
            face_send[side, f] = take_plane(in_adjoint(adj_a, f), side)
            face_send[side, 5 + f] = take_plane(in_adjoint(adj_b, f), side)
            face_send[side, 10 + f] = take_plane(in_table(coef, (0, 1, 2, 4, 5)[f]), side)
        outward = 2 * (side // 2) + 1 - side % 2
        along = 2 - 2 * (side // 2)
        face_send[side, 15] = take_plane(in_table(gface, outward), side)
        face_send[side, 16] = jnp.where(
            first_end,
            take_plane(in_table(gface, along + 1), side),
            jnp.where(last_end, take_plane(in_table(gface, along), side), 0.0),
        )

    def fill_edge(upper_x, upper_y):
        tile, home = ((1, 0), (columns, 3))[upper_y]
        row = 8 + 31 * upper_x
        lines = [adj_a[f, tile, pl.ds(row, 1), :] for f in range(5)]
        value = jnp.concatenate(lines + [jnp.zeros((3, LANES), F32)], axis=0)
        value = jnp.where(lane_block == home, value, 0.0)
        value = value + pltpu.roll(value, CAP, 1)
        edge_send[upper_x, upper_y] = value + pltpu.roll(value, 2 * CAP, 1)

    def halo_copies():
        parts = [
            (face_send.at[side], face_recv.at[side + 1 - 2 * (side % 2)], device)
            for side, device in enumerate((grp_down, grp_up, blk_down, blk_up))
        ] + [
            (edge_send.at[i, j], edge_recv.at[1 - i, 1 - j], diagonals[i][j])
            for i in range(2)
            for j in range(2)
        ]
        return [
            pltpu.make_async_remote_copy(
                src_ref=source,
                dst_ref=target,
                send_sem=halo_send.at[position],
                recv_sem=halo_recv.at[position],
                device_id=device,
                device_id_type=MESH,
            )
            for position, (source, target, device) in enumerate(parts)
        ]

    def one_way(faces_of, side, axis, sign, weight, value):
        velocity = [faces_of[side, 10 + k] for k in range(3)]
        enthalpy = faces_of[side, 13]
        reach = faces_of[side, 14]
        half_sq = (0.5 * (GAMMA - 1.0)) * (
            velocity[0] * velocity[0] + velocity[1] * velocity[1] + velocity[2] * velocity[2]
        )
        speed = velocity[axis]
        dot = (
            velocity[0] * value[1]
            + velocity[1] * value[2]
            + velocity[2] * value[3]
            + enthalpy * value[4]
        )
        turned = value[1 + axis] + speed * value[4]
        scaled_turn = (GAMMA - 1.0) * turned
        result = [half_sq * turned - speed * dot]
        for k in range(3):
            entry = speed * value[1 + k] - scaled_turn * velocity[k]
            result.append(entry + value[0] + dot if k == axis else entry)
        result.append(scaled_turn + speed * value[4])
        steady, signed = weight * reach, weight * sign
        return [signed * result[f] + steady * value[f] for f in range(5)]

    def complete(side):
        axis, cross_axis = side // 2, 1 - side // 2
        sign = 2.0 * (side % 2) - 1.0
        mine = [face_send[side, f] for f in range(5)]
        theirs = [face_recv[side, f] for f in range(5)]
        gain = one_way(face_send, side, axis, sign, face_send[side, 15], theirs)
        outer = one_way(face_recv, side, axis, -sign, face_recv[side, 15], mine)
        if side < 2:
            ends = edge_recv[side, 0], edge_recv[side, 1]
        else:
            ends = edge_recv[0, side - 2], edge_recv[1, side - 2]
        corner = [
            jnp.where(last_end, ends[1][f : f + 1], jnp.where(first_end, ends[0][f : f + 1], 0.0))
            for f in range(5)
        ]
        end_sign = jnp.where(last_end, 1.0, -1.0)
        extra = one_way(face_recv, side, cross_axis, end_sign, face_recv[side, 16], corner)
        for f in range(5):
            halo = face_recv[side, 5 + f] + outer[f] + extra[f]
            if side < 2:
                own_row, halo_row = ((8, 7), (39, 40))[side]
                for tile in range(columns):
                    adj_b[f, 1 + tile, pl.ds(halo_row, 1), :] = halo[tile : tile + 1]
                    adj_b[f, 1 + tile, pl.ds(own_row, 1), :] = (
                        adj_b[f, 1 + tile, pl.ds(own_row, 1), :] + gain[f][tile : tile + 1]
                    )
            else:
                tile, home, halo_tile, halo_home = ((1, 0, 0, 3), (columns, 3, columns + 1, 0))[side - 2]
                for part in range(4):
                    rows = pl.ds(8 + 8 * part, 8)
                    turn = (halo_home - part) % 4 * CAP
                    adj_b[f, halo_tile, rows, :] = pltpu.roll(halo, turn, 1) if turn else halo
                    turn = (home - part) % 4 * CAP
                    moved = pltpu.roll(gain[f], turn, 1) if turn else gain[f]
                    adj_b[f, tile, rows, :] = adj_b[f, tile, rows, :] + jnp.where(
                        lane_block == home, moved, 0.0
                    )

    def sweep_tile(source, store, tile, part):
        rows = pl.ds(8 * part, 8)
        here = pl.ds(8 * part + 8, 8)
        center = [source[f, tile + 1, here, :] for f in range(5)]
        upper = [source[f, tile + 2, here, :] for f in range(5)]
        lower = [source[f, tile, here, :] for f in range(5)]
        pairs = [
            (
                [source[f, tile + 1, pl.ds(8 * part + 9, 8), :] for f in range(5)],
                [source[f, tile + 1, pl.ds(8 * part + 7, 8), :] for f in range(5)],
            ),
            (
                [
                    pltpu.roll(jnp.where(tile_lane >= CAP, center[f], upper[f]), LANES - CAP, 1)
                    for f in range(5)
                ],
                [
                    pltpu.roll(jnp.where(tile_lane < LANES - CAP, center[f], lower[f]), CAP, 1)
                    for f in range(5)
                ],
            ),
            (
                [pltpu.roll(center[f], LANES - 1, 1) for f in range(5)],
                [pltpu.roll(center[f], 1, 1) for f in range(5)],
            ),
        ]
        velocity = [coef[k, tile, rows, :] for k in range(3)]
        half_sq = coef[3, tile, rows, :]
        enthalpy = coef[4, tile, rows, :]
        reach = coef[5, tile, rows, :]
        sums = None
        moved = None
        flux = None
        first = []
        turned = None
        for axis, (plus, minus) in enumerate(pairs):
            g_plus = gface[2 * axis, tile, rows, :]
            g_minus = gface[2 * axis + 1, tile, rows, :]
            ahead = [g_plus * value for value in plus]
            behind = [g_minus * value for value in minus]
            diff = [a - b for a, b in zip(ahead, behind)]
            both = [a + b for a, b in zip(ahead, behind)]
            sums = both if sums is None else [a + b for a, b in zip(sums, both)]
            dot = (
                velocity[0] * diff[1]
                + velocity[1] * diff[2]
                + velocity[2] * diff[3]
                + enthalpy * diff[4]
            )
            first.append(diff[0] + dot)
            speed = velocity[axis]
            part_moved = [speed * diff[k] for k in range(1, 5)]
            moved = part_moved if moved is None else [a + b for a, b in zip(moved, part_moved)]
            flux = speed * dot if flux is None else flux + speed * dot
            turned = diff[1 + axis] if turned is None else turned + diff[1 + axis]
        turned = turned + moved[3]
        scaled_turn = (GAMMA - 1.0) * turned
        result = [half_sq * turned - flux]
        for k in range(3):
            result.append(first[k] - scaled_turn * velocity[k] + moved[k])
        result.append(scaled_turn + moved[3])
        for f in range(5):
            store(f, tile, part, scaled[f, tile, rows, :] + reach * sums[f] + result[f])

    def store_b(f, tile, part, value):
        adj_b[f, tile + 1, pl.ds(8 * part + 8, 8), :] = value

    def store_c(f, tile, part, value):
        adj_c[f, pl.ds(8 * part, 8), pl.ds(pl.multiple_of(tile * LANES, LANES), LANES)] = value

    def sweep(source, store):
        def body(tile, carry):
            for part in range(4):
                sweep_tile(source, store, tile, part)
            return carry

        lax.fori_loop(0, columns, body, 0, unroll=2)

    def interior(source, store):
        def body(tile, carry):
            for part in (1, 2):
                sweep_tile(source, store, tile, part)
            return carry

        lax.fori_loop(1, columns - 1, body, 0, unroll=3)

    def boundary(source, store):
        def body(tile, carry):
            for part in (0, 3):
                sweep_tile(source, store, tile, part)
            return carry

        lax.fori_loop(0, columns, body, 0, unroll=4)
        for tile in (0, columns - 1):
            for part in (1, 2):
                sweep_tile(source, store, tile, part)

    nothing = jnp.zeros((8, LANES), F32)
    for f in range(5):
        for tile in range(columns):
            adj_a[f, 1 + tile, pl.ds(0, 8), :] = nothing
            adj_a[f, 1 + tile, pl.ds(40, 8), :] = nothing
        for part in range(4):
            adj_a[f, 0, pl.ds(8 + 8 * part, 8), :] = nothing
            adj_a[f, columns + 1, pl.ds(8 + 8 * part, 8), :] = nothing

    loaded(flow, face, pseudo, rhs)
    tall_row = row_iota((16, LANES))
    tall_lane = lane_iota((16, LANES))

    def coefficients(step, carry):
        tile = step // 2
        half = step % 2
        rows = pl.ds(pl.multiple_of(half * 16, 16), 16)
        lanes = pl.ds(pl.multiple_of(tile * LANES, LANES), LANES)
        density = flow[0, rows, lanes]
        inverse = 1.0 / density
        velocity = [flow[1 + k, rows, lanes] * inverse for k in range(3)]
        energy = flow[4, rows, lanes]
        speed_sq = (
            velocity[0] * velocity[0] + velocity[1] * velocity[1] + velocity[2] * velocity[2]
        )
        pressure = (GAMMA - 1.0) * (energy - 0.5 * density * speed_sq)
        enthalpy = (energy + pressure) * inverse
        reach = jnp.sqrt(speed_sq) + jnp.sqrt(GAMMA * pressure * inverse)
        for k in range(3):
            coef[k, tile, rows, :] = velocity[k]
        coef[3, tile, rows, :] = 0.5 * (GAMMA - 1.0) * speed_sq
        coef[4, tile, rows, :] = enthalpy
        coef[5, tile, rows, :] = reach
        press[tile, rows, :] = pressure
        faces = [face[d, rows, lanes].astype(F32) for d in range(6)]
        open_sum = faces[0] + faces[1] + faces[2] + faces[3] + faces[4] + faces[5]
        share = 1.0 / (pseudo[rows, lanes] + 0.5 * reach * open_sum)
        half_share = 0.5 * share
        across = tall_row + half * 16
        along = tall_lane + tile * LANES
        height = tall_lane % 32
        outside = [
            (across == 31) & (group == groups - 1),
            (across == 0) & (group == 0),
            (along >= 992) & (block == blocks - 1),
            (along < 32) & (block == 0),
            height == 31,
            height == 0,
        ]
        for d in range(6):
            gface[d, tile, rows, :] = jnp.where(outside[d], 0.0, faces[d] * half_share)
        for f in range(5):
            scaled[f, tile, rows, :] = rhs[f, rows, lanes] * share
        return carry

    lax.fori_loop(0, 2 * columns, coefficients, 0, unroll=2)
    pltpu.make_async_copy(inner(adj_a), inner(adj_a), load_sem.at[len(loads)]).wait()
    sweep(adj_a, store_b)

    for i in range(2):
        for j in range(2):
            fill_edge(i, j)
    for side in (2, 3):
        fill_face(side)
    pl.semaphore_wait(barrier, 8 + LOCAL - 1 + planes - 1)
    halo = halo_copies()
    for copy in halo[4:] + halo[2:4]:
        copy.start()
    for side in (0, 1):
        fill_face(side)
        halo[side].start()
    for device in column:
        pl.semaphore_signal(plane_sem, inc=1, device_id=device, device_id_type=MESH)

    interior(adj_b, store_c)

    loaded(cell, coords, weights, vertex, count)

    def pick_cells(chunk, carry):
        lanes = pl.ds(pl.multiple_of(chunk * 256, 256), 256)
        place = jnp.bitwise_and(cell[:, lanes], 1023)
        for band in range(8):
            rows = band * 128 + row_iota((128, 256))
            onehot[pl.ds(band * 128, 128), lanes] = jnp.where(rows == place, 1.0, 0.0).astype(BF16)
        return carry

    lax.fori_loop(0, chunks, pick_cells, 0)

    own_block = lane_block == tile_row % 4
    upper_half = tile_row < 4
    slot = tile_lane % CAP

    def spread(even, odd):
        value = jnp.where(own_block, jnp.where(upper_half, even, odd), 0.0)
        value = value + pltpu.roll(value, CAP, 1)
        return value + pltpu.roll(value, 2 * CAP, 1)

    def by_corner(values):
        total = values[3]
        for k in range(3):
            total = jnp.where(lane_block == k, values[k], total)
        return total

    def geometry(chunk, carry):
        even = pl.ds(pl.multiple_of(chunk * 256, 128), 128)
        odd = pl.ds(pl.multiple_of(chunk * 256 + 128, 128), 128)
        rows = pl.ds(pl.multiple_of(chunk * 8, 8), 8)
        corner = [
            [spread(coords[k, c : c + 1, even], coords[k, c : c + 1, odd]) for k in range(3)]
            for c in range(4)
        ]
        edge = [[corner[c][k] - corner[0][k] for k in range(3)] for c in range(1, 4)]
        grads = [
            [value / 6.0 for value in cross(edge[1], edge[2])],
            [value / 6.0 for value in cross(edge[2], edge[0])],
            [value / 6.0 for value in cross(edge[0], edge[1])],
        ]
        grad_zero = [-(grads[0][k] + grads[1][k] + grads[2][k]) for k in range(3)]
        side_two = [0.5 * (corner[3][k] - corner[1][k]) for k in range(3)]
        side_three = [-0.5 * (corner[2][k] - corner[1][k]) for k in range(3)]
        side_one = [-(side_two[k] + side_three[k]) for k in range(3)]
        weight = by_corner([spread(weights[c : c + 1, even], weights[c : c + 1, odd]) for c in range(4)])
        counts = jnp.broadcast_to(count[...], (8, blocks))
        wanted = lane_iota((8, blocks)) == chunk * 8 + row_iota((8, blocks))
        own_count = jnp.sum(jnp.where(wanted, counts, 0), axis=1, keepdims=True)
        weight = jnp.where(slot < own_count, weight, 0.0)
        for k in range(3):
            gradient = by_corner([grad_zero[k], grads[0][k], grads[1][k], grads[2][k]])
            side = by_corner([jnp.zeros_like(side_one[k]), side_one[k], side_two[k], side_three[k]])
            geom[k, rows, :] = weight * gradient
            geom[3 + k, rows, :] = weight * side
        send[3, rows, :] = by_corner(
            [
                spread(vertex[c : c + 1, even].astype(F32), vertex[c : c + 1, odd].astype(F32))
                for c in range(4)
            ]
        )
        return carry

    lax.fori_loop(0, chunks, geometry, 0, unroll=4)

    for copy in halo:
        copy.wait_recv()
    for side in range(4):
        complete(side)
    boundary(adj_b, store_c)
    adj_copy = pltpu.make_async_copy(adj_c, adj_out, out_sem.at[0])
    adj_copy.start()

    def fill_table(step, carry):
        tile = step // 2
        half = step % 2
        rows = pl.ds(pl.multiple_of(half * 16, 16), 16)
        lanes = pl.ds(pl.multiple_of(tile * LANES, LANES), LANES)
        pressure = press[tile, rows, :]
        for f in range(4):
            value = pressure * adj_c[1 + f, rows, lanes]
            high = value.astype(BF16)
            low = (value - high.astype(F32)).astype(BF16)
            table[pl.ds(pl.multiple_of(f * 32 + half * 16, 16), 16), lanes] = high
            table[pl.ds(pl.multiple_of(128 + f * 32 + half * 16, 16), 16), lanes] = low
        return carry

    lax.fori_loop(0, 2 * columns, fill_table, 0)

    found[...] = jnp.dot(table[...], onehot[...], preferred_element_type=F32)

    def terms(chunk, carry):
        lanes = pl.ds(pl.multiple_of(chunk * 256, 256), 256)
        rows = pl.ds(pl.multiple_of(chunk * 8, 8), 8)
        plane = jnp.right_shift(cell[:, lanes], 10)
        mine = row_iota((32, 256)) == plane
        fields = []
        for f in range(4):
            value = found[32 * f : 32 * f + 32, lanes] + found[128 + 32 * f : 160 + 32 * f, lanes]
            value = jnp.sum(jnp.where(mine, value, 0.0), axis=0, keepdims=True)
            fields.append(spread(value[:, :128], value[:, 128:]))
        b, a = fields[:3], fields[3]
        gradient = [geom[k, rows, :] for k in range(3)]
        side = [geom[3 + k, rows, :] for k in range(3)]
        turn = cross(side, b)
        for k in range(3):
            send[k, rows, :] = a * gradient[k] + turn[k]
        return carry

    lax.fori_loop(0, chunks, terms, 0, unroll=8)

    if planes > 1:
        pl.semaphore_wait(plane_sem, planes - 1)

    def post(step, carry):
        turn = step // LOCAL
        far = planes // 2 + (1 - 2 * (turn % 2)) * ((turn + 1) // 2)
        near = LOCAL - 1 - step % LOCAL
        owner = (
            lax.rem(z + far, planes) * LOCAL
            + lax.rem(x + near // 2, 4) * 2
            + lax.rem(core + near % 2, 2)
        )
        pltpu.make_async_remote_copy(
            src_ref=send.at[:, pl.ds(owner, 1), :],
            dst_ref=recv.at[:, pl.ds(step, 1), :],
            send_sem=term_send,
            recv_sem=term_recv,
            device_id={"blk": owner},
            device_id_type=MESH,
        ).start()
        return carry

    lax.fori_loop(0, blocks - 1, post, 0)
    own = pltpu.make_async_copy(
        send.at[:, pl.ds(block, 1), :], recv.at[:, pl.ds(blocks - 1, 1), :], out_sem.at[1]
    )
    own.start()
    others = pltpu.make_async_remote_copy(
        src_ref=send.at[:, pl.ds(0, blocks - 1), :],
        dst_ref=recv.at[:, pl.ds(0, blocks - 1), :],
        send_sem=term_send,
        recv_sem=term_recv,
        device_id=blk_up,
        device_id_type=MESH,
    )
    others.wait_recv()
    own.wait()

    for copy in halo:
        copy.wait_send()
    others.wait_send()
    adj_copy.wait()


def vertex_sums(adj, recv_hbm, adj_out, sens_out, recv, held, left_op, right_op, recv_sem, in_sem, back_sem):
    recv_copy = pltpu.make_async_copy(recv_hbm, recv, recv_sem)
    recv_copy.start()
    inward = [
        pltpu.make_async_copy(adj.at[f], held.at[f], in_sem.at[f]) for f in range(5)
    ]
    outward = [
        pltpu.make_async_copy(held.at[f], adj_out.at[f], back_sem.at[f]) for f in range(5)
    ]
    for copy in inward:
        copy.start()
    for arriving, leaving in zip(inward, outward):
        arriving.wait()
        leaving.start()
    recv_copy.wait()
    chunks = recv.shape[1] // 8

    bands = [(row_iota((16, LANES)) + 16 * band).astype(F32).astype(BF16) for band in range(8)]
    one, zero = jnp.ones((16, LANES), BF16), jnp.zeros((16, LANES), BF16)

    def operands(chunk, carry):
        rows = pl.ds(chunk * 8, 8)
        vertices = recv[3, rows, :].astype(jnp.int32)
        major = jnp.right_shift(vertices, 7)
        minor = jnp.bitwise_and(vertices, 127)
        halves = []
        for k in range(3):
            value = recv[k, rows, :]
            high = value.astype(BF16).astype(F32)
            halves += [high, value - high]
        for s in range(8):
            lanes = pl.ds(chunk * 1024 + s * LANES, LANES)
            low = jnp.broadcast_to(minor[s : s + 1].astype(F32), (16, LANES)).astype(BF16)
            for band in range(8):
                right_op[pl.ds(16 * band, 16), lanes] = jnp.where(low == bands[band], one, zero)
            hit = row_iota((16, LANES)) == major[s : s + 1]
            for n, value in enumerate(halves):
                left_op[pl.ds(16 * n, 16), lanes] = jnp.where(hit, value[s : s + 1], 0.0).astype(BF16)
        return carry

    sums = None
    for chunk in range(chunks):
        operands(chunk, 0)
        lanes = pl.ds(chunk * 1024, 1024)
        part = lax.dot_general(
            left_op[:, lanes],
            right_op[:, lanes],
            (((1,), (1,)), ((), ())),
            preferred_element_type=F32,
        )
        sums = part if sums is None else sums + part
    for k in range(3):
        both = sums[32 * k : 32 * k + 16] + sums[32 * k + 16 : 32 * k + 32]
        for h in range(VERT_DEV // LANES):
            sens_out[k : k + 1, h * LANES : (h + 1) * LANES] = both[h : h + 1]

    for copy in outward:
        copy.wait()


def local(groups, blocks, init, rhs, flow, face, pseudo, coords, weights, cell, vertex, count):
    slots = blocks * CAP
    vmem = pltpu.VMEM
    adjoint, received = pl.pallas_call(
        functools.partial(kernel, groups, blocks),
        out_shape=(
            jax.ShapeDtypeStruct((5, 32, 1024), F32),
            jax.ShapeDtypeStruct((4, blocks, LANES), F32),
        ),
        in_specs=[pl.BlockSpec(memory_space=pltpu.HBM)] * 10,
        out_specs=(
            pl.BlockSpec(memory_space=pl.ANY),
            pl.BlockSpec(memory_space=pl.ANY),
        ),
        scratch_shapes=[
            vmem((5, 10, 48, LANES), F32),
            vmem((5, 10, 48, LANES), F32),
            vmem((5, 32, 1024), F32),
            vmem((5, 32, 1024), F32),
            vmem((5, 32, 1024), F32),
            vmem((6, 32, 1024), BF16),
            vmem((32, 1024), F32),
            vmem((3, 4, slots), F32),
            vmem((4, slots), F32),
            vmem((1, slots), jnp.int32),
            vmem((4, slots), jnp.int32),
            vmem((1, blocks), jnp.int32),
            vmem((6, 8, 32, LANES), F32),
            vmem((5, 8, 32, LANES), F32),
            vmem((6, 8, 32, LANES), F32),
            vmem((8, 32, LANES), F32),
            vmem((4, PLANES, 8, LANES), F32),
            vmem((4, PLANES, 8, LANES), F32),
            vmem((2, 2, 8, LANES), F32),
            vmem((2, 2, 8, LANES), F32),
            vmem((256, 1024), BF16),
            vmem((1024, slots), BF16),
            vmem((256, slots), F32),
            vmem((6, blocks, LANES), F32),
            vmem((4, blocks, LANES), F32),
            pltpu.SemaphoreType.DMA((10,)),
            pltpu.SemaphoreType.DMA((2,)),
            pltpu.SemaphoreType.DMA((8,)),
            pltpu.SemaphoreType.DMA((8,)),
            pltpu.SemaphoreType.DMA,
            pltpu.SemaphoreType.DMA,
            pltpu.SemaphoreType.REGULAR,
        ],
        compiler_params=pltpu.CompilerParams(
            collective_id=0, has_side_effects=True, vmem_limit_bytes=60 * 1024 * 1024
        ),
    )(
        init,
        rhs,
        flow,
        face,
        pseudo,
        jnp.transpose(coords, (1, 0, 2)),
        weights,
        cell.reshape(1, slots),
        vertex,
        count,
    )
    return pl.pallas_call(
        vertex_sums,
        out_shape=(
            jax.ShapeDtypeStruct((5, 32, 1024), F32),
            jax.ShapeDtypeStruct((3, VERT_DEV), F32),
        ),
        in_specs=[pl.BlockSpec(memory_space=pl.ANY)] * 2,
        out_specs=(
            pl.BlockSpec(memory_space=pl.ANY),
            pl.BlockSpec(memory_space=pltpu.VMEM),
        ),
        scratch_shapes=[
            vmem((4, blocks, LANES), F32),
            vmem((5, 32, 1024), F32),
            vmem((96, slots * 4), BF16),
            vmem((128, slots * 4), BF16),
            pltpu.SemaphoreType.DMA,
            pltpu.SemaphoreType.DMA((5,)),
            pltpu.SemaphoreType.DMA((5,)),
        ],
        compiler_params=pltpu.CompilerParams(vmem_limit_bytes=60 * 1024 * 1024),
    )(adjoint, received)


def solution(mesh):
    return jax.shard_map(
        functools.partial(local, mesh.shape["grp"], mesh.shape["blk"]),
        mesh=mesh,
        in_specs=(
            P(None, "grp", "blk"),
            P(None, "grp", "blk"),
            P(None, "grp", "blk"),
            P(None, "grp", "blk"),
            P("grp", "blk"),
            P(None, None, ("grp", "blk")),
            P(None, ("grp", "blk")),
            P(("grp", "blk")),
            P(None, ("grp", "blk")),
            P(("grp", "blk"), None),
        ),
        out_specs=(P(None, "grp", "blk"), P(None, ("grp", "blk"))),
        check_vma=False,
    )
```

```python
import functools

import jax
import jax.numpy as jnp
from jax import lax
from jax.experimental import pallas as pl
from jax.experimental.pallas import tpu as pltpu
from jax.sharding import PartitionSpec as P

VERT_DEV = 1536
CAP = 32
PLANES = 17
LANES = 128
GAMMA = 1.4
LOCAL = 8
MESH = pl.DeviceIdType.MESH
F32 = jnp.float32
BF16 = jnp.bfloat16


def lane_iota(shape):
    return lax.broadcasted_iota(jnp.int32, shape, len(shape) - 1)


def row_iota(shape):
    return lax.broadcasted_iota(jnp.int32, shape, len(shape) - 2)


def cross(a, b):
    return [
        a[1] * b[2] - a[2] * b[1],
        a[2] * b[0] - a[0] * b[2],
        a[0] * b[1] - a[1] * b[0],
    ]


def kernel(
    groups,
    blocks,
    init_hbm,
    rhs_hbm,
    flow_hbm,
    face_hbm,
    pseudo_hbm,
    coords_hbm,
    weights_hbm,
    cell_hbm,
    vertex_hbm,
    count_hbm,
    adj_out,
    recv,
    adj_a,
    adj_b,
    adj_c,
    rhs,
    flow,
    face,
    pseudo,
    coords,
    weights,
    cell,
    vertex,
    count,
    gface,
    scaled,
    coef,
    press,
    face_send,
    face_recv,
    edge_send,
    edge_recv,
    table,
    onehot,
    found,
    geom,
    send,
    load_sem,
    out_sem,
    halo_send,
    halo_recv,
    term_send,
    term_recv,
    plane_sem,
):
    group = lax.axis_index("grp")
    block = lax.axis_index("blk")
    columns = 8
    chunks = blocks // 8

    def loaded(*wanted):
        for position, (source, target) in enumerate(loads):
            if any(target is one for one in wanted):
                pltpu.make_async_copy(source, target, load_sem.at[position]).wait()

    def inner(ref):
        return ref.at[:, pl.ds(1, columns), pl.ds(8, 32), :]

    grp_up = {"grp": lax.rem(group + 1, groups)}
    grp_down = {"grp": lax.rem(group + groups - 1, groups)}
    blk_up = {"blk": lax.rem(block + 1, blocks)}
    blk_down = {"blk": lax.rem(block + blocks - 1, blocks)}

    barrier = pltpu.get_barrier_semaphore()
    diagonals = [[{**one, **two} for two in (blk_down, blk_up)] for one in (grp_down, grp_up)]
    for device in [grp_up, grp_down, blk_up, blk_down] + diagonals[0] + diagonals[1]:
        pl.semaphore_signal(barrier, inc=1, device_id=device, device_id_type=MESH)

    loads = [
        (flow_hbm, flow),
        (face_hbm, face),
        (pseudo_hbm, pseudo),
        (rhs_hbm, rhs),
        (cell_hbm, cell),
        (coords_hbm, coords),
        (weights_hbm, weights),
        (vertex_hbm, vertex),
        (count_hbm, count),
    ]
    for position, (source, target) in enumerate(loads[:4]):
        pltpu.make_async_copy(source, target, load_sem.at[position]).start()
    for tile in range(columns):
        pltpu.make_async_copy(
            init_hbm.at[:, :, pl.ds(tile * LANES, LANES)],
            adj_a.at[:, 1 + tile, pl.ds(8, 32), :],
            load_sem.at[len(loads)],
        ).start()
    for position, (source, target) in enumerate(loads):
        if position >= 4:
            pltpu.make_async_copy(source, target, load_sem.at[position]).start()

    planes = blocks // LOCAL
    z, x, core = block // LOCAL, block % LOCAL // 2, block % 2
    for step in range(1, LOCAL):
        beside = z * LOCAL + lax.rem(x + step // 2, 4) * 2 + lax.rem(core + step % 2, 2)
        pl.semaphore_signal(barrier, inc=1, device_id={"blk": beside}, device_id_type=MESH)
    column = [
        {"blk": lax.rem(z + step, planes) * LOCAL + block % LOCAL} for step in range(1, planes)
    ]
    for device in column:
        pl.semaphore_signal(barrier, inc=1, device_id=device, device_id_type=MESH)

    tile_lane = lane_iota((8, LANES))
    tile_row = row_iota((8, LANES))
    lane_block = tile_lane // CAP

    first_end = (tile_row == 0) & (lane_block == 0)
    last_end = (tile_row == 7) & (lane_block == 3)

    def take_plane(read, side):
        if side < 2:
            row = 31 * side
            return jnp.concatenate([read(tile, row, 1) for tile in range(columns)], axis=0)
        tile, home = ((0, 0), (columns - 1, 3))[side - 2]
        total = None
        for part in range(4):
            value = read(tile, 8 * part, 8)
            turn = (part - home) % 4 * CAP
            if turn:
                value = pltpu.roll(value, turn, 1)
            total = value if total is None else jnp.where(lane_block == part, value, total)
        return total

    def in_adjoint(adj, field):
        return lambda tile, row, count: adj[field, tile + 1, pl.ds(8 + row, count), :]

    def in_table(ref, place):
        return lambda tile, row, count: ref[place, tile, pl.ds(row, count), :]

    def fill_face(side):
        for f in range(5):
            face_send[side, f] = take_plane(in_adjoint(adj_a, f), side)
            face_send[side, 5 + f] = take_plane(in_adjoint(adj_b, f), side)
            face_send[side, 10 + f] = take_plane(in_table(coef, (0, 1, 2, 4, 5)[f]), side)
        outward = 2 * (side // 2) + 1 - side % 2
        along = 2 - 2 * (side // 2)
        face_send[side, 15] = take_plane(in_table(gface, outward), side)
        face_send[side, 16] = jnp.where(
            first_end,
            take_plane(in_table(gface, along + 1), side),
            jnp.where(last_end, take_plane(in_table(gface, along), side), 0.0),
        )

    def fill_edge(upper_x, upper_y):
        tile, home = ((1, 0), (columns, 3))[upper_y]
        row = 8 + 31 * upper_x
        lines = [adj_a[f, tile, pl.ds(row, 1), :] for f in range(5)]
        value = jnp.concatenate(lines + [jnp.zeros((3, LANES), F32)], axis=0)
        value = jnp.where(lane_block == home, value, 0.0)
        value = value + pltpu.roll(value, CAP, 1)
        edge_send[upper_x, upper_y] = value + pltpu.roll(value, 2 * CAP, 1)

    def halo_copies():
        parts = [
            (face_send.at[side], face_recv.at[side + 1 - 2 * (side % 2)], device)
            for side, device in enumerate((grp_down, grp_up, blk_down, blk_up))
        ] + [
            (edge_send.at[i, j], edge_recv.at[1 - i, 1 - j], diagonals[i][j])
            for i in range(2)
            for j in range(2)
        ]
        return [
            pltpu.make_async_remote_copy(
                src_ref=source,
                dst_ref=target,
                send_sem=halo_send.at[position],
                recv_sem=halo_recv.at[position],
                device_id=device,
                device_id_type=MESH,
            )
            for position, (source, target, device) in enumerate(parts)
        ]

    def one_way(faces_of, side, axis, sign, weight, value):
        velocity = [faces_of[side, 10 + k] for k in range(3)]
        enthalpy = faces_of[side, 13]
        reach = faces_of[side, 14]
        half_sq = (0.5 * (GAMMA - 1.0)) * (
            velocity[0] * velocity[0] + velocity[1] * velocity[1] + velocity[2] * velocity[2]
        )
        speed = velocity[axis]
        dot = (
            velocity[0] * value[1]
            + velocity[1] * value[2]
            + velocity[2] * value[3]
            + enthalpy * value[4]
        )
        turned = value[1 + axis] + speed * value[4]
        scaled_turn = (GAMMA - 1.0) * turned
        result = [half_sq * turned - speed * dot]
        for k in range(3):
            entry = speed * value[1 + k] - scaled_turn * velocity[k]
            result.append(entry + value[0] + dot if k == axis else entry)
        result.append(scaled_turn + speed * value[4])
        steady, signed = weight * reach, weight * sign
        return [signed * result[f] + steady * value[f] for f in range(5)]

    def complete(side):
        axis, cross_axis = side // 2, 1 - side // 2
        sign = 2.0 * (side % 2) - 1.0
        mine = [face_send[side, f] for f in range(5)]
        theirs = [face_recv[side, f] for f in range(5)]
        gain = one_way(face_send, side, axis, sign, face_send[side, 15], theirs)
        outer = one_way(face_recv, side, axis, -sign, face_recv[side, 15], mine)
        if side < 2:
            ends = edge_recv[side, 0], edge_recv[side, 1]
        else:
            ends = edge_recv[0, side - 2], edge_recv[1, side - 2]
        corner = [
            jnp.where(last_end, ends[1][f : f + 1], jnp.where(first_end, ends[0][f : f + 1], 0.0))
            for f in range(5)
        ]
        end_sign = jnp.where(last_end, 1.0, -1.0)
        extra = one_way(face_recv, side, cross_axis, end_sign, face_recv[side, 16], corner)
        for f in range(5):
            halo = face_recv[side, 5 + f] + outer[f] + extra[f]
            if side < 2:
                own_row, halo_row = ((8, 7), (39, 40))[side]
                for tile in range(columns):
                    adj_b[f, 1 + tile, pl.ds(halo_row, 1), :] = halo[tile : tile + 1]
                    adj_b[f, 1 + tile, pl.ds(own_row, 1), :] = (
                        adj_b[f, 1 + tile, pl.ds(own_row, 1), :] + gain[f][tile : tile + 1]
                    )
            else:
                tile, home, halo_tile, halo_home = ((1, 0, 0, 3), (columns, 3, columns + 1, 0))[side - 2]
                for part in range(4):
                    rows = pl.ds(8 + 8 * part, 8)
                    turn = (halo_home - part) % 4 * CAP
                    adj_b[f, halo_tile, rows, :] = pltpu.roll(halo, turn, 1) if turn else halo
                    turn = (home - part) % 4 * CAP
                    moved = pltpu.roll(gain[f], turn, 1) if turn else gain[f]
                    adj_b[f, tile, rows, :] = adj_b[f, tile, rows, :] + jnp.where(
                        lane_block == home, moved, 0.0
                    )

    def sweep_tile(source, store, tile, part):
        rows = pl.ds(8 * part, 8)
        here = pl.ds(8 * part + 8, 8)
        center = [source[f, tile + 1, here, :] for f in range(5)]
        upper = [source[f, tile + 2, here, :] for f in range(5)]
        lower = [source[f, tile, here, :] for f in range(5)]
        pairs = [
            (
                [source[f, tile + 1, pl.ds(8 * part + 9, 8), :] for f in range(5)],
                [source[f, tile + 1, pl.ds(8 * part + 7, 8), :] for f in range(5)],
            ),
            (
                [
                    pltpu.roll(jnp.where(tile_lane >= CAP, center[f], upper[f]), LANES - CAP, 1)
                    for f in range(5)
                ],
                [
                    pltpu.roll(jnp.where(tile_lane < LANES - CAP, center[f], lower[f]), CAP, 1)
                    for f in range(5)
                ],
            ),
            (
                [pltpu.roll(center[f], LANES - 1, 1) for f in range(5)],
                [pltpu.roll(center[f], 1, 1) for f in range(5)],
            ),
        ]
        velocity = [coef[k, tile, rows, :] for k in range(3)]
        half_sq = coef[3, tile, rows, :]
        enthalpy = coef[4, tile, rows, :]
        reach = coef[5, tile, rows, :]
        sums = None
        moved = None
        flux = None
        first = []
        turned = None
        for axis, (plus, minus) in enumerate(pairs):
            g_plus = gface[2 * axis, tile, rows, :]
            g_minus = gface[2 * axis + 1, tile, rows, :]
            ahead = [g_plus * value for value in plus]
            behind = [g_minus * value for value in minus]
            diff = [a - b for a, b in zip(ahead, behind)]
            both = [a + b for a, b in zip(ahead, behind)]
            sums = both if sums is None else [a + b for a, b in zip(sums, both)]
            dot = (
                velocity[0] * diff[1]
                + velocity[1] * diff[2]
                + velocity[2] * diff[3]
                + enthalpy * diff[4]
            )
            first.append(diff[0] + dot)
            speed = velocity[axis]
            part_moved = [speed * diff[k] for k in range(1, 5)]
            moved = part_moved if moved is None else [a + b for a, b in zip(moved, part_moved)]
            flux = speed * dot if flux is None else flux + speed * dot
            turned = diff[1 + axis] if turned is None else turned + diff[1 + axis]
        turned = turned + moved[3]
        scaled_turn = (GAMMA - 1.0) * turned
        result = [half_sq * turned - flux]
        for k in range(3):
            result.append(first[k] - scaled_turn * velocity[k] + moved[k])
        result.append(scaled_turn + moved[3])
        for f in range(5):
            store(f, tile, part, scaled[f, tile, rows, :] + reach * sums[f] + result[f])

    def store_b(f, tile, part, value):
        adj_b[f, tile + 1, pl.ds(8 * part + 8, 8), :] = value

    def store_c(f, tile, part, value):
        adj_c[f, pl.ds(8 * part, 8), pl.ds(pl.multiple_of(tile * LANES, LANES), LANES)] = value

    def sweep(source, store):
        def body(tile, carry):
            for part in range(4):
                sweep_tile(source, store, tile, part)
            return carry

        lax.fori_loop(0, columns, body, 0, unroll=4)

    def interior(source, store):
        def body(tile, carry):
            for part in (1, 2):
                sweep_tile(source, store, tile, part)
            return carry

        lax.fori_loop(1, columns - 1, body, 0, unroll=3)

    def boundary(source, store):
        def body(tile, carry):
            for part in (0, 3):
                sweep_tile(source, store, tile, part)
            return carry

        lax.fori_loop(0, columns, body, 0, unroll=4)
        for tile in (0, columns - 1):
            for part in (1, 2):
                sweep_tile(source, store, tile, part)

    nothing = jnp.zeros((8, LANES), F32)
    for f in range(5):
        for tile in range(columns):
            adj_a[f, 1 + tile, pl.ds(0, 8), :] = nothing
            adj_a[f, 1 + tile, pl.ds(40, 8), :] = nothing
        for part in range(4):
            adj_a[f, 0, pl.ds(8 + 8 * part, 8), :] = nothing
            adj_a[f, columns + 1, pl.ds(8 + 8 * part, 8), :] = nothing

    loaded(flow, face, pseudo, rhs)
    tall_row = row_iota((16, LANES))
    tall_lane = lane_iota((16, LANES))

    def coefficients(step, carry):
        tile = step // 2
        half = step % 2
        rows = pl.ds(pl.multiple_of(half * 16, 16), 16)
        lanes = pl.ds(pl.multiple_of(tile * LANES, LANES), LANES)
        density = flow[0, rows, lanes]
        inverse = 1.0 / density
        velocity = [flow[1 + k, rows, lanes] * inverse for k in range(3)]
        energy = flow[4, rows, lanes]
        speed_sq = (
            velocity[0] * velocity[0] + velocity[1] * velocity[1] + velocity[2] * velocity[2]
        )
        pressure = (GAMMA - 1.0) * (energy - 0.5 * density * speed_sq)
        enthalpy = (energy + pressure) * inverse
        reach = jnp.sqrt(speed_sq) + jnp.sqrt(GAMMA * pressure * inverse)
        for k in range(3):
            coef[k, tile, rows, :] = velocity[k]
        coef[3, tile, rows, :] = 0.5 * (GAMMA - 1.0) * speed_sq
        coef[4, tile, rows, :] = enthalpy
        coef[5, tile, rows, :] = reach
        press[tile, rows, :] = pressure
        faces = [face[d, rows, lanes].astype(F32) for d in range(6)]
        open_sum = faces[0] + faces[1] + faces[2] + faces[3] + faces[4] + faces[5]
        share = 1.0 / (pseudo[rows, lanes] + 0.5 * reach * open_sum)
        half_share = 0.5 * share
        across = tall_row + half * 16
        along = tall_lane + tile * LANES
        height = tall_lane % 32
        outside = [
            (across == 31) & (group == groups - 1),
            (across == 0) & (group == 0),
            (along >= 992) & (block == blocks - 1),
            (along < 32) & (block == 0),
            height == 31,
            height == 0,
        ]
        for d in range(6):
            gface[d, tile, rows, :] = jnp.where(outside[d], 0.0, faces[d] * half_share)
        for f in range(5):
            scaled[f, tile, rows, :] = rhs[f, rows, lanes] * share
        return carry

    lax.fori_loop(0, 2 * columns, coefficients, 0, unroll=2)
    pltpu.make_async_copy(inner(adj_a), inner(adj_a), load_sem.at[len(loads)]).wait()
    sweep(adj_a, store_b)

    for i in range(2):
        for j in range(2):
            fill_edge(i, j)
    for side in (2, 3):
        fill_face(side)
    pl.semaphore_wait(barrier, 8 + LOCAL - 1 + planes - 1)
    halo = halo_copies()
    for copy in halo[4:] + halo[2:4]:
        copy.start()
    for side in (0, 1):
        fill_face(side)
        halo[side].start()
    for device in column:
        pl.semaphore_signal(plane_sem, inc=1, device_id=device, device_id_type=MESH)

    interior(adj_b, store_c)

    loaded(cell, coords, weights, vertex, count)

    def pick_cells(chunk, carry):
        lanes = pl.ds(pl.multiple_of(chunk * 256, 256), 256)
        place = jnp.bitwise_and(cell[:, lanes], 1023)
        for band in range(8):
            rows = band * 128 + row_iota((128, 256))
            onehot[pl.ds(band * 128, 128), lanes] = jnp.where(rows == place, 1.0, 0.0).astype(BF16)
        return carry

    lax.fori_loop(0, chunks, pick_cells, 0)

    own_block = lane_block == tile_row % 4
    upper_half = tile_row < 4
    slot = tile_lane % CAP

    def spread(even, odd):
        value = jnp.where(own_block, jnp.where(upper_half, even, odd), 0.0)
        value = value + pltpu.roll(value, CAP, 1)
        return value + pltpu.roll(value, 2 * CAP, 1)

    def by_corner(values):
        total = values[3]
        for k in range(3):
            total = jnp.where(lane_block == k, values[k], total)
        return total

    def geometry(chunk, carry):
        even = pl.ds(pl.multiple_of(chunk * 256, 128), 128)
        odd = pl.ds(pl.multiple_of(chunk * 256 + 128, 128), 128)
        rows = pl.ds(pl.multiple_of(chunk * 8, 8), 8)
        corner = [
            [spread(coords[k, c : c + 1, even], coords[k, c : c + 1, odd]) for k in range(3)]
            for c in range(4)
        ]
        edge = [[corner[c][k] - corner[0][k] for k in range(3)] for c in range(1, 4)]
        grads = [
            [value / 6.0 for value in cross(edge[1], edge[2])],
            [value / 6.0 for value in cross(edge[2], edge[0])],
            [value / 6.0 for value in cross(edge[0], edge[1])],
        ]
        grad_zero = [-(grads[0][k] + grads[1][k] + grads[2][k]) for k in range(3)]
        side_two = [0.5 * (corner[3][k] - corner[1][k]) for k in range(3)]
        side_three = [-0.5 * (corner[2][k] - corner[1][k]) for k in range(3)]
        side_one = [-(side_two[k] + side_three[k]) for k in range(3)]
        weight = by_corner([spread(weights[c : c + 1, even], weights[c : c + 1, odd]) for c in range(4)])
        counts = jnp.broadcast_to(count[...], (8, blocks))
        wanted = lane_iota((8, blocks)) == chunk * 8 + row_iota((8, blocks))
        own_count = jnp.sum(jnp.where(wanted, counts, 0), axis=1, keepdims=True)
        weight = jnp.where(slot < own_count, weight, 0.0)
        for k in range(3):
            gradient = by_corner([grad_zero[k], grads[0][k], grads[1][k], grads[2][k]])
            side = by_corner([jnp.zeros_like(side_one[k]), side_one[k], side_two[k], side_three[k]])
            geom[k, rows, :] = weight * gradient
            geom[3 + k, rows, :] = weight * side
        send[3, rows, :] = by_corner(
            [
                spread(vertex[c : c + 1, even].astype(F32), vertex[c : c + 1, odd].astype(F32))
                for c in range(4)
            ]
        )
        return carry

    lax.fori_loop(0, chunks, geometry, 0, unroll=4)

    for copy in halo:
        copy.wait_recv()
    for side in range(4):
        complete(side)
    boundary(adj_b, store_c)
    adj_copy = pltpu.make_async_copy(adj_c, adj_out, out_sem.at[0])
    adj_copy.start()

    def fill_table(step, carry):
        tile = step // 2
        half = step % 2
        rows = pl.ds(pl.multiple_of(half * 16, 16), 16)
        lanes = pl.ds(pl.multiple_of(tile * LANES, LANES), LANES)
        pressure = press[tile, rows, :]
        for f in range(4):
            value = pressure * adj_c[1 + f, rows, lanes]
            high = value.astype(BF16)
            low = (value - high.astype(F32)).astype(BF16)
            table[pl.ds(pl.multiple_of(f * 32 + half * 16, 16), 16), lanes] = high
            table[pl.ds(pl.multiple_of(128 + f * 32 + half * 16, 16), 16), lanes] = low
        return carry

    lax.fori_loop(0, 2 * columns, fill_table, 0)

    found[...] = jnp.dot(table[...], onehot[...], preferred_element_type=F32)

    def terms(chunk, carry):
        lanes = pl.ds(pl.multiple_of(chunk * 256, 256), 256)
        rows = pl.ds(pl.multiple_of(chunk * 8, 8), 8)
        plane = jnp.right_shift(cell[:, lanes], 10)
        mine = row_iota((32, 256)) == plane
        fields = []
        for f in range(4):
            value = found[32 * f : 32 * f + 32, lanes] + found[128 + 32 * f : 160 + 32 * f, lanes]
            value = jnp.sum(jnp.where(mine, value, 0.0), axis=0, keepdims=True)
            fields.append(spread(value[:, :128], value[:, 128:]))
        b, a = fields[:3], fields[3]
        gradient = [geom[k, rows, :] for k in range(3)]
        side = [geom[3 + k, rows, :] for k in range(3)]
        turn = cross(side, b)
        for k in range(3):
            send[k, rows, :] = a * gradient[k] + turn[k]
        return carry

    lax.fori_loop(0, chunks, terms, 0, unroll=8)

    if planes > 1:
        pl.semaphore_wait(plane_sem, planes - 1)

    def post(step, carry):
        turn = step // LOCAL
        far = planes // 2 + (1 - 2 * (turn % 2)) * ((turn + 1) // 2)
        near = LOCAL - 1 - step % LOCAL
        owner = (
            lax.rem(z + far, planes) * LOCAL
            + lax.rem(x + near // 2, 4) * 2
            + lax.rem(core + near % 2, 2)
        )
        pltpu.make_async_remote_copy(
            src_ref=send.at[:, pl.ds(owner, 1), :],
            dst_ref=recv.at[:, pl.ds(step, 1), :],
            send_sem=term_send,
            recv_sem=term_recv,
            device_id={"blk": owner},
            device_id_type=MESH,
        ).start()
        return carry

    lax.fori_loop(0, blocks - 1, post, 0)
    own = pltpu.make_async_copy(
        send.at[:, pl.ds(block, 1), :], recv.at[:, pl.ds(blocks - 1, 1), :], out_sem.at[1]
    )
    own.start()
    others = pltpu.make_async_remote_copy(
        src_ref=send.at[:, pl.ds(0, blocks - 1), :],
        dst_ref=recv.at[:, pl.ds(0, blocks - 1), :],
        send_sem=term_send,
        recv_sem=term_recv,
        device_id=blk_up,
        device_id_type=MESH,
    )
    others.wait_recv()
    own.wait()

    for copy in halo:
        copy.wait_send()
    others.wait_send()
    adj_copy.wait()


def vertex_sums(adj, recv_hbm, adj_out, sens_out, recv, held, left_op, right_op, recv_sem, in_sem, back_sem):
    recv_copy = pltpu.make_async_copy(recv_hbm, recv, recv_sem)
    recv_copy.start()
    inward = [
        pltpu.make_async_copy(adj.at[f], held.at[f], in_sem.at[f]) for f in range(5)
    ]
    outward = [
        pltpu.make_async_copy(held.at[f], adj_out.at[f], back_sem.at[f]) for f in range(5)
    ]
    for copy in inward:
        copy.start()
    for arriving, leaving in zip(inward, outward):
        arriving.wait()
        leaving.start()
    recv_copy.wait()
    chunks = recv.shape[1] // 8

    bands = [(row_iota((16, LANES)) + 16 * band).astype(F32).astype(BF16) for band in range(8)]
    one, zero = jnp.ones((16, LANES), BF16), jnp.zeros((16, LANES), BF16)

    def operands(chunk, carry):
        rows = pl.ds(chunk * 8, 8)
        vertices = recv[3, rows, :].astype(jnp.int32)
        major = jnp.right_shift(vertices, 7)
        minor = jnp.bitwise_and(vertices, 127)
        halves = []
        for k in range(3):
            value = recv[k, rows, :]
            high = value.astype(BF16).astype(F32)
            halves += [high, value - high]
        for s in range(8):
            lanes = pl.ds(chunk * 1024 + s * LANES, LANES)
            low = jnp.broadcast_to(minor[s : s + 1].astype(F32), (16, LANES)).astype(BF16)
            for band in range(8):
                right_op[pl.ds(16 * band, 16), lanes] = jnp.where(low == bands[band], one, zero)
            hit = row_iota((16, LANES)) == major[s : s + 1]
            for n, value in enumerate(halves):
                left_op[pl.ds(16 * n, 16), lanes] = jnp.where(hit, value[s : s + 1], 0.0).astype(BF16)
        return carry

    sums = None
    for chunk in range(chunks):
        operands(chunk, 0)
        lanes = pl.ds(chunk * 1024, 1024)
        part = lax.dot_general(
            left_op[:, lanes],
            right_op[:, lanes],
            (((1,), (1,)), ((), ())),
            preferred_element_type=F32,
        )
        sums = part if sums is None else sums + part
    for k in range(3):
        both = sums[32 * k : 32 * k + 16] + sums[32 * k + 16 : 32 * k + 32]
        for h in range(VERT_DEV // LANES):
            sens_out[k : k + 1, h * LANES : (h + 1) * LANES] = both[h : h + 1]

    for copy in outward:
        copy.wait()


def local(groups, blocks, init, rhs, flow, face, pseudo, coords, weights, cell, vertex, count):
    slots = blocks * CAP
    vmem = pltpu.VMEM
    adjoint, received = pl.pallas_call(
        functools.partial(kernel, groups, blocks),
        out_shape=(
            jax.ShapeDtypeStruct((5, 32, 1024), F32),
            jax.ShapeDtypeStruct((4, blocks, LANES), F32),
        ),
        in_specs=[pl.BlockSpec(memory_space=pltpu.HBM)] * 10,
        out_specs=(
            pl.BlockSpec(memory_space=pl.ANY),
            pl.BlockSpec(memory_space=pl.ANY),
        ),
        scratch_shapes=[
            vmem((5, 10, 48, LANES), F32),
            vmem((5, 10, 48, LANES), F32),
            vmem((5, 32, 1024), F32),
            vmem((5, 32, 1024), F32),
            vmem((5, 32, 1024), F32),
            vmem((6, 32, 1024), BF16),
            vmem((32, 1024), F32),
            vmem((3, 4, slots), F32),
            vmem((4, slots), F32),
            vmem((1, slots), jnp.int32),
            vmem((4, slots), jnp.int32),
            vmem((1, blocks), jnp.int32),
            vmem((6, 8, 32, LANES), F32),
            vmem((5, 8, 32, LANES), F32),
            vmem((6, 8, 32, LANES), F32),
            vmem((8, 32, LANES), F32),
            vmem((4, PLANES, 8, LANES), F32),
            vmem((4, PLANES, 8, LANES), F32),
            vmem((2, 2, 8, LANES), F32),
            vmem((2, 2, 8, LANES), F32),
            vmem((256, 1024), BF16),
            vmem((1024, slots), BF16),
            vmem((256, slots), F32),
            vmem((6, blocks, LANES), F32),
            vmem((4, blocks, LANES), F32),
            pltpu.SemaphoreType.DMA((10,)),
            pltpu.SemaphoreType.DMA((2,)),
            pltpu.SemaphoreType.DMA((8,)),
            pltpu.SemaphoreType.DMA((8,)),
            pltpu.SemaphoreType.DMA,
            pltpu.SemaphoreType.DMA,
            pltpu.SemaphoreType.REGULAR,
        ],
        compiler_params=pltpu.CompilerParams(
            collective_id=0, has_side_effects=True, vmem_limit_bytes=60 * 1024 * 1024
        ),
    )(
        init,
        rhs,
        flow,
        face,
        pseudo,
        jnp.transpose(coords, (1, 0, 2)),
        weights,
        cell.reshape(1, slots),
        vertex,
        count,
    )
    return pl.pallas_call(
        vertex_sums,
        out_shape=(
            jax.ShapeDtypeStruct((5, 32, 1024), F32),
            jax.ShapeDtypeStruct((3, VERT_DEV), F32),
        ),
        in_specs=[pl.BlockSpec(memory_space=pl.ANY)] * 2,
        out_specs=(
            pl.BlockSpec(memory_space=pl.ANY),
            pl.BlockSpec(memory_space=pltpu.VMEM),
        ),
        scratch_shapes=[
            vmem((4, blocks, LANES), F32),
            vmem((5, 32, 1024), F32),
            vmem((96, slots * 4), BF16),
            vmem((128, slots * 4), BF16),
            pltpu.SemaphoreType.DMA,
            pltpu.SemaphoreType.DMA((5,)),
            pltpu.SemaphoreType.DMA((5,)),
        ],
        compiler_params=pltpu.CompilerParams(vmem_limit_bytes=60 * 1024 * 1024),
    )(adjoint, received)


def solution(mesh):
    return jax.shard_map(
        functools.partial(local, mesh.shape["grp"], mesh.shape["blk"]),
        mesh=mesh,
        in_specs=(
            P(None, "grp", "blk"),
            P(None, "grp", "blk"),
            P(None, "grp", "blk"),
            P(None, "grp", "blk"),
            P("grp", "blk"),
            P(None, None, ("grp", "blk")),
            P(None, ("grp", "blk")),
            P(("grp", "blk")),
            P(None, ("grp", "blk")),
            P(("grp", "blk"), None),
        ),
        out_specs=(P(None, "grp", "blk"), P(None, ("grp", "blk"))),
        check_vma=False,
    )
```

```python
import functools

import jax
import jax.numpy as jnp
from jax import lax
from jax.experimental import pallas as pl
from jax.experimental.pallas import tpu as pltpu
from jax.sharding import PartitionSpec as P

VERT_DEV = 1536
CAP = 32
PLANES = 17
LANES = 128
GAMMA = 1.4
LOCAL = 8
MESH = pl.DeviceIdType.MESH
F32 = jnp.float32
BF16 = jnp.bfloat16


def lane_iota(shape):
    return lax.broadcasted_iota(jnp.int32, shape, len(shape) - 1)


def row_iota(shape):
    return lax.broadcasted_iota(jnp.int32, shape, len(shape) - 2)


def cross(a, b):
    return [
        a[1] * b[2] - a[2] * b[1],
        a[2] * b[0] - a[0] * b[2],
        a[0] * b[1] - a[1] * b[0],
    ]


def kernel(
    groups,
    blocks,
    init_hbm,
    rhs_hbm,
    flow_hbm,
    face_hbm,
    pseudo_hbm,
    coords_hbm,
    weights_hbm,
    cell_hbm,
    vertex_hbm,
    count_hbm,
    adj_out,
    recv,
    adj_a,
    adj_b,
    adj_c,
    rhs,
    flow,
    face,
    pseudo,
    coords,
    weights,
    cell,
    vertex,
    count,
    gface,
    scaled,
    coef,
    press,
    face_send,
    face_recv,
    edge_send,
    edge_recv,
    table,
    onehot,
    found,
    geom,
    send,
    load_sem,
    out_sem,
    halo_send,
    halo_recv,
    term_send,
    term_recv,
    plane_sem,
):
    group = lax.axis_index("grp")
    block = lax.axis_index("blk")
    columns = 8
    chunks = blocks // 8

    def loaded(*wanted):
        for position, (source, target) in enumerate(loads):
            if any(target is one for one in wanted):
                pltpu.make_async_copy(source, target, load_sem.at[position]).wait()

    def inner(ref):
        return ref.at[:, pl.ds(1, columns), pl.ds(8, 32), :]

    grp_up = {"grp": lax.rem(group + 1, groups)}
    grp_down = {"grp": lax.rem(group + groups - 1, groups)}
    blk_up = {"blk": lax.rem(block + 1, blocks)}
    blk_down = {"blk": lax.rem(block + blocks - 1, blocks)}

    barrier = pltpu.get_barrier_semaphore()
    diagonals = [[{**one, **two} for two in (blk_down, blk_up)] for one in (grp_down, grp_up)]
    for device in [grp_up, grp_down, blk_up, blk_down] + diagonals[0] + diagonals[1]:
        pl.semaphore_signal(barrier, inc=1, device_id=device, device_id_type=MESH)

    loads = [
        (flow_hbm, flow),
        (face_hbm, face),
        (pseudo_hbm, pseudo),
        (rhs_hbm, rhs),
        (cell_hbm, cell),
        (coords_hbm, coords),
        (weights_hbm, weights),
        (vertex_hbm, vertex),
        (count_hbm, count),
    ]
    for position, (source, target) in enumerate(loads[:4]):
        pltpu.make_async_copy(source, target, load_sem.at[position]).start()
    for tile in range(columns):
        pltpu.make_async_copy(
            init_hbm.at[:, :, pl.ds(tile * LANES, LANES)],
            adj_a.at[:, 1 + tile, pl.ds(8, 32), :],
            load_sem.at[len(loads)],
        ).start()
    for position, (source, target) in enumerate(loads):
        if position >= 4:
            pltpu.make_async_copy(source, target, load_sem.at[position]).start()

    planes = blocks // LOCAL
    z, x, core = block // LOCAL, block % LOCAL // 2, block % 2
    for step in range(1, LOCAL):
        beside = z * LOCAL + lax.rem(x + step // 2, 4) * 2 + lax.rem(core + step % 2, 2)
        pl.semaphore_signal(barrier, inc=1, device_id={"blk": beside}, device_id_type=MESH)
    column = [
        {"blk": lax.rem(z + step, planes) * LOCAL + block % LOCAL} for step in range(1, planes)
    ]
    for device in column:
        pl.semaphore_signal(barrier, inc=1, device_id=device, device_id_type=MESH)

    tile_lane = lane_iota((8, LANES))
    tile_row = row_iota((8, LANES))
    lane_block = tile_lane // CAP

    first_end = (tile_row == 0) & (lane_block == 0)
    last_end = (tile_row == 7) & (lane_block == 3)

    def take_plane(read, side):
        if side < 2:
            row = 31 * side
            return jnp.concatenate([read(tile, row, 1) for tile in range(columns)], axis=0)
        tile, home = ((0, 0), (columns - 1, 3))[side - 2]
        total = None
        for part in range(4):
            value = read(tile, 8 * part, 8)
            turn = (part - home) % 4 * CAP
            if turn:
                value = pltpu.roll(value, turn, 1)
            total = value if total is None else jnp.where(lane_block == part, value, total)
        return total

    def in_adjoint(adj, field):
        return lambda tile, row, count: adj[field, tile + 1, pl.ds(8 + row, count), :]

    def in_table(ref, place):
        return lambda tile, row, count: ref[place, tile, pl.ds(row, count), :]

    def fill_face(side):
        for f in range(5):
            face_send[side, f] = take_plane(in_adjoint(adj_a, f), side)
            face_send[side, 5 + f] = take_plane(in_adjoint(adj_b, f), side)
            face_send[side, 10 + f] = take_plane(in_table(coef, (0, 1, 2, 4, 5)[f]), side)
        outward = 2 * (side // 2) + 1 - side % 2
        along = 2 - 2 * (side // 2)
        face_send[side, 15] = take_plane(in_table(gface, outward), side)
        face_send[side, 16] = jnp.where(
            first_end,
            take_plane(in_table(gface, along + 1), side),
            jnp.where(last_end, take_plane(in_table(gface, along), side), 0.0),
        )

    def fill_edge(upper_x, upper_y):
        tile, home = ((1, 0), (columns, 3))[upper_y]
        row = 8 + 31 * upper_x
        lines = [adj_a[f, tile, pl.ds(row, 1), :] for f in range(5)]
        value = jnp.concatenate(lines + [jnp.zeros((3, LANES), F32)], axis=0)
        value = jnp.where(lane_block == home, value, 0.0)
        value = value + pltpu.roll(value, CAP, 1)
        edge_send[upper_x, upper_y] = value + pltpu.roll(value, 2 * CAP, 1)

    def halo_copies():
        parts = [
            (face_send.at[side], face_recv.at[side + 1 - 2 * (side % 2)], device)
            for side, device in enumerate((grp_down, grp_up, blk_down, blk_up))
        ] + [
            (edge_send.at[i, j], edge_recv.at[1 - i, 1 - j], diagonals[i][j])
            for i in range(2)
            for j in range(2)
        ]
        return [
            pltpu.make_async_remote_copy(
                src_ref=source,
                dst_ref=target,
                send_sem=halo_send.at[position],
                recv_sem=halo_recv.at[position],
                device_id=device,
                device_id_type=MESH,
            )
            for position, (source, target, device) in enumerate(parts)
        ]

    def one_way(faces_of, side, axis, sign, weight, value):
        velocity = [faces_of[side, 10 + k] for k in range(3)]
        enthalpy = faces_of[side, 13]
        reach = faces_of[side, 14]
        half_sq = (0.5 * (GAMMA - 1.0)) * (
            velocity[0] * velocity[0] + velocity[1] * velocity[1] + velocity[2] * velocity[2]
        )
        speed = velocity[axis]
        dot = (
            velocity[0] * value[1]
            + velocity[1] * value[2]
            + velocity[2] * value[3]
            + enthalpy * value[4]
        )
        turned = value[1 + axis] + speed * value[4]
        scaled_turn = (GAMMA - 1.0) * turned
        result = [half_sq * turned - speed * dot]
        for k in range(3):
            entry = speed * value[1 + k] - scaled_turn * velocity[k]
            result.append(entry + value[0] + dot if k == axis else entry)
        result.append(scaled_turn + speed * value[4])
        steady, signed = weight * reach, weight * sign
        return [signed * result[f] + steady * value[f] for f in range(5)]

    def complete(side):
        axis, cross_axis = side // 2, 1 - side // 2
        sign = 2.0 * (side % 2) - 1.0
        mine = [face_send[side, f] for f in range(5)]
        theirs = [face_recv[side, f] for f in range(5)]
        gain = one_way(face_send, side, axis, sign, face_send[side, 15], theirs)
        outer = one_way(face_recv, side, axis, -sign, face_recv[side, 15], mine)
        if side < 2:
            ends = edge_recv[side, 0], edge_recv[side, 1]
        else:
            ends = edge_recv[0, side - 2], edge_recv[1, side - 2]
        corner = [
            jnp.where(last_end, ends[1][f : f + 1], jnp.where(first_end, ends[0][f : f + 1], 0.0))
            for f in range(5)
        ]
        end_sign = jnp.where(last_end, 1.0, -1.0)
        extra = one_way(face_recv, side, cross_axis, end_sign, face_recv[side, 16], corner)
        for f in range(5):
            halo = face_recv[side, 5 + f] + outer[f] + extra[f]
            if side < 2:
                own_row, halo_row = ((8, 7), (39, 40))[side]
                for tile in range(columns):
                    adj_b[f, 1 + tile, pl.ds(halo_row, 1), :] = halo[tile : tile + 1]
                    adj_b[f, 1 + tile, pl.ds(own_row, 1), :] = (
                        adj_b[f, 1 + tile, pl.ds(own_row, 1), :] + gain[f][tile : tile + 1]
                    )
            else:
                tile, home, halo_tile, halo_home = ((1, 0, 0, 3), (columns, 3, columns + 1, 0))[side - 2]
                for part in range(4):
                    rows = pl.ds(8 + 8 * part, 8)
                    turn = (halo_home - part) % 4 * CAP
                    adj_b[f, halo_tile, rows, :] = pltpu.roll(halo, turn, 1) if turn else halo
                    turn = (home - part) % 4 * CAP
                    moved = pltpu.roll(gain[f], turn, 1) if turn else gain[f]
                    adj_b[f, tile, rows, :] = adj_b[f, tile, rows, :] + jnp.where(
                        lane_block == home, moved, 0.0
                    )

    def sweep_tile(source, store, tile, part):
        rows = pl.ds(8 * part, 8)
        here = pl.ds(8 * part + 8, 8)
        center = [source[f, tile + 1, here, :] for f in range(5)]
        upper = [source[f, tile + 2, here, :] for f in range(5)]
        lower = [source[f, tile, here, :] for f in range(5)]
        pairs = [
            (
                [source[f, tile + 1, pl.ds(8 * part + 9, 8), :] for f in range(5)],
                [source[f, tile + 1, pl.ds(8 * part + 7, 8), :] for f in range(5)],
            ),
            (
                [
                    pltpu.roll(jnp.where(tile_lane >= CAP, center[f], upper[f]), LANES - CAP, 1)
                    for f in range(5)
                ],
                [
                    pltpu.roll(jnp.where(tile_lane < LANES - CAP, center[f], lower[f]), CAP, 1)
                    for f in range(5)
                ],
            ),
            (
                [pltpu.roll(center[f], LANES - 1, 1) for f in range(5)],
                [pltpu.roll(center[f], 1, 1) for f in range(5)],
            ),
        ]
        velocity = [coef[k, tile, rows, :] for k in range(3)]
        half_sq = coef[3, tile, rows, :]
        enthalpy = coef[4, tile, rows, :]
        reach = coef[5, tile, rows, :]
        sums = None
        moved = None
        flux = None
        first = []
        turned = None
        for axis, (plus, minus) in enumerate(pairs):
            g_plus = gface[2 * axis, tile, rows, :]
            g_minus = gface[2 * axis + 1, tile, rows, :]
            ahead = [g_plus * value for value in plus]
            behind = [g_minus * value for value in minus]
            diff = [a - b for a, b in zip(ahead, behind)]
            both = [a + b for a, b in zip(ahead, behind)]
            sums = both if sums is None else [a + b for a, b in zip(sums, both)]
            dot = (
                velocity[0] * diff[1]
                + velocity[1] * diff[2]
                + velocity[2] * diff[3]
                + enthalpy * diff[4]
            )
            first.append(diff[0] + dot)
            speed = velocity[axis]
            part_moved = [speed * diff[k] for k in range(1, 5)]
            moved = part_moved if moved is None else [a + b for a, b in zip(moved, part_moved)]
            flux = speed * dot if flux is None else flux + speed * dot
            turned = diff[1 + axis] if turned is None else turned + diff[1 + axis]
        turned = turned + moved[3]
        scaled_turn = (GAMMA - 1.0) * turned
        result = [half_sq * turned - flux]
        for k in range(3):
            result.append(first[k] - scaled_turn * velocity[k] + moved[k])
        result.append(scaled_turn + moved[3])
        for f in range(5):
            store(f, tile, part, scaled[f, tile, rows, :] + reach * sums[f] + result[f])

    def store_b(f, tile, part, value):
        adj_b[f, tile + 1, pl.ds(8 * part + 8, 8), :] = value

    def store_c(f, tile, part, value):
        adj_c[f, pl.ds(8 * part, 8), pl.ds(pl.multiple_of(tile * LANES, LANES), LANES)] = value

    def sweep(source, store):
        def body(tile, carry):
            for part in range(4):
                sweep_tile(source, store, tile, part)
            return carry

        lax.fori_loop(0, columns, body, 0, unroll=4)

    def interior(source, store):
        def body(tile, carry):
            for part in (1, 2):
                sweep_tile(source, store, tile, part)
            return carry

        lax.fori_loop(1, columns - 1, body, 0, unroll=3)

    def boundary(source, store):
        def body(tile, carry):
            for part in (0, 3):
                sweep_tile(source, store, tile, part)
            return carry

        lax.fori_loop(0, columns, body, 0, unroll=4)
        for tile in (0, columns - 1):
            for part in (1, 2):
                sweep_tile(source, store, tile, part)

    nothing = jnp.zeros((8, LANES), F32)
    for f in range(5):
        for tile in range(columns):
            adj_a[f, 1 + tile, pl.ds(0, 8), :] = nothing
            adj_a[f, 1 + tile, pl.ds(40, 8), :] = nothing
        for part in range(4):
            adj_a[f, 0, pl.ds(8 + 8 * part, 8), :] = nothing
            adj_a[f, columns + 1, pl.ds(8 + 8 * part, 8), :] = nothing

    loaded(flow, face, pseudo, rhs)
    tall_row = row_iota((16, LANES))
    tall_lane = lane_iota((16, LANES))

    def coefficients(step, carry):
        tile = step // 2
        half = step % 2
        rows = pl.ds(pl.multiple_of(half * 16, 16), 16)
        lanes = pl.ds(pl.multiple_of(tile * LANES, LANES), LANES)
        density = flow[0, rows, lanes]
        inverse = 1.0 / density
        velocity = [flow[1 + k, rows, lanes] * inverse for k in range(3)]
        energy = flow[4, rows, lanes]
        speed_sq = (
            velocity[0] * velocity[0] + velocity[1] * velocity[1] + velocity[2] * velocity[2]
        )
        pressure = (GAMMA - 1.0) * (energy - 0.5 * density * speed_sq)
        enthalpy = (energy + pressure) * inverse
        reach = jnp.sqrt(speed_sq) + jnp.sqrt(GAMMA * pressure * inverse)
        for k in range(3):
            coef[k, tile, rows, :] = velocity[k]
        coef[3, tile, rows, :] = 0.5 * (GAMMA - 1.0) * speed_sq
        coef[4, tile, rows, :] = enthalpy
        coef[5, tile, rows, :] = reach
        press[tile, rows, :] = pressure
        faces = [face[d, rows, lanes].astype(F32) for d in range(6)]
        open_sum = faces[0] + faces[1] + faces[2] + faces[3] + faces[4] + faces[5]
        share = 1.0 / (pseudo[rows, lanes] + 0.5 * reach * open_sum)
        half_share = 0.5 * share
        across = tall_row + half * 16
        along = tall_lane + tile * LANES
        height = tall_lane % 32
        outside = [
            (across == 31) & (group == groups - 1),
            (across == 0) & (group == 0),
            (along >= 992) & (block == blocks - 1),
            (along < 32) & (block == 0),
            height == 31,
            height == 0,
        ]
        for d in range(6):
            gface[d, tile, rows, :] = jnp.where(outside[d], 0.0, faces[d] * half_share)
        for f in range(5):
            scaled[f, tile, rows, :] = rhs[f, rows, lanes] * share
        return carry

    lax.fori_loop(0, 2 * columns, coefficients, 0, unroll=2)
    pltpu.make_async_copy(inner(adj_a), inner(adj_a), load_sem.at[len(loads)]).wait()
    sweep(adj_a, store_b)

    for i in range(2):
        for j in range(2):
            fill_edge(i, j)
    for side in (2, 3):
        fill_face(side)
    pl.semaphore_wait(barrier, 8 + LOCAL - 1 + planes - 1)
    halo = halo_copies()
    for copy in halo[4:] + halo[2:4]:
        copy.start()
    for side in (0, 1):
        fill_face(side)
        halo[side].start()
    for device in column:
        pl.semaphore_signal(plane_sem, inc=1, device_id=device, device_id_type=MESH)

    interior(adj_b, store_c)

    loaded(cell, coords, weights, vertex, count)

    def pick_cells(chunk, carry):
        lanes = pl.ds(pl.multiple_of(chunk * 256, 256), 256)
        place = jnp.bitwise_and(cell[:, lanes], 1023)
        for band in range(8):
            rows = band * 128 + row_iota((128, 256))
            onehot[pl.ds(band * 128, 128), lanes] = jnp.where(rows == place, 1.0, 0.0).astype(BF16)
        return carry

    lax.fori_loop(0, chunks, pick_cells, 0)

    own_block = lane_block == tile_row % 4
    upper_half = tile_row < 4
    slot = tile_lane % CAP

    def spread(even, odd):
        value = jnp.where(own_block, jnp.where(upper_half, even, odd), 0.0)
        value = value + pltpu.roll(value, CAP, 1)
        return value + pltpu.roll(value, 2 * CAP, 1)

    def by_corner(values):
        total = values[3]
        for k in range(3):
            total = jnp.where(lane_block == k, values[k], total)
        return total

    def geometry(chunk, carry):
        even = pl.ds(pl.multiple_of(chunk * 256, 128), 128)
        odd = pl.ds(pl.multiple_of(chunk * 256 + 128, 128), 128)
        rows = pl.ds(pl.multiple_of(chunk * 8, 8), 8)
        corner = [
            [spread(coords[k, c : c + 1, even], coords[k, c : c + 1, odd]) for k in range(3)]
            for c in range(4)
        ]
        edge = [[corner[c][k] - corner[0][k] for k in range(3)] for c in range(1, 4)]
        grads = [
            [value / 6.0 for value in cross(edge[1], edge[2])],
            [value / 6.0 for value in cross(edge[2], edge[0])],
            [value / 6.0 for value in cross(edge[0], edge[1])],
        ]
        grad_zero = [-(grads[0][k] + grads[1][k] + grads[2][k]) for k in range(3)]
        side_two = [0.5 * (corner[3][k] - corner[1][k]) for k in range(3)]
        side_three = [-0.5 * (corner[2][k] - corner[1][k]) for k in range(3)]
        side_one = [-(side_two[k] + side_three[k]) for k in range(3)]
        weight = by_corner([spread(weights[c : c + 1, even], weights[c : c + 1, odd]) for c in range(4)])
        counts = jnp.broadcast_to(count[...], (8, blocks))
        wanted = lane_iota((8, blocks)) == chunk * 8 + row_iota((8, blocks))
        own_count = jnp.sum(jnp.where(wanted, counts, 0), axis=1, keepdims=True)
        weight = jnp.where(slot < own_count, weight, 0.0)
        for k in range(3):
            gradient = by_corner([grad_zero[k], grads[0][k], grads[1][k], grads[2][k]])
            side = by_corner([jnp.zeros_like(side_one[k]), side_one[k], side_two[k], side_three[k]])
            geom[k, rows, :] = weight * gradient
            geom[3 + k, rows, :] = weight * side
        send[3, rows, :] = by_corner(
            [
                spread(vertex[c : c + 1, even].astype(F32), vertex[c : c + 1, odd].astype(F32))
                for c in range(4)
            ]
        )
        return carry

    lax.fori_loop(0, chunks, geometry, 0, unroll=4)

    for copy in halo:
        copy.wait_recv()
    for side in range(4):
        complete(side)
    boundary(adj_b, store_c)
    adj_copy = pltpu.make_async_copy(adj_c, adj_out, out_sem.at[0])
    adj_copy.start()

    def fill_table(step, carry):
        tile = step // 2
        half = step % 2
        rows = pl.ds(pl.multiple_of(half * 16, 16), 16)
        lanes = pl.ds(pl.multiple_of(tile * LANES, LANES), LANES)
        pressure = press[tile, rows, :]
        for f in range(4):
            value = pressure * adj_c[1 + f, rows, lanes]
            high = value.astype(BF16)
            low = (value - high.astype(F32)).astype(BF16)
            table[pl.ds(pl.multiple_of(f * 32 + half * 16, 16), 16), lanes] = high
            table[pl.ds(pl.multiple_of(128 + f * 32 + half * 16, 16), 16), lanes] = low
        return carry

    lax.fori_loop(0, 2 * columns, fill_table, 0)

    def terms(chunk, place):
        lanes = pl.ds(pl.multiple_of(chunk * 256, 256), 256)
        rows = pl.ds(pl.multiple_of(chunk * 8, 8), 8)
        plane = jnp.right_shift(cell[:, lanes], 10)
        mine = row_iota((32, 256)) == plane
        fields = []
        for f in range(4):
            value = found[32 * f : 32 * f + 32, place] + found[128 + 32 * f : 160 + 32 * f, place]
            value = jnp.sum(jnp.where(mine, value, 0.0), axis=0, keepdims=True)
            fields.append(spread(value[:, :128], value[:, 128:]))
        b, a = fields[:3], fields[3]
        gradient = [geom[k, rows, :] for k in range(3)]
        side = [geom[3 + k, rows, :] for k in range(3)]
        turn = cross(side, b)
        for k in range(3):
            send[k, rows, :] = a * gradient[k] + turn[k]

    pl.semaphore_wait(plane_sem, planes - 1)
    for turn, far in enumerate((2, 1, 3, 0)):
        pair = lax.rem(z // 2 + far, planes // 2)
        found[:, pl.ds(turn * 512, 512)] = jnp.dot(
            table[...],
            onehot[:, pl.ds(pl.multiple_of(pair * 512, 512), 512)],
            preferred_element_type=F32,
        )
        for half in range(2):
            terms(2 * pair + half, pl.ds(turn * 512 + half * 256, 256))

        def post(step, carry):
            plane = 2 * pair + lax.rem(z + 1 - step // LOCAL, 2)
            near = LOCAL - 1 - step % LOCAL
            owner = (
                plane * LOCAL
                + lax.rem(x + near // 2, 4) * 2
                + lax.rem(core + near % 2, 2)
            )
            away = lax.rem(plane - z + planes, planes)
            pltpu.make_async_remote_copy(
                src_ref=send.at[:, pl.ds(owner, 1), :],
                dst_ref=recv.at[:, pl.ds(away * LOCAL + near - 1, 1), :],
                send_sem=term_send,
                recv_sem=term_recv,
                device_id={"blk": owner},
                device_id_type=MESH,
            ).start()
            return carry

        lax.fori_loop(0, 2 * LOCAL - (far == 0), post, 0)
    own = pltpu.make_async_copy(
        send.at[:, pl.ds(block, 1), :], recv.at[:, pl.ds(blocks - 1, 1), :], out_sem.at[1]
    )
    own.start()
    others = pltpu.make_async_remote_copy(
        src_ref=send.at[:, pl.ds(0, blocks - 1), :],
        dst_ref=recv.at[:, pl.ds(0, blocks - 1), :],
        send_sem=term_send,
        recv_sem=term_recv,
        device_id=blk_up,
        device_id_type=MESH,
    )
    others.wait_recv()
    own.wait()

    for copy in halo:
        copy.wait_send()
    others.wait_send()
    adj_copy.wait()


def vertex_sums(adj, recv_hbm, adj_out, sens_out, recv, held, left_op, right_op, recv_sem, in_sem, back_sem):
    recv_copy = pltpu.make_async_copy(recv_hbm, recv, recv_sem)
    recv_copy.start()
    inward = [
        pltpu.make_async_copy(adj.at[f], held.at[f], in_sem.at[f]) for f in range(5)
    ]
    outward = [
        pltpu.make_async_copy(held.at[f], adj_out.at[f], back_sem.at[f]) for f in range(5)
    ]
    for copy in inward:
        copy.start()
    for arriving, leaving in zip(inward, outward):
        arriving.wait()
        leaving.start()
    recv_copy.wait()
    chunks = recv.shape[1] // 8

    bands = [(row_iota((16, LANES)) + 16 * band).astype(F32).astype(BF16) for band in range(8)]
    one, zero = jnp.ones((16, LANES), BF16), jnp.zeros((16, LANES), BF16)

    def operands(chunk, carry):
        rows = pl.ds(chunk * 8, 8)
        vertices = recv[3, rows, :].astype(jnp.int32)
        major = jnp.right_shift(vertices, 7)
        minor = jnp.bitwise_and(vertices, 127)
        halves = []
        for k in range(3):
            value = recv[k, rows, :]
            high = value.astype(BF16).astype(F32)
            halves += [high, value - high]
        for s in range(8):
            lanes = pl.ds(chunk * 1024 + s * LANES, LANES)
            low = jnp.broadcast_to(minor[s : s + 1].astype(F32), (16, LANES)).astype(BF16)
            for band in range(8):
                right_op[pl.ds(16 * band, 16), lanes] = jnp.where(low == bands[band], one, zero)
            hit = row_iota((16, LANES)) == major[s : s + 1]
            for n, value in enumerate(halves):
                left_op[pl.ds(16 * n, 16), lanes] = jnp.where(hit, value[s : s + 1], 0.0).astype(BF16)
        return carry

    sums = None
    for chunk in range(chunks):
        operands(chunk, 0)
        lanes = pl.ds(chunk * 1024, 1024)
        part = lax.dot_general(
            left_op[:, lanes],
            right_op[:, lanes],
            (((1,), (1,)), ((), ())),
            preferred_element_type=F32,
        )
        sums = part if sums is None else sums + part
    for k in range(3):
        both = sums[32 * k : 32 * k + 16] + sums[32 * k + 16 : 32 * k + 32]
        for h in range(VERT_DEV // LANES):
            sens_out[k : k + 1, h * LANES : (h + 1) * LANES] = both[h : h + 1]

    for copy in outward:
        copy.wait()


def local(groups, blocks, init, rhs, flow, face, pseudo, coords, weights, cell, vertex, count):
    slots = blocks * CAP
    vmem = pltpu.VMEM
    adjoint, received = pl.pallas_call(
        functools.partial(kernel, groups, blocks),
        out_shape=(
            jax.ShapeDtypeStruct((5, 32, 1024), F32),
            jax.ShapeDtypeStruct((4, blocks, LANES), F32),
        ),
        in_specs=[pl.BlockSpec(memory_space=pltpu.HBM)] * 10,
        out_specs=(
            pl.BlockSpec(memory_space=pl.ANY),
            pl.BlockSpec(memory_space=pl.ANY),
        ),
        scratch_shapes=[
            vmem((5, 10, 48, LANES), F32),
            vmem((5, 10, 48, LANES), F32),
            vmem((5, 32, 1024), F32),
            vmem((5, 32, 1024), F32),
            vmem((5, 32, 1024), F32),
            vmem((6, 32, 1024), BF16),
            vmem((32, 1024), F32),
            vmem((3, 4, slots), F32),
            vmem((4, slots), F32),
            vmem((1, slots), jnp.int32),
            vmem((4, slots), jnp.int32),
            vmem((1, blocks), jnp.int32),
            vmem((6, 8, 32, LANES), F32),
            vmem((5, 8, 32, LANES), F32),
            vmem((6, 8, 32, LANES), F32),
            vmem((8, 32, LANES), F32),
            vmem((4, PLANES, 8, LANES), F32),
            vmem((4, PLANES, 8, LANES), F32),
            vmem((2, 2, 8, LANES), F32),
            vmem((2, 2, 8, LANES), F32),
            vmem((256, 1024), BF16),
            vmem((1024, slots), BF16),
            vmem((256, slots), F32),
            vmem((6, blocks, LANES), F32),
            vmem((4, blocks, LANES), F32),
            pltpu.SemaphoreType.DMA((10,)),
            pltpu.SemaphoreType.DMA((2,)),
            pltpu.SemaphoreType.DMA((8,)),
            pltpu.SemaphoreType.DMA((8,)),
            pltpu.SemaphoreType.DMA,
            pltpu.SemaphoreType.DMA,
            pltpu.SemaphoreType.REGULAR,
        ],
        compiler_params=pltpu.CompilerParams(
            collective_id=0, has_side_effects=True, vmem_limit_bytes=60 * 1024 * 1024
        ),
    )(
        init,
        rhs,
        flow,
        face,
        pseudo,
        jnp.transpose(coords, (1, 0, 2)),
        weights,
        cell.reshape(1, slots),
        vertex,
        count,
    )
    return pl.pallas_call(
        vertex_sums,
        out_shape=(
            jax.ShapeDtypeStruct((5, 32, 1024), F32),
            jax.ShapeDtypeStruct((3, VERT_DEV), F32),
        ),
        in_specs=[pl.BlockSpec(memory_space=pl.ANY)] * 2,
        out_specs=(
            pl.BlockSpec(memory_space=pl.ANY),
            pl.BlockSpec(memory_space=pltpu.VMEM),
        ),
        scratch_shapes=[
            vmem((4, blocks, LANES), F32),
            vmem((5, 32, 1024), F32),
            vmem((96, slots * 4), BF16),
            vmem((128, slots * 4), BF16),
            pltpu.SemaphoreType.DMA,
            pltpu.SemaphoreType.DMA((5,)),
            pltpu.SemaphoreType.DMA((5,)),
        ],
        compiler_params=pltpu.CompilerParams(vmem_limit_bytes=60 * 1024 * 1024),
    )(adjoint, received)


def solution(mesh):
    return jax.shard_map(
        functools.partial(local, mesh.shape["grp"], mesh.shape["blk"]),
        mesh=mesh,
        in_specs=(
            P(None, "grp", "blk"),
            P(None, "grp", "blk"),
            P(None, "grp", "blk"),
            P(None, "grp", "blk"),
            P("grp", "blk"),
            P(None, None, ("grp", "blk")),
            P(None, ("grp", "blk")),
            P(("grp", "blk")),
            P(None, ("grp", "blk")),
            P(("grp", "blk"), None),
        ),
        out_specs=(P(None, "grp", "blk"), P(None, ("grp", "blk"))),
        check_vma=False,
    )
```
